128 devices in a mesh: gz: 2 (over core), gx: 32 (over z, y, x_hi), gy: 2 (over x_lo).
Axes of the slice: x: 4 (x_hi: 2, x_lo: 2; x = x_hi * 2 + x_lo), y: 4, z: 4, core: 2. Of those that a mesh axis runs over, the one named last changes fastest.
Arguments:
- prediction: float32 [64, 512, 256], P('gz', 'gx', 'gy'), may hold values from 0.01 to 0.99
- label: float32 [64, 512, 256], P('gz', 'gx', 'gy'), may hold values from 0.001 to 1
Outputs:
- loss: float32 [], replicated
- pred_grad: float32 [64, 512, 256], P('gz', 'gx', 'gy')
The draws below stay inside these ranges and needn't reach their ends.
All inputs are finite; a program needn't handle non-finite values.
Results may differ from the reference program's by a relative error of at most 0.0003.
Values sent between devices are 32-bit elements; how exact they have to be, the bound alone decides.
A program may use at most 128 MiB of HBM per device.

```python
import jax
import jax.numpy as jnp
from jax import lax

ITERS = 5
NZ = 64
NX = 512
NY = 256
VOXELS = 8388608


def steps_of(stream_key, dims, shards, least, high):
    def one(position, shards_of):
        heights = jax.random.uniform(jax.random.fold_in(jax.random.fold_in(stream_key, 6), position), (shards_of,), jnp.float32, least / len(shards), high / len(shards))
        return jnp.repeat(jnp.exp(heights), dims[position] // shards_of).reshape((-1,) + (1,) * (len(dims) - position - 1))

    loudness = one(*shards[0])
    for cut in shards[1:]:
        loudness = loudness * one(*cut)
    return loudness


def setup_inputs(seed: int = 0) -> dict:
    splits = jax.random.split(jax.random.key(seed), 3)
    return {
        "prediction": jnp.clip(0.01 + 0.98 * jax.random.uniform(splits[0], (NZ, NX, NY), jnp.float32) ** steps_of(splits[0], (NZ, NX, NY), ((0, 2), (1, 32), (2, 2)), -0.2, 0.2), 0.01, 0.99),
        "label": jnp.clip(0.001 + 0.999 * jax.random.uniform(splits[1], (NZ, NX, NY), jnp.float32) ** steps_of(splits[1], (NZ, NX, NY), ((0, 2), (1, 32), (2, 2)), -0.2, 0.2), 0.001, 1.0),
    }


def pick(padded, dim, larger):
    count = padded.shape[dim] - 2
    lower = lax.slice_in_dim(padded, 0, count, axis=dim)
    centre = lax.slice_in_dim(padded, 1, count + 1, axis=dim)
    upper = lax.slice_in_dim(padded, 2, count + 2, axis=dim)
    if larger:
        best = jnp.where(lower > centre, lower, centre)
        best = jnp.where(upper > best, upper, best)
    else:
        best = jnp.where(lower < centre, lower, centre)
        best = jnp.where(upper < best, upper, best)
    return best

def pad_dim(field, dim, value):
    widths = [(0, 0), (0, 0), (0, 0)]
    widths[dim] = (1, 1)
    return jnp.pad(field, widths, constant_values=value)

def erode(field):
    depth_min = pick(pad_dim(field, 0, 2.0), 0, False)
    rows_min = pick(pad_dim(field, 1, 2.0), 1, False)
    cols_min = pick(pad_dim(field, 2, 2.0), 2, False)
    best = jnp.where(rows_min < depth_min, rows_min, depth_min)
    return jnp.where(cols_min < best, cols_min, best)

def dilate(field):
    for dim in range(3):
        field = pick(pad_dim(field, dim, 0.0), dim, True)
    return field

def relu_where(value):
    return jnp.where(value > 0, value, jnp.zeros_like(value))

def skeleton(image):
    eroded = erode(image)
    skel = relu_where(image - dilate(eroded))
    for level in range(ITERS):
        image = eroded
        eroded = erode(image)
        delta = relu_where(image - dilate(eroded))
        skel = skel + relu_where(delta - skel * delta)
    return skel

def reference(prediction, label):
    label_skel = skeleton(label)

    def loss_of(pred):
        pred_skel = skeleton(pred)
        tprec = (jnp.sum(pred_skel * label) + 1.0) / (jnp.sum(pred_skel) + 1.0)
        tsens = (jnp.sum(label_skel * pred) + 1.0) / (jnp.sum(label_skel) + 1.0)
        return 1.0 - 2.0 * tprec * tsens / (tprec + tsens)
    loss, pull = jax.vjp(loss_of, prediction)
    grads, = pull(jnp.ones_like(loss))
    return (loss, grads * VOXELS)
```

```python
import functools

import jax
import jax.numpy as jnp
from jax import lax
from jax.experimental import pallas as pl
from jax.experimental.pallas import tpu as pltpu
from jax.sharding import PartitionSpec as P

LEVELS = 6
Z, X, Y = 32, 16, 128
WIN = Z + 8
PAD = WIN + 16
ROWS = X + 16
GROUP = 16
LO = 4
SEMS = 64
MESH = pl.DeviceIdType.MESH

W, WL, WU = pl.ds(8, WIN), pl.ds(7, WIN), pl.ds(9, WIN)


def lane_of(v):
    return lax.broadcasted_iota(jnp.int32, v.shape, 1)


def plane_of(v):
    return lax.broadcasted_iota(jnp.int32, v.shape, 0)


def roll(v, by):
    return pltpu.roll(v, by, 1)


def max3(a, b, c):
    return jnp.maximum(jnp.maximum(a, b), c)


def route(g, best, candidates):
    zero = jnp.zeros_like(g)
    parts = []
    for value in candidates:
        hit = value == best
        parts.append(jnp.where(hit, g, zero))
        g = jnp.where(hit, zero, g)
    parts.append(g)
    return parts


def run(start, blocks, size, row):
    def block(b, _):
        todo, memo = [], {}
        first = start + b * size
        for q in range(size):
            todo += row(first + q, q, memo)
        for ref, at, value in todo:
            ref[at] = value
        return 0
    if isinstance(blocks, int) and blocks == 1:
        block(0, 0)
    else:
        lax.fori_loop(0, blocks, block, 0)


def once(memo, key, load):
    if key not in memo:
        memo[key] = load()
    return memo[key]


def kernel(nx, pred_hbm, label_hbm, out, loss, pred, label, in_sem, E, S, M1, M2, SM1, SM2, D, SP, SD, SSP, GB, SGB, SK, SSK,
           HX, SHX, HZ, G, SG, T, T2, SX, SX2, F, FO, RZ, RX, PS, PR, ARS, AR1, AR2S, AR2,
           send_sem, recv_sem, ar_send, ar_recv):
    gz, gx, gy = lax.axis_index("gz"), lax.axis_index("gx"), lax.axis_index("gy")
    prev, nxt = lax.rem(gx + nx - 1, nx), lax.rem(gx + 1, nx)
    nhi = nx // LO
    hi, lo = gx // LO, lax.rem(gx, LO)
    me1 = (gz * LO + lo) * 2 + gy
    o = pl.multiple_of(8 + 8 * gz, 8)
    O, OL, OU = pl.ds(o, Z), pl.ds(o - 1, Z), pl.ds(o + 1, Z)
    seam = 127 * (1 - gy)
    zlow = jnp.where(gz == 0, 0, -1)
    zhigh = jnp.where(gz == 1, Z - 1, -1)
    first_lane = jnp.where(gx == 0, 32, 0)
    last_lane = jnp.where(gx == nx - 1, 96, 128)

    def member(i):
        return (i // (2 * LO), hi * LO + lax.rem(i // 2, LO), lax.rem(i, 2))

    barrier = pltpu.get_barrier_semaphore()
    greet = [(gz, prev, gy), (gz, nxt, gy), (gz, prev, 1 - gy), (gz, nxt, 1 - gy)]
    greet += [member(lax.rem(me1 + d, GROUP)) for d in range(1, GROUP)]
    greet += [(gz, lax.rem(hi + d, nhi) * LO + lo, gy) for d in range(1, nhi)]
    for device in greet:
        pl.semaphore_signal(barrier, inc=1, device_id=device, device_id_type=MESH)

    loads = [pltpu.make_async_copy(src, dst, in_sem.at[f])
             for f, (src, dst) in enumerate(((pred_hbm, pred), (label_hbm, label)))]
    for load in loads:
        load.start()

    for f, ref in ((0, pred), (1, label)):
        loads[f].wait()

        def bring(x, _, memo, f=f, ref=ref):
            return [(E, (f, 0, 9 + x, pl.ds(o + 8 * t, 8)), ref[pl.ds(x + X * 8 * t, 8, stride=X), :])
                    for t in range(Z // 8)]
        run(0, 2, 8, bring)

    pl.semaphore_wait(barrier, len(greet))

    copies = []

    def send(number, src, dst, device):
        copy = pltpu.make_async_remote_copy(
            src_ref=src, dst_ref=dst, send_sem=send_sem.at[number], recv_sem=recv_sem.at[number],
            device_id=device, device_id_type=MESH)
        copy.start()
        copies.append(copy)
        return copy

    near = pl.multiple_of(32 - 16 * gz, 8)
    far = pl.multiple_of(8 + 32 * gz, 8)
    below, above = (gz, prev, gy), (gz, nxt, gy)
    arrived = [[], []]

    def pass_rows(f, base, planes):
        arrived[f] += [
            send(base, E.at[f, 0, pl.ds(9, 7), planes], E.at[f, 0, pl.ds(25, 7), planes], below),
            send(base + 1, E.at[f, 0, pl.ds(18, 7), planes], E.at[f, 0, pl.ds(2, 7), planes], above)]

    def first_halos(f):
        copy = send(8 * f, E.at[f, 0, pl.ds(9, X), pl.ds(near, 8)], E.at[f, 0, pl.ds(9, X), pl.ds(far, 8)],
                    (1 - gz, gx, gy))
        pass_rows(f, 8 * f + 1, O)
        return copy

    def second_halos(f, depth):
        depth.wait_recv()
        pass_rows(f, 8 * f + 3, pl.ds(pl.multiple_of(40 - 32 * gz, 8), 8))
        for half in (0, 1):
            packed = zero_w
            for i in range(8):
                v = E[f, 0, 9 + 8 * half + i, W]
                packed = jnp.where(lane_of(v) // 16 == i, roll(v, lax.rem(16 * i + 16 * (1 - gy), 128)), packed)
            PS[f, half] = packed
        arrived[f] += [
            send(8 * f + 5, PS.at[f], PR.at[f, pl.ds(1, 2)], (gz, gx, 1 - gy)),
            send(8 * f + 6, PS.at[f, 0], PR.at[f, 3], (gz, prev, 1 - gy)),
            send(8 * f + 7, PS.at[f, 1], PR.at[f, 0], (gz, nxt, 1 - gy))]

    zero_w = jnp.zeros((WIN, Y), jnp.float32)
    zero_o = jnp.zeros((Z, Y), jnp.float32)
    depth = first_halos(0)
    second_halos(0, depth)
    depth = first_halos(1)
    second_halos(1, depth)

    two = jnp.full((8, Y), 2.0, jnp.float32)

    def rims(r, _, memo):
        return [(E, (f, k, r, pl.ds(at, 8)), two)
                for f in (0, 1) for k in range(LEVELS + 1) for at in (0, PAD - 8)]
    run(0, 17, 2, rims)

    def strip_rims(j, _, memo):
        return [(S, (f, k, j, pl.ds(at, 8)), two)
                for f in (0, 1) for k in range(LEVELS + 1) for at in (0, PAD - 8)]
    run(1, 4, 2, strip_rims)
    run(0, 17, 2, lambda r, _, m: [(G, (p, q, r), zero_w) for p in (0, 1) for q in range(3)])
    run(0, 4, 8, lambda r, _, m: [(HZ, (r,), zero_w)])
    run(0, 2, 5, lambda j, _, m: [(SG, (p, q, j), zero_w) for p in (0, 1) for q in range(3)])
    run(0, 4, 5, lambda i, _, m: [(HX, (q, i), zero_o) for q in range(3)])
    run(0, 4, 4, lambda i, _, m: [(SK, (0, i), zero_o), (SK, (1, i), zero_o), (GB, (LEVELS, i + 1), zero_o)])
    run(0, 1, 8, lambda j, _, m: [(SSK, (j,), zero_o), (SGB, (LEVELS, j), zero_o)])
    for k in range(LEVELS + 1):
        GB[k, 0] = zero_o
        GB[k, X + 1] = zero_o
    for q in range(10):
        for p in range(3):
            T[q, p] = jnp.zeros((PAD, Y), jnp.float32)
        for p in range(2):
            T2[q, p] = jnp.zeros((PAD, Y), jnp.float32)
    for f in (0, 1):
        for r in (0, 1, ROWS, ROWS + 1):
            for k in range(LEVELS + 1) if r in (0, ROWS + 1) else (0,):
                E[f, k, r, W] = zero_w + 2.0

    def turn(r):
        return lax.rem(128 + 111 + 2 * gy - 32 * (r // 8), 128)

    def sides(v, seen):
        lane = lane_of(v)
        t = jnp.where(lane == seam, seen, v)
        return jnp.where(lane == 0, t, roll(v, 1)), jnp.where(lane == 127, t, roll(v, 127))

    def strip_sides(v):
        return roll(v, 1), roll(v, 127)

    def gather_sides(lower, upper, seen):
        lane = lane_of(lower)
        t = jnp.where(lane == seam, seen, 0.0)
        return jnp.where(lane == 127, t, roll(lower, 127)) + jnp.where(lane == 0, t, roll(upper, 1))

    def wrap_strip(ref, at, window, value):
        v = ref[at + (8, window)]
        v = jnp.where(lane_of(v) < first_lane, value, v)
        ref[at + (8, window)] = v
        ref[at + (0, window)] = roll(v, 32)
        v = ref[at + (1, window)]
        v = jnp.where(lane_of(v) >= last_lane, value, v)
        ref[at + (1, window)] = v
        ref[at + (9, window)] = roll(v, 96)

    def cap_rows(f, k):
        @pl.when(gx == 0)
        def _():
            E[f, k, 8, W] = zero_w + 2.0

        @pl.when(gx == nx - 1)
        def _():
            E[f, k, 25, W] = zero_w + 2.0

    def build_strip(f):
        def row(j, _, memo):
            acc = zero_w
            lane = lane_of(acc) // 16
            for g in range(4):
                own = roll(E[f, 0, 8 * g + j + 1, W], lax.rem(32 * g + 16, 128))
                other = roll(PR[f, g], lax.rem(32 * g - 16 * j + 16 * (1 - gy) + 128, 128))
                acc = jnp.where(lane == 2 * g + gy, own, acc)
                acc = jnp.where(lane == 2 * g + 1 - gy, other, acc)
            return [(S, (f, 0, j + 1, W), acc)]
        run(0, 2, 4, row)
        wrap_strip(S, (f, 0), W, 2.0)

    def eroded(ref, at, i, q, memo, pair):
        def centre(step):
            return once(memo, q + step, lambda: ref[at + (i + step, W)])
        c = centre(0)
        lower, upper = pair(c)
        m = jnp.minimum(jnp.minimum(c, lower), upper)
        m = jnp.minimum(m, jnp.minimum(ref[at + (i, WL)], ref[at + (i, WU)]))
        return jnp.minimum(m, jnp.minimum(centre(-1), centre(1)))

    def depth_max(ref, at, i):
        c = ref[at + (i, O)]
        plane = plane_of(c)
        lower = jnp.where(plane == zlow, c, ref[at + (i, OL)])
        upper = jnp.where(plane == zhigh, c, ref[at + (i, OU)])
        return max3(lower, c, upper)

    def level_forward(f, k, slot):
        start = jnp.where(k < 4, 1, 6)
        blocks = jnp.where(k < 4, 3, 2)

        def strip_erode(j, q, memo):
            return [(S, (f, k + 1, j + 1, W), eroded(S, (f, k), j + 1, q, memo, strip_sides))]
        run(0, 1, 8, strip_erode)
        wrap_strip(S, (f, k + 1), W, 2.0)

        def erode(r, q, memo):
            seen = roll(S[f, k, lax.rem(r, 8) + 1, W], turn(r))
            return [(E, (f, k + 1, r + 1, W), eroded(E, (f, k), r + 1, q, memo, lambda c: sides(c, seen)))]
        run(start, blocks, 10, erode)
        cap_rows(f, k + 1)

        def strip_depth(j, _, memo):
            return [(SM1, (slot, j + 1), depth_max(S, (f, k + 1), j + 1))]
        run(0, 1, 8, strip_depth)
        wrap_strip(SM1, (slot,), slice(None), 0.0)

        def strip_rows(j, q, memo):
            v = max3(*[once(memo, q + d, lambda d=d: SM1[slot, j + d]) for d in range(3)])
            todo = [(SM2, (slot, j), v)]
            if f == 0:
                lower, upper = strip_sides(v)
                delta = jnp.maximum(S[f, k, j + 1, O] - max3(lower, v, upper), 0.0)
                prior = SSK[j]
                todo += [(SD, (k, j), delta), (SSP, (k, j), prior),
                         (SSK, (j,), prior + jnp.maximum(delta - prior * delta, 0.0))]
            return todo
        run(0, 1, 8, strip_rows)

        def depth_rows(i, _, memo):
            return [(M1, (slot, i), depth_max(E, (f, k + 1), i + 8))]
        run(0, 2, 9, depth_rows)

        @pl.when(gx == 0)
        def _():
            M1[slot, 0] = zero_o

        @pl.when(gx == nx - 1)
        def _():
            M1[slot, X + 1] = zero_o

        def rest(i, q, memo):
            v = max3(*[once(memo, q + d, lambda d=d: M1[slot, i + d]) for d in range(3)])
            r = i + 8
            lower, upper = sides(v, roll(SM2[slot, lax.rem(r, 8)], turn(r)))
            delta = jnp.maximum(E[f, k, r + 1, O] - max3(lower, v, upper), 0.0)
            prior = SK[f, i]
            todo = [(M2, (slot, i), v), (SK, (f, i), prior + jnp.maximum(delta - prior * delta, 0.0))]
            if f == 0:
                todo += [(D, (k, i), delta), (SP, (k, i), prior)]
            return todo
        run(0, 2, 8, rest)

    def ar_copy(n, phase, slot, src, dst, number, device):
        return pltpu.make_async_remote_copy(
            src_ref=src, dst_ref=dst, send_sem=ar_send.at[n, phase, number], recv_sem=ar_recv.at[n, phase, slot],
            device_id=device, device_id_type=MESH)

    def ar_first(n, d):
        return ar_copy(n, 0, me1, ARS.at[n], AR1.at[n, me1], d, member(lax.rem(me1 + d, GROUP)))

    def ar_second(n, d):
        return ar_copy(n, 1, hi, AR2S.at[n], AR2.at[n, hi], d, (gz, lax.rem(hi + d, nhi) * LO + lo, gy))

    def ar_start(n, f):
        def add(b, carry):
            both, alone = carry
            for q in range(4):
                v = SK[f, 4 * b + q]
                both, alone = both + v * E[1 - f, 0, 4 * b + q + 9, O], alone + v
            return both, alone
        both, alone = lax.fori_loop(0, X // 4, add, (zero_o, zero_o))
        both = jnp.sum(both, axis=0, keepdims=True)
        alone = jnp.sum(alone, axis=0, keepdims=True)
        sub = plane_of(two)
        tile = jnp.where(sub == 0, both, jnp.where(sub == 1, alone, 0.0))
        ARS[n] = tile
        AR1[n, me1] = tile
        for d in range(1, GROUP):
            ar_first(n, d).start()

    def ar_middle(n):
        for d in range(1, GROUP):
            s = lax.rem(me1 + d, GROUP)
            ar_copy(n, 0, s, ARS.at[n], AR1.at[n, s], d, member(s)).wait_recv()
        tile = AR1[n, 0]
        for s in range(1, GROUP):
            tile = tile + AR1[n, s]
        AR2S[n] = tile
        AR2[n, hi] = tile
        for d in range(1, nhi):
            ar_second(n, d).start()

    def ar_end(n):
        for d in range(1, nhi):
            s = lax.rem(hi + d, nhi)
            ar_copy(n, 1, s, AR2S.at[n], AR2.at[n, s], d, (gz, s * LO + lo, gy)).wait_recv()
        tile = AR2[n, 0]
        for s in range(1, nhi):
            tile = tile + AR2[n, s]
        for d in range(1, GROUP):
            ar_first(n, d).wait_send()
        for d in range(1, nhi):
            ar_second(n, d).wait_send()
        tile = jnp.sum(tile, axis=1, keepdims=True)
        return tile[0:1], tile[1:2]

    for f in (0, 1):
        for copy in arrived[f]:
            copy.wait_recv()
        cap_rows(f, 0)
        build_strip(f)

        def level(k, _, f=f):
            level_forward(f, k, k if f == 0 else LEVELS)
            if f == 1:
                @pl.when(k == 2)
                def _():
                    ar_middle(0)
            return 0
        lax.fori_loop(0, LEVELS, level, 0)
        ar_start(f, f)

    both, alone = ar_end(0)
    pred_total = alone
    tprec = (both + 1.0) / (pred_total + 1.0)

    def chain(i, _, memo):
        t = E[1, 0, i + 9, O] - tprec
        todo = []
        for k in range(LEVELS - 1, -1, -1):
            delta, prior = D[k, i], SP[k, i]
            on = delta - prior * delta > 0
            GB[k, i + 1] = jnp.where(on, t * (1.0 - prior), 0.0)
            t = jnp.where(on, t * (1.0 - delta), t)
        return todo
    run(0, 4, 4, chain)

    def strip_chain(j, _, memo):
        t = S[1, 0, j + 1, O] - tprec
        lane = lane_of(t)
        mine = (lane >= 32) & (lane < 96)
        for k in range(LEVELS - 1, -1, -1):
            delta, prior = SD[k, j], SSP[k, j]
            on = delta - prior * delta > 0
            SGB[k, j] = jnp.where(on & mine, t * (1.0 - prior), 0.0)
            t = jnp.where(on, t * (1.0 - delta), t)
        return []
    run(0, 2, 4, strip_chain)

    def level_back(step, _):
        k = LEVELS - 1 - step
        old = lax.rem(step, 2)
        new = 1 - old

        start = jnp.where(k < 4, 1, 6)
        blocks = jnp.where(k < 4, 3, 2)

        def strip_cols(j, _, memo):
            a = SM2[k, j]
            lower, upper = strip_sides(a)
            gc, gl, gu = route(-SGB[k, j], max3(lower, a, upper), (a, lower))
            todo = [(SX, (0, j), gl), (SX, (1, j), gu)]
            g = gc + roll(gl, 127) + roll(gu, 1)
            gc, gl, gu = route(g, a, (SM1[k, j + 1], SM1[k, j]))
            return todo + [(SHX, (0, j + 1), gc), (SHX, (1, j + 1), gl), (SHX, (2, j + 1), gu)]
        run(0, 1, 8, strip_cols)
        SHX[1, 9] = roll(SHX[1, 1], 96)
        SHX[2, 0] = roll(SHX[2, 8], 32)

        def strip_depth(j, q, memo):
            g = SHX[0, j + 1] + SHX[1, j + 2] + SHX[2, j]
            gc, gl, gu = route(g, SM1[k, j + 1], (S[0, k + 1, j + 1, O], S[0, k + 1, j + 1, OL]))
            T[q, 0, O] = gc + SGB[k + 1, j]
            T[q, 1, O] = gl
            T[q, 2, O] = gu
            g = SG[old, 0, j + 1] + SG[old, 1, j + 2] + SG[old, 2, j]
            g = g + T[q, 0, W] + T[q, 1, WU] + T[q, 2, WL]
            c = S[0, k, j + 1, W]
            lower, upper = strip_sides(c)
            gc, zl, zu, xl, xu, yl, yu = route(
                g, S[0, k + 1, j + 1, W],
                (c, S[0, k, j + 1, WL], S[0, k, j + 1, WU], S[0, k, j, W], S[0, k, j + 2, W], lower))
            T2[q, 0, W] = zl
            T2[q, 1, W] = zu
            return [(SX2, (0, j), yl), (SX2, (1, j), yu),
                    (SG, (new, 0, j + 1), gc + roll(yl, 127) + roll(yu, 1) + T2[q, 0, WU] + T2[q, 1, WL]),
                    (SG, (new, 1, j + 1), xl), (SG, (new, 2, j + 1), xu)]
        run(0, 1, 8, strip_depth)
        SG[new, 1, 9] = roll(SG[new, 1, 1], 96)
        SG[new, 2, 0] = roll(SG[new, 2, 8], 32)

        def cols(i, _, memo):
            a = M2[k, i]
            r = i + 8
            by, j = turn(r), lax.rem(r, 8)
            lower, upper = sides(a, roll(SM2[k, j], by))
            gc, gl, gu = route(-GB[k, i + 1], max3(lower, a, upper), (a, lower))
            g = gc + gather_sides(gl, gu, roll(SX[gy, j], by))
            gc, gl, gu = route(g, a, (M1[k, i + 1], M1[k, i]))
            return [(HX, (0, i + 2), gc), (HX, (1, i + 2), gl), (HX, (2, i + 2), gu)]
        run(0, 2, 8, cols)

        def depths(i, q, memo):
            g = HX[0, i + 1] + HX[1, i + 2] + HX[2, i]
            gc, gl, gu = route(g, M1[k, i], (E[0, k + 1, i + 8, O], E[0, k + 1, i + 8, OL]))
            T[q, 0, O] = gc + GB[k + 1, i]
            T[q, 1, O] = gl
            T[q, 2, O] = gu
            return [(HZ, (i + 7,), T[q, 0, W] + T[q, 1, WU] + T[q, 2, WL])]
        run(0, 2, 9, depths)

        def back(r, q, memo):
            g = G[old, 0, r + 1] + G[old, 1, r + 2] + G[old, 2, r] + HZ[r]
            by, j = turn(r), lax.rem(r, 8)
            below, c, above = [once(memo, q + d, lambda d=d: E[0, k, r + d, W]) for d in range(3)]
            lower, upper = sides(c, roll(S[0, k, j + 1, W], by))
            gc, zl, zu, xl, xu, yl, yu = route(
                g, E[0, k + 1, r + 1, W],
                (c, E[0, k, r + 1, WL], E[0, k, r + 1, WU], below, above, lower))
            T2[q, 0, W] = zl
            T2[q, 1, W] = zu
            return [(G, (new, 0, r + 1), gc + gather_sides(yl, yu, roll(SX2[gy, j], by)) + T2[q, 0, WU] + T2[q, 1, WL]),
                    (G, (new, 1, r + 1), xl), (G, (new, 2, r + 1), xu)]
        run(start, blocks, 10, back)

        @pl.when(step == 2)
        def _():
            ar_middle(1)
        return 0
    lax.fori_loop(0, LEVELS, level_back, 0)

    last = LEVELS % 2

    def total(r, _, memo):
        return [(F, (r,), G[last, 0, r + 1] + G[last, 1, r + 2] + G[last, 2, r])]
    run(0, 4, 8, total)
    beyond = pl.multiple_of(32 - 32 * gz, 8)
    mine = pl.multiple_of(8 * gz, 8)
    inner = pl.multiple_of(24 - 24 * gz, 8)
    rest_at = pl.multiple_of(8 * gz, 8)
    quiet = pl.ds(rest_at, Z - 8)
    edge = pl.ds(inner, 8)
    copy = send(16, F.at[pl.ds(1, 30), pl.ds(beyond, 8)], RZ.at[pl.ds(1, 30)], (1 - gz, gx, gy))
    back_rows = []

    def return_rows(base, planes):
        back_rows.append(send(base, FO.at[pl.ds(1, 7), planes], RX.at[0, :, planes], below))
        back_rows.append(send(base + 1, FO.at[pl.ds(24, 7), planes], RX.at[1, :, planes], above))

    run(1, 5, 6, lambda r, _, m: [(FO, (r,), F[r, pl.ds(mine, Z)])])
    return_rows(17, quiet)
    copy.wait_recv()
    run(1, 5, 6, lambda r, _, m: [(FO, (r, edge), F[r, pl.ds(mine + inner, 8)] + RZ[r])])
    return_rows(19, edge)

    both, alone = ar_end(1)
    tsens = (both + 1.0) / (alone + 1.0)
    square = (tprec + tsens) * (tprec + tsens)
    voxels = float(2 * nx * 2 * Z * X * Y)
    by_prec = -2.0 * tsens * tsens / square / (pred_total + 1.0) * voxels
    by_sens = -2.0 * tprec * tprec / square / (alone + 1.0) * voxels
    loss[...] = 1.0 - 2.0 * tprec * tsens / (tprec + tsens)

    for copy in back_rows:
        copy.wait_recv()

    def give(x, _, memo, extra):
        g = FO[x + 8] + GB[0, x + 1]
        if extra is not None:
            g = g + extra(x)
        g = g * by_prec + SK[1, x] * by_sens
        return [(out, (pl.ds(x + X * 8 * t, 8, stride=X), slice(None)), g[8 * t:8 * t + 8]) for t in range(Z // 8)]
    run(0, 1, 7, functools.partial(give, extra=lambda x: RX[1, x]))
    run(7, 1, 2, functools.partial(give, extra=None))
    run(9, 1, 7, functools.partial(give, extra=lambda x: RX[0, x - 9]))
    for copy in copies:
        copy.wait_send()


def local(prediction, label):
    nx = lax.axis_size("gx")
    nhi = nx // LO
    f32 = jnp.float32

    def vmem(*shape):
        return pltpu.VMEM(shape + (Y,), f32)

    grad, loss = pl.pallas_call(
        functools.partial(kernel, nx),
        out_shape=(jax.ShapeDtypeStruct((Z * X, Y), f32), jax.ShapeDtypeStruct((1, 1), f32)),
        in_specs=[pl.BlockSpec(memory_space=pl.ANY)] * 2,
        out_specs=[pl.BlockSpec(memory_space=pltpu.VMEM)] * 2,
        scratch_shapes=[
            vmem(Z * X), vmem(Z * X), pltpu.SemaphoreType.DMA((2,)),
            vmem(2, 7, ROWS + 2, PAD), vmem(2, 7, 10, PAD),
            vmem(7, X + 2, Z), vmem(7, X, Z), vmem(7, 10, Z), vmem(7, 8, Z),
            vmem(6, X, Z), vmem(6, X, Z), vmem(6, 8, Z), vmem(6, 8, Z),
            vmem(7, X + 2, Z), vmem(7, 8, Z),
            vmem(2, X, Z), vmem(8, Z),
            vmem(3, X + 4, Z), vmem(3, 10, Z), vmem(ROWS, WIN),
            vmem(2, 3, ROWS + 2, WIN), vmem(2, 3, 10, WIN),
            vmem(10, 3, PAD), vmem(10, 2, PAD), vmem(2, 8, Z), vmem(2, 8, WIN),
            vmem(ROWS, WIN), vmem(ROWS, Z), vmem(ROWS, 8), vmem(2, 7, Z),
            vmem(2, 2, WIN), vmem(2, 4, WIN),
            vmem(2, 8), vmem(2, GROUP, 8), vmem(2, 8), vmem(2, nhi, 8),
            pltpu.SemaphoreType.DMA((21,)), pltpu.SemaphoreType.DMA((21,)),
            pltpu.SemaphoreType.DMA((2, 2, GROUP)), pltpu.SemaphoreType.DMA((2, 2, GROUP)),
        ],
        compiler_params=pltpu.CompilerParams(
            collective_id=0, has_side_effects=True, vmem_limit_bytes=56 * 1024 * 1024),
    )(prediction.reshape(Z * X, Y), label.reshape(Z * X, Y))
    return loss.reshape(()), grad.reshape(Z, X, Y)


def solution(mesh):
    in_specs = (P("gz", "gx", "gy"), P("gz", "gx", "gy"))
    out_specs = (P(), P("gz", "gx", "gy"))
    return jax.shard_map(local, mesh=mesh, in_specs=in_specs, out_specs=out_specs, check_vma=False)
```

```python
import functools

import jax
import jax.numpy as jnp
from jax import lax
from jax.experimental import pallas as pl
from jax.experimental.pallas import tpu as pltpu
from jax.sharding import PartitionSpec as P

LEVELS = 6
Z, X, Y = 32, 16, 128
WIN = Z + 8
PAD = WIN + 16
ROWS = X + 16
GROUP = 16
LO = 4
SEMS = 64
MESH = pl.DeviceIdType.MESH

W, WL, WU = pl.ds(8, WIN), pl.ds(7, WIN), pl.ds(9, WIN)


def lane_of(v):
    return lax.broadcasted_iota(jnp.int32, v.shape, 1)


def plane_of(v):
    return lax.broadcasted_iota(jnp.int32, v.shape, 0)


def roll(v, by):
    return pltpu.roll(v, by, 1)


def max3(a, b, c):
    return jnp.maximum(jnp.maximum(a, b), c)


def route(g, best, candidates):
    zero = jnp.zeros_like(g)
    parts = []
    for value in candidates:
        hit = value == best
        parts.append(jnp.where(hit, g, zero))
        g = jnp.where(hit, zero, g)
    parts.append(g)
    return parts


def run(start, blocks, size, row):
    def block(b, _):
        todo, memo = [], {}
        first = start(b) if callable(start) else start + b * size
        for q in range(size):
            todo += row(first + q, q, memo)
        for ref, at, value in todo:
            ref[at] = value
        return 0
    if isinstance(blocks, int) and blocks == 1:
        block(0, 0)
    else:
        lax.fori_loop(0, blocks, block, 0)


def once(memo, key, load):
    if key not in memo:
        memo[key] = load()
    return memo[key]


def slot_of(f, k):
    if f == 0:
        return k
    if isinstance(k, int) and k == 0:
        return 7
    return jnp.where(k == 0, 7, 8 + lax.rem(k, 2))


def kernel(nx, pred_hbm, label_hbm, out, loss, pred, label, in_sem, E, S, M1, M2, SM1, SM2, D, SP, SD, SSP, GB, SGB, SK, SSK,
           HX, SHX, HZ, G, SG, T, T2, SX, SX2, F, FO, RZ, RX, PS, PR, ARS, AR1, AR2S, AR2,
           send_sem, recv_sem, ar_send, ar_recv):
    gz, gx, gy = lax.axis_index("gz"), lax.axis_index("gx"), lax.axis_index("gy")
    prev, nxt = lax.rem(gx + nx - 1, nx), lax.rem(gx + 1, nx)
    nhi = nx // LO
    hi, lo = gx // LO, lax.rem(gx, LO)
    me1 = (gz * LO + lo) * 2 + gy
    o = pl.multiple_of(8 + 8 * gz, 8)
    O, OL, OU = pl.ds(o, Z), pl.ds(o - 1, Z), pl.ds(o + 1, Z)
    seam = 127 * (1 - gy)
    zlow = jnp.where(gz == 0, 0, -1)
    zhigh = jnp.where(gz == 1, Z - 1, -1)
    first_lane = jnp.where(gx == 0, 32, 0)
    last_lane = jnp.where(gx == nx - 1, 96, 128)

    def member(i):
        return (i // (2 * LO), hi * LO + lax.rem(i // 2, LO), lax.rem(i, 2))

    barrier = pltpu.get_barrier_semaphore()
    has_prev, has_nxt = gx > 0, gx < nx - 1
    for inside, row in ((has_prev, prev), (has_nxt, nxt)):
        @pl.when(inside)
        def _(row=row):
            for cols in (gy, 1 - gy):
                pl.semaphore_signal(barrier, inc=1, device_id=(gz, row, cols), device_id_type=MESH)
    greet = [member(lax.rem(me1 + d, GROUP)) for d in range(1, GROUP)]
    greet += [(gz, lax.rem(hi + d, nhi) * LO + lo, gy) for d in range(1, nhi)]
    for device in greet:
        pl.semaphore_signal(barrier, inc=1, device_id=device, device_id_type=MESH)

    loads = [pltpu.make_async_copy(src, dst, in_sem.at[f])
             for f, (src, dst) in enumerate(((pred_hbm, pred), (label_hbm, label)))]
    for load in loads:
        load.start()

    for f, ref in ((0, pred), (1, label)):
        loads[f].wait()

        def bring(x, _, memo, f=f, ref=ref):
            return [(E, (7 * f, 9 + x, pl.ds(o + 8 * t, 8)), ref[pl.ds(x + X * 8 * t, 8, stride=X), :])
                    for t in range(Z // 8)]
        run(0, 2, 8, bring)

    zero_w = jnp.zeros((WIN, Y), jnp.float32)
    zero_o = jnp.zeros((Z, Y), jnp.float32)
    pl.semaphore_wait(barrier, len(greet) + jnp.where(has_prev, 2, 0) + jnp.where(has_nxt, 2, 0))

    copies = []

    def only(inside, act):
        if inside is None:
            act()
        else:
            pl.when(inside)(act)

    class Sent:
        def __init__(self, copy, sends, gets):
            self.copy, self.sends, self.gets = copy, sends, gets

        def start(self):
            only(self.sends, self.copy.start)

        def wait_recv(self):
            only(self.gets, self.copy.wait_recv)

        def wait_send(self):
            only(self.sends, self.copy.wait_send)

    def send(number, src, dst, device, step=0, now=True):
        copy = pltpu.make_async_remote_copy(
            src_ref=src, dst_ref=dst, send_sem=send_sem.at[number], recv_sem=recv_sem.at[number],
            device_id=device, device_id_type=MESH)
        sends = {0: None, -1: has_prev, 1: has_nxt}[step]
        gets = {0: None, -1: has_nxt, 1: has_prev}[step]
        copies.append(Sent(copy, sends, gets))
        if now:
            copies[-1].start()
        return copies[-1]

    near = pl.multiple_of(32 - 16 * gz, 8)
    far = pl.multiple_of(8 + 32 * gz, 8)
    below, above = (gz, prev, gy), (gz, nxt, gy)
    arrived = [[], []]

    def pass_rows(f, base, planes):
        arrived[f] += [
            send(base, E.at[7 * f, pl.ds(9, 7), planes], E.at[7 * f, pl.ds(25, 7), planes], below, -1),
            send(base + 1, E.at[7 * f, pl.ds(18, 7), planes], E.at[7 * f, pl.ds(2, 7), planes], above, 1)]

    def first_halos(f):
        copy = send(8 * f, E.at[7 * f, pl.ds(9, X), pl.ds(near, 8)], E.at[7 * f, pl.ds(9, X), pl.ds(far, 8)],
                    (1 - gz, gx, gy))
        pass_rows(f, 8 * f + 1, O)
        return copy

    def second_halos(f, depth):
        depth.wait_recv()
        pass_rows(f, 8 * f + 3, pl.ds(pl.multiple_of(40 - 32 * gz, 8), 8))
        for half in (0, 1):
            packed = zero_w
            for i in range(8):
                v = E[7 * f, 9 + 8 * half + i, W]
                packed = jnp.where(lane_of(v) // 16 == i, roll(v, lax.rem(16 * i + 16 * (1 - gy), 128)), packed)
            PS[f, half] = packed
        arrived[f] += [
            send(8 * f + 5, PS.at[f], PR.at[f, pl.ds(1, 2)], (gz, gx, 1 - gy)),
            send(8 * f + 6, PS.at[f, 0], PR.at[f, 3], (gz, prev, 1 - gy), -1),
            send(8 * f + 7, PS.at[f, 1], PR.at[f, 0], (gz, nxt, 1 - gy), 1)]

    depth = first_halos(0)
    second_halos(0, depth)
    depth = first_halos(1)
    second_halos(1, depth)

    two = jnp.full((8, Y), 2.0, jnp.float32)

    def rims(r, _, memo):
        return [(E, (slot, r, pl.ds(at, 8)), two) for slot in range(10) for at in (0, PAD - 8)]
    run(0, 17, 2, rims)

    def strip_rims(j, _, memo):
        return [(S, (f, k, j, pl.ds(at, 8)), two)
                for f in (0, 1) for k in range(LEVELS + 1) for at in (0, PAD - 8)]
    run(1, 4, 2, strip_rims)
    run(0, 17, 2, lambda r, _, m: [(G, (p, q, r), zero_w) for p in range(LEVELS + 1) for q in range(3)])
    run(0, 4, 8, lambda r, _, m: [(HZ, (k, r), zero_w) for k in range(LEVELS)])
    run(0, 2, 5, lambda j, _, m: [(SG, (p, q, j), zero_w) for p in (0, 1) for q in range(3)])
    run(0, 4, 5, lambda i, _, m: [(HX, (q, i), zero_o) for q in range(3)])
    run(0, 4, 4, lambda i, _, m: [(SK, (0, i), zero_o), (SK, (1, i), zero_o), (GB, (LEVELS, i + 1), zero_o)])
    run(0, 1, 8, lambda j, _, m: [(SSK, (j,), zero_o), (SGB, (LEVELS, j), zero_o)])
    for k in range(LEVELS + 1):
        GB[k, 0] = zero_o
        GB[k, X + 1] = zero_o
    for q in range(10):
        for p in range(3):
            T[q, p] = jnp.zeros((PAD, Y), jnp.float32)
        for p in range(2):
            T2[q, p] = jnp.zeros((PAD, Y), jnp.float32)
    for r in (0, 1, ROWS, ROWS + 1):
        for slot in range(10) if r in (0, ROWS + 1) else (0, 7):
            E[slot, r, W] = zero_w + 2.0

    @pl.when(gx == 0)
    def _():
        for f in (0, 1):
            PR[f, 0] = zero_w + 2.0
            for r in range(2, 9):
                E[7 * f, r, W] = zero_w + 2.0
        RX[1] = jnp.zeros((7, Z, Y), jnp.float32)

    @pl.when(gx == nx - 1)
    def _():
        for f in (0, 1):
            PR[f, 3] = zero_w + 2.0
            for r in range(25, 32):
                E[7 * f, r, W] = zero_w + 2.0
        RX[0] = jnp.zeros((7, Z, Y), jnp.float32)

    def turn(r):
        return lax.rem(128 + 111 + 2 * gy - 32 * (r // 8), 128)

    def sides(v, seen):
        lane = lane_of(v)
        t = jnp.where(lane == seam, seen, v)
        return jnp.where(lane == 0, t, roll(v, 1)), jnp.where(lane == 127, t, roll(v, 127))

    def strip_sides(v):
        return roll(v, 1), roll(v, 127)

    def gather_sides(lower, upper, seen):
        lane = lane_of(lower)
        t = jnp.where(lane == seam, seen, 0.0)
        return jnp.where(lane == 127, t, roll(lower, 127)) + jnp.where(lane == 0, t, roll(upper, 1))

    def wrap_strip(ref, at, window, value):
        v = ref[at + (8, window)]
        v = jnp.where(lane_of(v) < first_lane, value, v)
        ref[at + (8, window)] = v
        ref[at + (0, window)] = roll(v, 32)
        v = ref[at + (1, window)]
        v = jnp.where(lane_of(v) >= last_lane, value, v)
        ref[at + (1, window)] = v
        ref[at + (9, window)] = roll(v, 96)

    def cap_rows(f, k):
        @pl.when(gx == 0)
        def _():
            E[slot_of(f, k), 8, W] = zero_w + 2.0

        @pl.when(gx == nx - 1)
        def _():
            E[slot_of(f, k), 25, W] = zero_w + 2.0

    def build_strip(f):
        def row(j, _, memo):
            acc = zero_w
            lane = lane_of(acc) // 16
            for g in range(4):
                own = roll(E[7 * f, 8 * g + j + 1, W], lax.rem(32 * g + 16, 128))
                other = roll(PR[f, g], lax.rem(32 * g - 16 * j + 16 * (1 - gy) + 128, 128))
                acc = jnp.where(lane == 2 * g + gy, own, acc)
                acc = jnp.where(lane == 2 * g + 1 - gy, other, acc)
            return [(S, (f, 0, j + 1, W), acc)]
        run(0, 2, 4, row)
        wrap_strip(S, (f, 0), W, 2.0)

    def eroded(ref, at, i, q, memo, pair):
        def centre(step):
            return once(memo, q + step, lambda: ref[at + (i + step, W)])
        c = centre(0)
        lower, upper = pair(c)
        m = jnp.minimum(jnp.minimum(c, lower), upper)
        m = jnp.minimum(m, jnp.minimum(ref[at + (i, WL)], ref[at + (i, WU)]))
        return jnp.minimum(m, jnp.minimum(centre(-1), centre(1)))

    def depth_max(ref, at, i):
        c = ref[at + (i, O)]
        plane = plane_of(c)
        lower = jnp.where(plane == zlow, c, ref[at + (i, OL)])
        upper = jnp.where(plane == zhigh, c, ref[at + (i, OU)])
        return max3(lower, c, upper)

    def level_forward(f, k, slot):
        start = jnp.where(k < 4, 1, 6)
        blocks = jnp.where(k < 4, 3, 2)

        def strip_erode(j, q, memo):
            return [(S, (f, k + 1, j + 1, W), eroded(S, (f, k), j + 1, q, memo, strip_sides))]
        run(0, 1, 8, strip_erode)
        wrap_strip(S, (f, k + 1), W, 2.0)

        def erode(r, q, memo):
            seen = roll(S[f, k, lax.rem(r, 8) + 1, W], turn(r))
            return [(E, (slot_of(f, k + 1), r + 1, W), eroded(E, (slot_of(f, k),), r + 1, q, memo, lambda c: sides(c, seen)))]
        run(start, blocks, 10, erode)
        cap_rows(f, k + 1)

        def strip_depth(j, _, memo):
            return [(SM1, (slot, j + 1), depth_max(S, (f, k + 1), j + 1))]
        run(0, 1, 8, strip_depth)
        wrap_strip(SM1, (slot,), slice(None), 0.0)

        def strip_rows(j, q, memo):
            v = max3(*[once(memo, q + d, lambda d=d: SM1[slot, j + d]) for d in range(3)])
            todo = [(SM2, (slot, j), v)]
            if f == 0:
                lower, upper = strip_sides(v)
                delta = jnp.maximum(S[f, k, j + 1, O] - max3(lower, v, upper), 0.0)
                prior = SSK[j]
                todo += [(SD, (k, j), delta), (SSP, (k, j), prior),
                         (SSK, (j,), prior + jnp.maximum(delta - prior * delta, 0.0))]
            return todo
        run(0, 1, 8, strip_rows)

        def depth_rows(i, _, memo):
            return [(M1, (slot, i), depth_max(E, (slot_of(f, k + 1),), i + 8))]
        run(0, 2, 9, depth_rows)

        @pl.when(gx == 0)
        def _():
            M1[slot, 0] = zero_o

        @pl.when(gx == nx - 1)
        def _():
            M1[slot, X + 1] = zero_o

        def rest(i, q, memo):
            v = max3(*[once(memo, q + d, lambda d=d: M1[slot, i + d]) for d in range(3)])
            r = i + 8
            lower, upper = sides(v, roll(SM2[slot, lax.rem(r, 8)], turn(r)))
            delta = jnp.maximum(E[slot_of(f, k), r + 1, O] - max3(lower, v, upper), 0.0)
            prior = SK[f, i]
            todo = [(M2, (slot, i), v), (SK, (f, i), prior + jnp.maximum(delta - prior * delta, 0.0))]
            if f == 0:
                todo += [(D, (k, i), delta), (SP, (k, i), prior)]
            return todo
        run(0, 2, 8, rest)

    def ar_copy(n, phase, slot, src, dst, number, device):
        return pltpu.make_async_remote_copy(
            src_ref=src, dst_ref=dst, send_sem=ar_send.at[n, phase, number], recv_sem=ar_recv.at[n, phase, slot],
            device_id=device, device_id_type=MESH)

    def ar_first(n, d):
        return ar_copy(n, 0, me1, ARS.at[n], AR1.at[n, me1], d, member(lax.rem(me1 + d, GROUP)))

    def ar_second(n, d):
        return ar_copy(n, 1, hi, AR2S.at[n], AR2.at[n, hi], d, (gz, lax.rem(hi + d, nhi) * LO + lo, gy))

    def ar_start(n, f):
        def add(b, carry):
            both, alone = carry
            for q in range(4):
                v = SK[f, 4 * b + q]
                both, alone = both + v * E[7 - 7 * f, 4 * b + q + 9, O], alone + v
            return both, alone
        both, alone = lax.fori_loop(0, X // 4, add, (zero_o, zero_o))
        both = jnp.sum(both, axis=0, keepdims=True)
        alone = jnp.sum(alone, axis=0, keepdims=True)
        sub = plane_of(two)
        tile = jnp.where(sub == 0, both, jnp.where(sub == 1, alone, 0.0))
        ARS[n] = tile
        AR1[n, me1] = tile
        for d in range(1, GROUP):
            ar_first(n, d).start()

    def ar_middle(n):
        for d in range(1, GROUP):
            s = lax.rem(me1 + d, GROUP)
            ar_copy(n, 0, s, ARS.at[n], AR1.at[n, s], d, member(s)).wait_recv()
        tile = AR1[n, 0]
        for s in range(1, GROUP):
            tile = tile + AR1[n, s]
        AR2S[n] = tile
        AR2[n, hi] = tile
        for d in range(1, nhi):
            ar_second(n, d).start()

    def ar_end(n):
        for d in range(1, nhi):
            s = lax.rem(hi + d, nhi)
            ar_copy(n, 1, s, AR2S.at[n], AR2.at[n, s], d, (gz, s * LO + lo, gy)).wait_recv()
        tile = AR2[n, 0]
        for s in range(1, nhi):
            tile = tile + AR2[n, s]
        for d in range(1, GROUP):
            ar_first(n, d).wait_send()
        for d in range(1, nhi):
            ar_second(n, d).wait_send()
        tile = jnp.sum(tile, axis=1, keepdims=True)
        return tile[0:1], tile[1:2]

    for f in (0, 1):
        for copy in arrived[f]:
            copy.wait_recv()
        cap_rows(f, 0)
        build_strip(f)

        def level(k, _, f=f):
            level_forward(f, k, k if f == 0 else LEVELS)
            if f == 1:
                @pl.when(k == 2)
                def _():
                    ar_middle(0)
            return 0
        lax.fori_loop(0, LEVELS, level, 0)
        ar_start(f, f)

    both, alone = ar_end(0)
    pred_total = alone
    tprec = (both + 1.0) / (pred_total + 1.0)

    def chain(i, _, memo):
        t = E[7, i + 9, O] - tprec
        todo = []
        for k in range(LEVELS - 1, -1, -1):
            delta, prior = D[k, i], SP[k, i]
            on = delta - prior * delta > 0
            GB[k, i + 1] = jnp.where(on, t * (1.0 - prior), 0.0)
            t = jnp.where(on, t * (1.0 - delta), t)
        return todo
    run(0, 4, 4, chain)

    def strip_chain(j, _, memo):
        t = S[1, 0, j + 1, O] - tprec
        lane = lane_of(t)
        mine = (lane >= 32) & (lane < 96)
        for k in range(LEVELS - 1, -1, -1):
            delta, prior = SD[k, j], SSP[k, j]
            on = delta - prior * delta > 0
            SGB[k, j] = jnp.where(on & mine, t * (1.0 - prior), 0.0)
            t = jnp.where(on, t * (1.0 - delta), t)
        return []
    run(0, 2, 4, strip_chain)

    def strip_back(step, _):
        k = LEVELS - 1 - step
        old = lax.rem(step, 2)
        new = 1 - old

        def strip_cols(j, _, memo):
            a = SM2[k, j]
            lower, upper = strip_sides(a)
            gc, gl, gu = route(-SGB[k, j], max3(lower, a, upper), (a, lower))
            todo = [(SX, (k, 0, j), gl), (SX, (k, 1, j), gu)]
            g = gc + roll(gl, 127) + roll(gu, 1)
            gc, gl, gu = route(g, a, (SM1[k, j + 1], SM1[k, j]))
            return todo + [(SHX, (0, j + 1), gc), (SHX, (1, j + 1), gl), (SHX, (2, j + 1), gu)]
        run(0, 1, 8, strip_cols)
        SHX[1, 9] = roll(SHX[1, 1], 96)
        SHX[2, 0] = roll(SHX[2, 8], 32)

        def strip_depth(j, q, memo):
            g = SHX[0, j + 1] + SHX[1, j + 2] + SHX[2, j]
            gc, gl, gu = route(g, SM1[k, j + 1], (S[0, k + 1, j + 1, O], S[0, k + 1, j + 1, OL]))
            T[q, 0, O] = gc + SGB[k + 1, j]
            T[q, 1, O] = gl
            T[q, 2, O] = gu
            g = SG[old, 0, j + 1] + SG[old, 1, j + 2] + SG[old, 2, j]
            g = g + T[q, 0, W] + T[q, 1, WU] + T[q, 2, WL]
            c = S[0, k, j + 1, W]
            lower, upper = strip_sides(c)
            gc, zl, zu, xl, xu, yl, yu = route(
                g, S[0, k + 1, j + 1, W],
                (c, S[0, k, j + 1, WL], S[0, k, j + 1, WU], S[0, k, j, W], S[0, k, j + 2, W], lower))
            T2[q, 0, W] = zl
            T2[q, 1, W] = zu
            return [(SX2, (k, 0, j), yl), (SX2, (k, 1, j), yu),
                    (SG, (new, 0, j + 1), gc + roll(yl, 127) + roll(yu, 1) + T2[q, 0, WU] + T2[q, 1, WL]),
                    (SG, (new, 1, j + 1), xl), (SG, (new, 2, j + 1), xu)]
        run(0, 2, 4, strip_depth)
        SG[new, 1, 9] = roll(SG[new, 1, 1], 96)
        SG[new, 2, 0] = roll(SG[new, 2, 8], 32)
        return 0
    lax.fori_loop(0, LEVELS, strip_back, 0)

    def open_back(k, _):
        def cols(i, _, memo):
            a = M2[k, i]
            r = i + 8
            by, j = turn(r), lax.rem(r, 8)
            lower, upper = sides(a, roll(SM2[k, j], by))
            gc, gl, gu = route(-GB[k, i + 1], max3(lower, a, upper), (a, lower))
            g = gc + gather_sides(gl, gu, roll(SX[k, gy, j], by))
            gc, gl, gu = route(g, a, (M1[k, i + 1], M1[k, i]))
            return [(HX, (0, i + 2), gc), (HX, (1, i + 2), gl), (HX, (2, i + 2), gu)]
        run(0, 2, 8, cols)

        def depths(i, q, memo):
            g = HX[0, i + 1] + HX[1, i + 2] + HX[2, i]
            gc, gl, gu = route(g, M1[k, i], (E[k + 1, i + 8, O], E[k + 1, i + 8, OL]))
            T[q, 0, O] = gc + GB[k + 1, i]
            T[q, 1, O] = gl
            T[q, 2, O] = gu
            return [(HZ, (k, i + 7), T[q, 0, W] + T[q, 1, WU] + T[q, 2, WL])]
        run(0, 3, 6, depths)

        @pl.when(k == 2)
        def _():
            ar_middle(1)
        return 0
    lax.fori_loop(0, LEVELS, open_back, 0)

    def erode_back(k, r, q, memo):
        g = G[k + 1, 0, r + 1] + G[k + 1, 1, r + 2] + G[k + 1, 2, r] + HZ[k, r]
        by, j = turn(r), lax.rem(r, 8)
        under, c, over = [once(memo, q + d, lambda d=d: E[k, r + d, W]) for d in range(3)]
        lower, upper = sides(c, roll(S[0, k, j + 1, W], by))
        gc, zl, zu, xl, xu, yl, yu = route(
            g, E[k + 1, r + 1, W],
            (c, E[k, r + 1, WL], E[k, r + 1, WU], under, over, lower))
        T2[q, 0, W] = zl
        T2[q, 1, W] = zu
        return [(G, (k, 0, r + 1), gc + gather_sides(yl, yu, roll(SX2[k, gy, j], by)) + T2[q, 0, WU] + T2[q, 1, WL]),
                (G, (k, 1, r + 1), xl), (G, (k, 2, r + 1), xu)]

    def outer(step, _):
        k = LEVELS - 1 - step
        run(lambda b: jnp.where(b < 2, 1 + k + 4 * b, 15 - k + 4 * b), 4, 4, lambda r, q, memo: erode_back(k, r, q, memo))
        return 0
    lax.fori_loop(0, LEVELS, outer, 0)

    beyond = pl.multiple_of(32 - 32 * gz, 8)
    mine = pl.multiple_of(8 * gz, 8)
    inner = pl.multiple_of(24 - 24 * gz, 8)
    quiet = pl.ds(mine, Z - 8)
    edge = pl.ds(inner, 8)
    back_rows = []

    def total(r, _, memo):
        v = G[0, 0, r + 1] + G[0, 1, r + 2] + G[0, 2, r]
        return [(F, (r,), v)]

    def from_depth(r, _, memo):
        return [(FO, (r, edge), F[r, pl.ds(mine + inner, 8)] + RZ[r])]

    def own_planes(r, _, memo):
        return [(FO, (r,), F[r, pl.ds(mine, Z)])]

    def return_rows(base, planes, now):
        back_rows.append(send(base, FO.at[pl.ds(1, 7), planes], RX.at[0, :, planes], below, -1, now))
        back_rows.append(send(base + 1, FO.at[pl.ds(24, 7), planes], RX.at[1, :, planes], above, 1, now))

    def to_depth(number, rows):
        return send(number, F.at[rows, pl.ds(beyond, 8)], RZ.at[rows], (1 - gz, gx, gy))

    for start in (1, 24):
        run(start, 1, 7, total)
    margin = [to_depth(16, pl.ds(1, 7)), to_depth(17, pl.ds(24, 7))]
    for start in (1, 24):
        run(start, 1, 7, own_planes)
    return_rows(18, quiet, True)
    return_rows(20, edge, False)

    def inside(step, _):
        k = LEVELS - 1 - step
        at = (k + 1) // 2
        run(8 + 2 * at, 4 - at, 4, lambda r, q, memo: erode_back(k, r, q, memo))

        @pl.when(step == 1)
        def _():
            for copy in margin:
                copy.wait_recv()
            for start in (1, 24):
                run(start, 1, 7, from_depth)
            for copy in back_rows[2:]:
                copy.start()
        return 0
    lax.fori_loop(0, LEVELS, inside, 0)
    run(8, 2, 8, total)
    copy = to_depth(22, pl.ds(8, 16))
    run(8, 2, 8, own_planes)
    copy.wait_recv()
    run(8, 2, 8, from_depth)

    both, alone = ar_end(1)
    tsens = (both + 1.0) / (alone + 1.0)
    square = (tprec + tsens) * (tprec + tsens)
    voxels = float(2 * nx * 2 * Z * X * Y)
    by_prec = -2.0 * tsens * tsens / square / (pred_total + 1.0) * voxels
    by_sens = -2.0 * tprec * tprec / square / (alone + 1.0) * voxels
    loss[...] = 1.0 - 2.0 * tprec * tsens / (tprec + tsens)

    for copy in back_rows:
        copy.wait_recv()

    def give(x, _, memo, extra):
        g = FO[x + 8] + GB[0, x + 1]
        if extra is not None:
            g = g + extra(x)
        g = g * by_prec + SK[1, x] * by_sens
        return [(out, (pl.ds(x + X * 8 * t, 8, stride=X), slice(None)), g[8 * t:8 * t + 8]) for t in range(Z // 8)]
    run(0, 1, 7, functools.partial(give, extra=lambda x: RX[1, x]))
    run(7, 1, 2, functools.partial(give, extra=None))
    run(9, 1, 7, functools.partial(give, extra=lambda x: RX[0, x - 9]))
    for copy in copies:
        copy.wait_send()


def local(prediction, label):
    nx = lax.axis_size("gx")
    nhi = nx // LO
    f32 = jnp.float32

    def vmem(*shape):
        return pltpu.VMEM(shape + (Y,), f32)

    grad, loss = pl.pallas_call(
        functools.partial(kernel, nx),
        out_shape=(jax.ShapeDtypeStruct((Z * X, Y), f32), jax.ShapeDtypeStruct((1, 1), f32)),
        in_specs=[pl.BlockSpec(memory_space=pl.ANY)] * 2,
        out_specs=[pl.BlockSpec(memory_space=pltpu.VMEM)] * 2,
        scratch_shapes=[
            vmem(Z * X), vmem(Z * X), pltpu.SemaphoreType.DMA((2,)),
            vmem(10, ROWS + 2, PAD), vmem(2, 7, 10, PAD),
            vmem(7, X + 2, Z), vmem(7, X, Z), vmem(7, 10, Z), vmem(7, 8, Z),
            vmem(6, X, Z), vmem(6, X, Z), vmem(6, 8, Z), vmem(6, 8, Z),
            vmem(7, X + 2, Z), vmem(7, 8, Z),
            vmem(2, X, Z), vmem(8, Z),
            vmem(3, X + 4, Z), vmem(3, 10, Z), vmem(LEVELS, ROWS, WIN),
            vmem(7, 3, ROWS + 2, WIN), vmem(2, 3, 10, WIN),
            vmem(10, 3, PAD), vmem(10, 2, PAD), vmem(6, 2, 8, Z), vmem(6, 2, 8, WIN),
            vmem(ROWS, WIN), vmem(ROWS, Z), vmem(ROWS, 8), vmem(2, 7, Z),
            vmem(2, 2, WIN), vmem(2, 4, WIN),
            vmem(2, 8), vmem(2, GROUP, 8), vmem(2, 8), vmem(2, nhi, 8),
            pltpu.SemaphoreType.DMA((23,)), pltpu.SemaphoreType.DMA((23,)),
            pltpu.SemaphoreType.DMA((2, 2, GROUP)), pltpu.SemaphoreType.DMA((2, 2, GROUP)),
        ],
        compiler_params=pltpu.CompilerParams(
            collective_id=0, has_side_effects=True, vmem_limit_bytes=56 * 1024 * 1024),
    )(prediction.reshape(Z * X, Y), label.reshape(Z * X, Y))
    return loss.reshape(()), grad.reshape(Z, X, Y)


def solution(mesh):
    in_specs = (P("gz", "gx", "gy"), P("gz", "gx", "gy"))
    out_specs = (P(), P("gz", "gx", "gy"))
    return jax.shard_map(local, mesh=mesh, in_specs=in_specs, out_specs=out_specs, check_vma=False)
```

```python
import functools

import jax
import jax.numpy as jnp
from jax import lax
from jax.experimental import pallas as pl
from jax.experimental.pallas import tpu as pltpu
from jax.sharding import PartitionSpec as P

LEVELS = 6
Z, X, Y = 32, 16, 128
WIN = Z + 8
PAD = WIN + 16
ROWS = X + 16
GROUP = 16
LO = 4
SEMS = 64
MESH = pl.DeviceIdType.MESH

W, WL, WU = pl.ds(8, WIN), pl.ds(7, WIN), pl.ds(9, WIN)


def lane_of(v):
    return lax.broadcasted_iota(jnp.int32, v.shape, 1)


def plane_of(v):
    return lax.broadcasted_iota(jnp.int32, v.shape, 0)


def roll(v, by):
    return pltpu.roll(v, by, 1)


def max3(a, b, c):
    return jnp.maximum(jnp.maximum(a, b), c)


def route(g, best, candidates):
    zero = jnp.zeros_like(g)
    parts = []
    for value in candidates:
        hit = value == best
        parts.append(jnp.where(hit, g, zero))
        g = jnp.where(hit, zero, g)
    parts.append(g)
    return parts


def run(start, blocks, size, row):
    def block(b, _):
        todo, memo = [], {}
        first = start(b) if callable(start) else start + b * size
        for q in range(size):
            todo += row(first + q, q, memo)
        for ref, at, value in todo:
            ref[at] = value
        return 0
    if isinstance(blocks, int) and blocks == 1:
        block(0, 0)
        return
    else:
        lax.fori_loop(0, blocks, block, 0)


def once(memo, key, load):
    if key not in memo:
        memo[key] = load()
    return memo[key]


def slot_of(f, k):
    if f == 0:
        return k
    if isinstance(k, int) and k == 0:
        return 7
    return jnp.where(k == 0, 7, 8 + lax.rem(k, 2))


def kernel(nx, pred_hbm, label_hbm, out, loss, pred, label, in_sem, E, S, M1, M2, SM1, SM2, D, SP, SD, SSP, GB, SGB, CT, SCT, SK, SSK,
           HX, SHX, HZ, G, SG, T, T2, SX, SX2, LE, SLE, LM, BM, SLM, SBM, F, FO, RZ, RX, PS, PR, ARS, AR1, AR2S, AR2,
           send_sem, recv_sem, ar_send, ar_recv):
    gz, gx, gy = lax.axis_index("gz"), lax.axis_index("gx"), lax.axis_index("gy")
    prev, nxt = lax.rem(gx + nx - 1, nx), lax.rem(gx + 1, nx)
    nhi = nx // LO
    hi, lo = gx // LO, lax.rem(gx, LO)
    me1 = (gz * LO + lo) * 2 + gy
    o = pl.multiple_of(8 + 8 * gz, 8)
    O, OL, OU = pl.ds(o, Z), pl.ds(o - 1, Z), pl.ds(o + 1, Z)
    seam = 127 * (1 - gy)
    zlow = jnp.where(gz == 0, 0, -1)
    zhigh = jnp.where(gz == 1, Z - 1, -1)
    first_lane = jnp.where(gx == 0, 32, 0)
    last_lane = jnp.where(gx == nx - 1, 96, 128)

    def member(i):
        return (i // (2 * LO), hi * LO + lax.rem(i // 2, LO), lax.rem(i, 2))

    barrier = pltpu.get_barrier_semaphore()
    has_prev, has_nxt = gx > 0, gx < nx - 1
    for inside, row in ((has_prev, prev), (has_nxt, nxt)):
        @pl.when(inside)
        def _(row=row):
            for cols in (gy, 1 - gy):
                pl.semaphore_signal(barrier, inc=1, device_id=(gz, row, cols), device_id_type=MESH)
    greet = [member(lax.rem(me1 + d, GROUP)) for d in range(1, GROUP)]
    greet += [(gz, lax.rem(hi + d, nhi) * LO + lo, gy) for d in range(1, nhi)]
    for device in greet:
        pl.semaphore_signal(barrier, inc=1, device_id=device, device_id_type=MESH)

    loads = [pltpu.make_async_copy(src, dst, in_sem.at[f])
             for f, (src, dst) in enumerate(((pred_hbm, pred), (label_hbm, label)))]
    for load in loads:
        load.start()

    for f, ref in ((0, pred), (1, label)):
        loads[f].wait()

        def bring(x, _, memo, f=f, ref=ref):
            return [(E, (7 * f, 9 + x, pl.ds(o + 8 * t, 8)), ref[pl.ds(x + X * 8 * t, 8, stride=X), :])
                    for t in range(Z // 8)]
        run(0, 2, 8, bring)

    zero_w = jnp.zeros((WIN, Y), jnp.float32)
    zero_o = jnp.zeros((Z, Y), jnp.float32)
    pl.semaphore_wait(barrier, len(greet) + jnp.where(has_prev, 2, 0) + jnp.where(has_nxt, 2, 0))

    copies = []

    def only(inside, act):
        if inside is None:
            act()
        else:
            pl.when(inside)(act)

    class Sent:
        def __init__(self, copy, sends, gets):
            self.copy, self.sends, self.gets = copy, sends, gets

        def start(self):
            only(self.sends, self.copy.start)

        def wait_recv(self):
            only(self.gets, self.copy.wait_recv)

        def wait_send(self):
            only(self.sends, self.copy.wait_send)

    def send(number, src, dst, device, step=0, now=True):
        copy = pltpu.make_async_remote_copy(
            src_ref=src, dst_ref=dst, send_sem=send_sem.at[number], recv_sem=recv_sem.at[number],
            device_id=device, device_id_type=MESH)
        sends = {0: None, -1: has_prev, 1: has_nxt}[step]
        gets = {0: None, -1: has_nxt, 1: has_prev}[step]
        copies.append(Sent(copy, sends, gets))
        if now:
            copies[-1].start()
        return copies[-1]

    near = pl.multiple_of(32 - 16 * gz, 8)
    far = pl.multiple_of(8 + 32 * gz, 8)
    below, above = (gz, prev, gy), (gz, nxt, gy)
    arrived = [[], []]

    def pass_rows(f, base, planes):
        arrived[f] += [
            send(base, E.at[7 * f, pl.ds(9, 7), planes], E.at[7 * f, pl.ds(25, 7), planes], below, -1),
            send(base + 1, E.at[7 * f, pl.ds(18, 7), planes], E.at[7 * f, pl.ds(2, 7), planes], above, 1)]

    def first_halos(f):
        copy = send(8 * f, E.at[7 * f, pl.ds(9, X), pl.ds(near, 8)], E.at[7 * f, pl.ds(9, X), pl.ds(far, 8)],
                    (1 - gz, gx, gy))
        pass_rows(f, 8 * f + 1, O)
        return copy

    def second_halos(f, depth):
        depth.wait_recv()
        pass_rows(f, 8 * f + 3, pl.ds(pl.multiple_of(40 - 32 * gz, 8), 8))
        for half in (0, 1):
            packed = zero_w
            for i in range(8):
                v = E[7 * f, 9 + 8 * half + i, W]
                packed = jnp.where(lane_of(v) // 16 == i, roll(v, lax.rem(16 * i + 16 * (1 - gy), 128)), packed)
            PS[f, half] = packed
        arrived[f] += [
            send(8 * f + 5, PS.at[f], PR.at[f, pl.ds(1, 2)], (gz, gx, 1 - gy)),
            send(8 * f + 6, PS.at[f, 0], PR.at[f, 3], (gz, prev, 1 - gy), -1),
            send(8 * f + 7, PS.at[f, 1], PR.at[f, 0], (gz, nxt, 1 - gy), 1)]

    depth = first_halos(0)
    second_halos(0, depth)
    depth = first_halos(1)
    second_halos(1, depth)

    two = jnp.full((8, Y), 2.0, jnp.float32)

    def rims(r, _, memo):
        return [(E, (slot, r, pl.ds(at, 8)), two) for slot in range(10) for at in (0, PAD - 8)]
    run(0, 17, 2, rims)

    def strip_rims(j, _, memo):
        return [(S, (f, k, j, pl.ds(at, 8)), two)
                for f in (0, 1) for k in range(LEVELS + 1) for at in (0, PAD - 8)]
    run(1, 4, 2, strip_rims)
    run(0, 17, 2, lambda r, _, m: [(G, (p, q, r), zero_w) for p in range(LEVELS + 1) for q in range(3)])
    for k in range(LEVELS):
        HZ[k, 0] = zero_w
    run(0, 2, 5, lambda j, _, m: [(SG, (p, q, j), zero_w) for p in (0, 1) for q in range(3)])
    run(0, 4, 5, lambda i, _, m: [(HX, (q, i), zero_o) for q in range(3)])
    run(0, 4, 4, lambda i, _, m: [(SK, (0, i), zero_o), (SK, (1, i), zero_o), (GB, (LEVELS, i + 1), zero_o)])
    run(0, 1, 8, lambda j, _, m: [(SSK, (j,), zero_o), (SGB, (LEVELS, j), zero_o)])
    for k in range(LEVELS + 1):
        GB[k, 0] = zero_o
        CT[0] = zero_o
        CT[X + 1] = zero_o
        GB[k, X + 1] = zero_o
    for q in range(10):
        for p in range(3):
            T[q, p] = jnp.zeros((PAD, Y), jnp.float32)
        for p in range(2):
            T2[q, p] = jnp.zeros((PAD, Y), jnp.float32)
    for r in (0, 1, ROWS, ROWS + 1):
        for slot in range(10) if r in (0, ROWS + 1) else (0, 7):
            E[slot, r, W] = zero_w + 2.0

    @pl.when(gx == 0)
    def _():
        for f in (0, 1):
            PR[f, 0] = zero_w + 2.0
            for r in range(2, 9):
                E[7 * f, r, W] = zero_w + 2.0
        RX[1] = jnp.zeros((7, Z, Y), jnp.float32)

    @pl.when(gx == nx - 1)
    def _():
        for f in (0, 1):
            PR[f, 3] = zero_w + 2.0
            for r in range(25, 32):
                E[7 * f, r, W] = zero_w + 2.0
        RX[0] = jnp.zeros((7, Z, Y), jnp.float32)

    seam_turn = 111 + 2 * gy

    def place(r):
        g = lax.div(r, 8)
        return r - 8 * g, seam_turn - 32 * g

    def sides(v, seen):
        lane = lane_of(v)
        t = jnp.where(lane == seam, seen, v)
        return jnp.where(lane == 0, t, roll(v, 1)), jnp.where(lane == 127, t, roll(v, 127))

    def strip_sides(v):
        return roll(v, 1), roll(v, 127)

    def gather_sides(lower, upper, seen):
        lane = lane_of(lower)
        t = jnp.where(lane == seam, seen, 0.0)
        return jnp.where(lane == 127, t, roll(lower, 127)) + jnp.where(lane == 0, t, roll(upper, 1))

    def wrap_strip(ref, at, window, value):
        v = ref[at + (8, window)]
        v = jnp.where(lane_of(v) < first_lane, value, v)
        ref[at + (8, window)] = v
        ref[at + (0, window)] = roll(v, 32)
        v = ref[at + (1, window)]
        v = jnp.where(lane_of(v) >= last_lane, value, v)
        ref[at + (1, window)] = v
        ref[at + (9, window)] = roll(v, 96)

    def cap_rows(f, k):
        @pl.when(gx == 0)
        def _():
            E[slot_of(f, k), 8, W] = zero_w + 2.0

        @pl.when(gx == nx - 1)
        def _():
            E[slot_of(f, k), 25, W] = zero_w + 2.0

    def build_strip(f):
        def row(j, _, memo):
            acc = zero_w
            lane = lane_of(acc) // 16
            for g in range(4):
                own = roll(E[7 * f, 8 * g + j + 1, W], lax.rem(32 * g + 16, 128))
                other = roll(PR[f, g], lax.rem(32 * g - 16 * j + 16 * (1 - gy) + 128, 128))
                acc = jnp.where(lane == 2 * g + gy, own, acc)
                acc = jnp.where(lane == 2 * g + 1 - gy, other, acc)
            return [(S, (f, 0, j + 1, W), acc)]
        run(0, 2, 4, row)
        wrap_strip(S, (f, 0), W, 2.0)

    def eroded(ref, at, i, q, memo, pair):
        def centre(step):
            return once(memo, q + step, lambda: ref[at + (i + step, W)])
        c = centre(0)
        lower, upper = pair(c)
        m = jnp.minimum(jnp.minimum(c, lower), upper)
        m = jnp.minimum(m, jnp.minimum(ref[at + (i, WL)], ref[at + (i, WU)]))
        return jnp.minimum(m, jnp.minimum(centre(-1), centre(1))), lower

    def depth_max(ref, at, i):
        c = ref[at + (i, O)]
        plane = plane_of(c)
        lower = jnp.where(plane == zlow, c, ref[at + (i, OL)])
        upper = jnp.where(plane == zhigh, c, ref[at + (i, OU)])
        return max3(lower, c, upper)

    def level_forward(f, k, slot):
        start = jnp.where(k < 4, 1, 6)
        blocks = jnp.where(k < 4, 3, 2)

        def strip_erode(j, q, memo):
            m, lower = eroded(S, (f, k), j + 1, q, memo, strip_sides)
            return [(S, (f, k + 1, j + 1, W), m)] + ([(SLE, (k, j), lower)] if f == 0 else [])
        run(0, 1, 8, strip_erode)
        wrap_strip(S, (f, k + 1), W, 2.0)

        def erode(r, q, memo):
            j, by = place(r)
            seen = roll(S[f, k, j + 1, W], by)
            m, lower = eroded(E, (slot_of(f, k),), r + 1, q, memo, lambda c: sides(c, seen))
            return [(E, (slot_of(f, k + 1), r + 1, W), m)] + ([(LE, (k, r), lower)] if f == 0 else [])
        run(start, blocks, 10, erode)
        cap_rows(f, k + 1)

        def strip_depth(j, _, memo):
            return [(SM1, (slot, j + 1), depth_max(S, (f, k + 1), j + 1))]
        run(0, 1, 8, strip_depth)
        wrap_strip(SM1, (slot,), slice(None), 0.0)

        def strip_rows(j, q, memo):
            v = max3(*[once(memo, q + d, lambda d=d: SM1[slot, j + d]) for d in range(3)])
            todo = [(SM2, (slot, j), v)]
            if f == 0:
                lower, upper = strip_sides(v)
                best = max3(lower, v, upper)
                delta = jnp.maximum(S[f, k, j + 1, O] - best, 0.0)
                prior = SSK[j]
                todo += [(SLM, (k, j), lower), (SBM, (k, j), best), (SD, (k, j), delta), (SSP, (k, j), prior),
                         (SSK, (j,), prior + jnp.maximum(delta - prior * delta, 0.0))]
            return todo
        run(0, 1, 8, strip_rows)

        def depth_rows(i, _, memo):
            return [(M1, (slot, i), depth_max(E, (slot_of(f, k + 1),), i + 8))]
        run(0, 2, 9, depth_rows)

        @pl.when(gx == 0)
        def _():
            M1[slot, 0] = zero_o

        @pl.when(gx == nx - 1)
        def _():
            M1[slot, X + 1] = zero_o

        def rest(i, q, memo):
            v = max3(*[once(memo, q + d, lambda d=d: M1[slot, i + d]) for d in range(3)])
            r = i + 8
            lower, upper = sides(v, roll(SM2[slot, q], seam_turn - 4 * (r - q)))
            best = max3(lower, v, upper)
            delta = jnp.maximum(E[slot_of(f, k), r + 1, O] - best, 0.0)
            prior = SK[f, i]
            todo = [(M2, (slot, i), v), (SK, (f, i), prior + jnp.maximum(delta - prior * delta, 0.0))]
            if f == 0:
                todo += [(D, (k, i), delta), (SP, (k, i), prior), (LM, (k, i), lower), (BM, (k, i), best)]
            return todo
        run(0, 2, 8, rest)

    def ar_copy(n, phase, slot, src, dst, number, device):
        return pltpu.make_async_remote_copy(
            src_ref=src, dst_ref=dst, send_sem=ar_send.at[n, phase, number], recv_sem=ar_recv.at[n, phase, slot],
            device_id=device, device_id_type=MESH)

    def ar_first(n, d):
        return ar_copy(n, 0, me1, ARS.at[n], AR1.at[n, me1], d, member(lax.rem(me1 + d, GROUP)))

    def ar_second(n, d):
        return ar_copy(n, 1, hi, AR2S.at[n], AR2.at[n, hi], d, (gz, lax.rem(hi + d, nhi) * LO + lo, gy))

    def ar_start(n, f):
        def add(b, carry):
            both, alone = carry
            for q in range(4):
                v = SK[f, 4 * b + q]
                both, alone = both + v * E[7 - 7 * f, 4 * b + q + 9, O], alone + v
            return both, alone
        both, alone = lax.fori_loop(0, X // 4, add, (zero_o, zero_o))
        both = jnp.sum(both, axis=0, keepdims=True)
        alone = jnp.sum(alone, axis=0, keepdims=True)
        sub = plane_of(two)
        tile = jnp.where(sub == 0, both, jnp.where(sub == 1, alone, 0.0))
        ARS[n] = tile
        AR1[n, me1] = tile
        for d in range(1, GROUP):
            ar_first(n, d).start()

    def ar_middle(n):
        for d in range(1, GROUP):
            s = lax.rem(me1 + d, GROUP)
            ar_copy(n, 0, s, ARS.at[n], AR1.at[n, s], d, member(s)).wait_recv()
        tile = AR1[n, 0]
        for s in range(1, GROUP):
            tile = tile + AR1[n, s]
        AR2S[n] = tile
        AR2[n, hi] = tile
        for d in range(1, nhi):
            ar_second(n, d).start()

    def ar_end(n):
        for d in range(1, nhi):
            s = lax.rem(hi + d, nhi)
            ar_copy(n, 1, s, AR2S.at[n], AR2.at[n, s], d, (gz, s * LO + lo, gy)).wait_recv()
        tile = AR2[n, 0]
        for s in range(1, nhi):
            tile = tile + AR2[n, s]
        for d in range(1, GROUP):
            ar_first(n, d).wait_send()
        for d in range(1, nhi):
            ar_second(n, d).wait_send()
        tile = jnp.sum(tile, axis=1, keepdims=True)
        return tile[0:1], tile[1:2]

    for f in (0, 1):
        for copy in arrived[f]:
            copy.wait_recv()
        cap_rows(f, 0)
        build_strip(f)

        def level(k, _, f=f):
            level_forward(f, k, k if f == 0 else LEVELS)
            if f == 1:
                @pl.when(k == 2)
                def _():
                    ar_middle(0)
            return 0
        lax.fori_loop(0, LEVELS, level, 0)
        ar_start(f, f)

    def chain(i, _, memo):
        t = zero_o + 1.0
        todo = []
        for k in range(LEVELS - 1, -1, -1):
            delta, prior = D[k, i], SP[k, i]
            on = delta - prior * delta > 0
            GB[k, i + 1] = jnp.where(on, t * (1.0 - prior), 0.0)
            t = jnp.where(on, t * (1.0 - delta), t)
        return todo
    run(0, 4, 4, chain)

    def strip_chain(j, _, memo):
        t = zero_o + 1.0
        lane = lane_of(t)
        mine = (lane >= 32) & (lane < 96)
        for k in range(LEVELS - 1, -1, -1):
            delta, prior = SD[k, j], SSP[k, j]
            on = delta - prior * delta > 0
            SGB[k, j] = jnp.where(on & mine, t * (1.0 - prior), 0.0)
            t = jnp.where(on, t * (1.0 - delta), t)
        return []
    run(0, 2, 4, strip_chain)

    both, alone = ar_end(0)
    pred_total = alone
    tprec = (both + 1.0) / (pred_total + 1.0)

    run(0, 2, 8, lambda i, _, m: [(CT, (i + 1,), E[7, i + 9, O] - tprec)])
    run(0, 1, 8, lambda j, _, m: [(SCT, (j,), S[1, 0, j + 1, O] - tprec)])

    def strip_back(step, _):
        k = LEVELS - 1 - step
        old = lax.rem(step, 2)
        new = 1 - old

        def strip_cols(j, _, memo):
            a = SM2[k, j]
            gc, gl, gu = route(-SGB[k, j] * SCT[j], SBM[k, j], (a, SLM[k, j]))
            todo = [(SX, (k, j), jnp.where(gy == 0, gl, gu))]
            g = gc + roll(gl, 127) + roll(gu, 1)
            gc, gl, gu = route(g, a, (SM1[k, j + 1], SM1[k, j]))
            return todo + [(SHX, (0, j + 1), gc), (SHX, (1, j + 1), gl), (SHX, (2, j + 1), gu)]
        run(0, 1, 8, strip_cols)
        SHX[1, 9] = roll(SHX[1, 1], 96)
        SHX[2, 0] = roll(SHX[2, 8], 32)

        def strip_depth(j, q, memo):
            g = SHX[0, j + 1] + SHX[1, j + 2] + SHX[2, j]
            gc, gl, gu = route(g, SM1[k, j + 1], (S[0, k + 1, j + 1, O], S[0, k + 1, j + 1, OL]))
            T[q, 0, O] = gc + SGB[k + 1, j] * SCT[j]
            T[q, 1, O] = gl
            T[q, 2, O] = gu
            g = SG[old, 0, j + 1] + SG[old, 1, j + 2] + SG[old, 2, j]
            g = g + T[q, 0, W] + T[q, 1, WU] + T[q, 2, WL]
            c = S[0, k, j + 1, W]
            gc, zl, zu, xl, xu, yl, yu = route(
                g, S[0, k + 1, j + 1, W],
                (c, S[0, k, j + 1, WL], S[0, k, j + 1, WU], S[0, k, j, W], S[0, k, j + 2, W], SLE[k, j]))
            T2[q, 0, W] = zl
            T2[q, 1, W] = zu
            return [(SX2, (k, j), jnp.where(gy == 0, yl, yu)),
                    (SG, (new, 0, j + 1), gc + roll(yl, 127) + roll(yu, 1) + T2[q, 0, WU] + T2[q, 1, WL]),
                    (SG, (new, 1, j + 1), xl), (SG, (new, 2, j + 1), xu)]
        run(0, 2, 4, strip_depth)
        SG[new, 1, 9] = roll(SG[new, 1, 1], 96)
        SG[new, 2, 0] = roll(SG[new, 2, 8], 32)
        return 0
    lax.fori_loop(0, LEVELS, strip_back, 0)

    def open_cols(k, i, j, g):
        a = M2[k, i]
        by = seam_turn - 32 * g
        gc, gl, gu = route(-GB[k, i + 1] * CT[i + 1], BM[k, i], (a, LM[k, i]))
        g = gc + gather_sides(gl, gu, roll(SX[k, j], by))
        gc, gl, gu = route(g, a, (M1[k, i + 1], M1[k, i]))
        return [(HX, (0, i + 2), gc), (HX, (1, i + 2), gl), (HX, (2, i + 2), gu)]

    def open_depths(k, i, q):
        g = HX[0, i + 1] + HX[1, i + 2] + HX[2, i]
        gc, gl, gu = route(g, M1[k, i], (E[k + 1, i + 8, O], E[k + 1, i + 8, OL]))
        T[q, 0, O] = gc + GB[k + 1, i] * CT[i]
        T[q, 1, O] = gl
        T[q, 2, O] = gu
        return [(HZ, (k, i + 1), T[q, 0, W] + T[q, 1, WU] + T[q, 2, WL])]

    def open_all(k, _):
        lax.fori_loop(0, 2, lambda b, c: run(8 * b, 1, 8, lambda i, q, memo: open_cols(k, i, q, b + 1)) or 0, 0)
        run(0, 3, 6, lambda i, q, memo: open_depths(k, i, q))
        return 0

    def open_outer(k, _):
        lax.fori_loop(0, 2, lambda b, c: run(12 * b, 1, 4, lambda i, q, memo: open_cols(k, i, 4 * b + q, b + 1)) or 0, 0)
        run(lambda b: 14 * b, 2, 4, lambda i, q, memo: open_depths(k, i, q))
        return 0

    def open_inner(k):
        lax.fori_loop(0, 2, lambda b, c: run(8 * b, 1, 8, lambda i, q, memo: open_cols(k, i, q, b + 1)) or 0, 0)
        run(4, 2, 5, lambda i, q, memo: open_depths(k, i, q))

    lax.fori_loop(3, LEVELS, open_all, 0)
    ar_middle(1)
    lax.fori_loop(0, 3, open_outer, 0)

    def erode_back(k, r, q, memo):
        g = G[k + 1, 0, r + 1] + G[k + 1, 1, r + 2] + G[k + 1, 2, r] + HZ[k, jnp.where((r > 6) & (r < 25), r - 6, 0)]
        j, by = place(r)
        under, c, over = [once(memo, q + d, lambda d=d: E[k, r + d, W]) for d in range(3)]
        gc, zl, zu, xl, xu, yl, yu = route(
            g, E[k + 1, r + 1, W],
            (c, E[k, r + 1, WL], E[k, r + 1, WU], under, over, LE[k, r]))
        T2[q, 0, W] = zl
        T2[q, 1, W] = zu
        return [(G, (k, 0, r + 1), gc + gather_sides(yl, yu, roll(SX2[k, j], by)) + T2[q, 0, WU] + T2[q, 1, WL]),
                (G, (k, 1, r + 1), xl), (G, (k, 2, r + 1), xu)]

    def outer(step, _):
        k = LEVELS - 1 - step
        run(lambda b: jnp.where(b < 2, 1 + k + 4 * b, 15 - k + 4 * b), 4, 4, lambda r, q, memo: erode_back(k, r, q, memo))
        return 0
    lax.fori_loop(0, LEVELS, outer, 0)

    beyond = pl.multiple_of(32 - 32 * gz, 8)
    mine = pl.multiple_of(8 * gz, 8)
    inner = pl.multiple_of(24 - 24 * gz, 8)
    quiet = pl.ds(mine, Z - 8)
    edge = pl.ds(inner, 8)
    back_rows = []

    def total(r, _, memo):
        v = G[0, 0, r + 1] + G[0, 1, r + 2] + G[0, 2, r]
        return [(F, (r,), v)]

    def from_depth(r, _, memo):
        return [(FO, (r, edge), F[r, pl.ds(mine + inner, 8)] + RZ[r])]

    def own_planes(r, _, memo):
        return [(FO, (r,), F[r, pl.ds(mine, Z)])]

    def return_rows(base, planes, now):
        back_rows.append(send(base, FO.at[pl.ds(1, 7), planes], RX.at[0, :, planes], below, -1, now))
        back_rows.append(send(base + 1, FO.at[pl.ds(24, 7), planes], RX.at[1, :, planes], above, 1, now))

    def to_depth(number, rows):
        return send(number, F.at[rows, pl.ds(beyond, 8)], RZ.at[rows], (1 - gz, gx, gy))

    for start in (1, 24):
        run(start, 1, 7, total)
    margin = [to_depth(16, pl.ds(1, 7)), to_depth(17, pl.ds(24, 7))]
    for start in (1, 24):
        run(start, 1, 7, own_planes)
    return_rows(18, quiet, True)
    return_rows(20, edge, False)

    def inside(step, _):
        k = LEVELS - 1 - step
        at = (k + 1) // 2

        @pl.when(k < 3)
        def _():
            open_inner(k)
        run(8 + 2 * at, 4 - at, 4, lambda r, q, memo: erode_back(k, r, q, memo))

        @pl.when(step == 1)
        def _():
            for copy in margin:
                copy.wait_recv()
            for start in (1, 24):
                run(start, 1, 7, from_depth)
            for copy in back_rows[2:]:
                copy.start()
        return 0
    lax.fori_loop(0, LEVELS, inside, 0)
    run(8, 2, 8, total)
    copy = to_depth(22, pl.ds(8, 16))
    run(8, 2, 8, own_planes)
    copy.wait_recv()
    run(8, 2, 8, from_depth)

    both, alone = ar_end(1)
    tsens = (both + 1.0) / (alone + 1.0)
    square = (tprec + tsens) * (tprec + tsens)
    voxels = float(2 * nx * 2 * Z * X * Y)
    by_prec = -2.0 * tsens * tsens / square / (pred_total + 1.0) * voxels
    by_sens = -2.0 * tprec * tprec / square / (alone + 1.0) * voxels
    loss[...] = 1.0 - 2.0 * tprec * tsens / (tprec + tsens)

    for copy in back_rows:
        copy.wait_recv()

    def give(x, _, memo, extra):
        g = FO[x + 8] + GB[0, x + 1] * CT[x + 1]
        if extra is not None:
            g = g + extra(x)
        g = g * by_prec + SK[1, x] * by_sens
        return [(out, (x,), g)]
    run(0, 1, 7, functools.partial(give, extra=lambda x: RX[1, x]))
    run(7, 1, 2, functools.partial(give, extra=None))
    run(9, 1, 7, functools.partial(give, extra=lambda x: RX[0, x - 9]))
    for copy in copies:
        copy.wait_send()


def local(prediction, label):
    nx = lax.axis_size("gx")
    nhi = nx // LO
    f32 = jnp.float32

    def vmem(*shape):
        return pltpu.VMEM(shape + (Y,), f32)

    grad, loss = pl.pallas_call(
        functools.partial(kernel, nx),
        out_shape=(jax.ShapeDtypeStruct((X, Z, Y), f32), jax.ShapeDtypeStruct((1, 1), f32)),
        in_specs=[pl.BlockSpec(memory_space=pl.ANY)] * 2,
        out_specs=[pl.BlockSpec(memory_space=pltpu.VMEM)] * 2,
        scratch_shapes=[
            vmem(Z * X), vmem(Z * X), pltpu.SemaphoreType.DMA((2,)),
            vmem(10, ROWS + 2, PAD), vmem(2, 7, 10, PAD),
            vmem(7, X + 2, Z), vmem(7, X, Z), vmem(7, 10, Z), vmem(7, 8, Z),
            vmem(6, X, Z), vmem(6, X, Z), vmem(6, 8, Z), vmem(6, 8, Z),
            vmem(7, X + 2, Z), vmem(7, 8, Z), vmem(X + 2, Z), vmem(8, Z),
            vmem(2, X, Z), vmem(8, Z),
            vmem(3, X + 4, Z), vmem(3, 10, Z), vmem(LEVELS, X + 3, WIN),
            vmem(7, 3, ROWS + 2, WIN), vmem(2, 3, 10, WIN),
            vmem(10, 3, PAD), vmem(10, 2, PAD), vmem(6, 8, Z), vmem(6, 8, WIN),
            vmem(6, ROWS, WIN), vmem(6, 8, WIN),
            vmem(6, X, Z), vmem(6, X, Z), vmem(6, 8, Z), vmem(6, 8, Z),
            vmem(ROWS, WIN), vmem(ROWS, Z), vmem(ROWS, 8), vmem(2, 7, Z),
            vmem(2, 2, WIN), vmem(2, 4, WIN),
            vmem(2, 8), vmem(2, GROUP, 8), vmem(2, 8), vmem(2, nhi, 8),
            pltpu.SemaphoreType.DMA((23,)), pltpu.SemaphoreType.DMA((23,)),
            pltpu.SemaphoreType.DMA((2, 2, GROUP)), pltpu.SemaphoreType.DMA((2, 2, GROUP)),
        ],
        compiler_params=pltpu.CompilerParams(
            collective_id=0, has_side_effects=True, vmem_limit_bytes=62 * 1024 * 1024),
    )(prediction.reshape(Z * X, Y), label.reshape(Z * X, Y))
    return loss.reshape(()), jnp.transpose(grad, (1, 0, 2))


def solution(mesh):
    in_specs = (P("gz", "gx", "gy"), P("gz", "gx", "gy"))
    out_specs = (P(), P("gz", "gx", "gy"))
    return jax.shard_map(local, mesh=mesh, in_specs=in_specs, out_specs=out_specs, check_vma=False)
```

```python
import functools

import jax
import jax.numpy as jnp
from jax import lax
from jax.experimental import pallas as pl
from jax.experimental.pallas import tpu as pltpu
from jax.sharding import PartitionSpec as P

LEVELS = 6
Z, X, Y = 32, 16, 128
WIN = Z + 8
PAD = WIN + 16
ROWS = X + 16
GROUP = 16
LO = 4
SEMS = 64
MESH = pl.DeviceIdType.MESH

W, WL, WU = pl.ds(8, WIN), pl.ds(7, WIN), pl.ds(9, WIN)


def lane_of(v):
    return lax.broadcasted_iota(jnp.int32, v.shape, 1)


def plane_of(v):
    return lax.broadcasted_iota(jnp.int32, v.shape, 0)


def roll(v, by):
    return pltpu.roll(v, by, 1)


def max3(a, b, c):
    return jnp.maximum(jnp.maximum(a, b), c)


def route(g, best, candidates):
    zero = jnp.zeros_like(g)
    parts = []
    for value in candidates:
        hit = value == best
        parts.append(jnp.where(hit, g, zero))
        g = jnp.where(hit, zero, g)
    parts.append(g)
    return parts


def run(start, blocks, size, row):
    def block(b, _):
        todo, memo = [], {}
        first = start(b) if callable(start) else start + b * size
        for q in range(size):
            todo += row(first + q, q, memo)
        for ref, at, value in todo:
            ref[at] = value
        return 0
    if isinstance(blocks, int) and blocks == 1:
        block(0, 0)
        return
    else:
        lax.fori_loop(0, blocks, block, 0)


def once(memo, key, load):
    if key not in memo:
        memo[key] = load()
    return memo[key]


def slot_of(f, k):
    if f == 0:
        return k
    if isinstance(k, int) and k == 0:
        return 7
    return jnp.where(k == 0, 7, 8 + lax.rem(k, 2))


def kernel(nx, pred_hbm, label_hbm, out, loss, pred, label, in_sem, E, S, M1, M2, SM1, SM2, D, SP, SD, SSP, GB, SGB, CT, SCT, SK, SSK,
           HX, SHX, HZ, G, SG, T, T2, SX, SX2, LE, SLE, LM, BM, SLM, SBM, F, FO, RZ, RX, PS, PR, ARS, AR1, AR2S, AR2,
           send_sem, recv_sem, ar_send, ar_recv):
    gz, gx, gy = lax.axis_index("gz"), lax.axis_index("gx"), lax.axis_index("gy")
    prev, nxt = lax.rem(gx + nx - 1, nx), lax.rem(gx + 1, nx)
    nhi = nx // LO
    hi, lo = gx // LO, lax.rem(gx, LO)
    me1 = (gz * LO + lo) * 2 + gy
    o = pl.multiple_of(8 + 8 * gz, 8)
    O, OL, OU = pl.ds(o, Z), pl.ds(o - 1, Z), pl.ds(o + 1, Z)
    seam = 127 * (1 - gy)
    zlow = jnp.where(gz == 0, 0, -1)
    zhigh = jnp.where(gz == 1, Z - 1, -1)
    first_lane = jnp.where(gx == 0, 32, 0)
    last_lane = jnp.where(gx == nx - 1, 96, 128)

    def member(i):
        return (i // (2 * LO), hi * LO + lax.rem(i // 2, LO), lax.rem(i, 2))

    loads = [pltpu.make_async_copy(src, dst, in_sem.at[f])
             for f, (src, dst) in enumerate(((pred_hbm, pred), (label_hbm, label)))]
    for load in loads:
        load.start()

    barrier = pltpu.get_barrier_semaphore()
    has_prev, has_nxt = gx > 0, gx < nx - 1
    for inside, row in ((has_prev, prev), (has_nxt, nxt)):
        @pl.when(inside)
        def _(row=row):
            for cols in (gy, 1 - gy):
                pl.semaphore_signal(barrier, inc=1, device_id=(gz, row, cols), device_id_type=MESH)
    greet = [member(lax.rem(me1 + d, GROUP)) for d in range(1, GROUP)]
    greet += [(gz, lax.rem(hi + d, nhi) * LO + lo, gy) for d in range(1, nhi)]
    for device in greet:
        pl.semaphore_signal(barrier, inc=1, device_id=device, device_id_type=MESH)

    def lay_out(f):
        ref = (pred, label)[f]
        loads[f].wait()

        def bring(x, _, memo):
            return [(E, (7 * f, 9 + x, pl.ds(o + 8 * t, 8)), ref[pl.ds(x + X * 8 * t, 8, stride=X), :])
                    for t in range(Z // 8)]
        run(0, 2, 8, bring)

    lay_out(0)
    zero_w = jnp.zeros((WIN, Y), jnp.float32)
    zero_o = jnp.zeros((Z, Y), jnp.float32)
    pl.semaphore_wait(barrier, len(greet) + jnp.where(has_prev, 2, 0) + jnp.where(has_nxt, 2, 0))

    copies = []

    def only(inside, act):
        if inside is None:
            act()
        else:
            pl.when(inside)(act)

    class Sent:
        def __init__(self, copy, sends, gets):
            self.copy, self.sends, self.gets = copy, sends, gets

        def start(self):
            only(self.sends, self.copy.start)

        def wait_recv(self):
            only(self.gets, self.copy.wait_recv)

        def wait_send(self):
            only(self.sends, self.copy.wait_send)

    def send(number, src, dst, device, step=0, now=True):
        copy = pltpu.make_async_remote_copy(
            src_ref=src, dst_ref=dst, send_sem=send_sem.at[number], recv_sem=recv_sem.at[number],
            device_id=device, device_id_type=MESH)
        sends = {0: None, -1: has_prev, 1: has_nxt}[step]
        gets = {0: None, -1: has_nxt, 1: has_prev}[step]
        copies.append(Sent(copy, sends, gets))
        if now:
            copies[-1].start()
        return copies[-1]

    near = pl.multiple_of(32 - 16 * gz, 8)
    far = pl.multiple_of(8 + 32 * gz, 8)
    below, above = (gz, prev, gy), (gz, nxt, gy)
    arrived = [[], []]

    def pass_rows(f, base, planes):
        arrived[f] += [
            send(base, E.at[7 * f, pl.ds(9, 7), planes], E.at[7 * f, pl.ds(25, 7), planes], below, -1),
            send(base + 1, E.at[7 * f, pl.ds(18, 7), planes], E.at[7 * f, pl.ds(2, 7), planes], above, 1)]

    def first_halos(f):
        copy = send(8 * f, E.at[7 * f, pl.ds(9, X), pl.ds(near, 8)], E.at[7 * f, pl.ds(9, X), pl.ds(far, 8)],
                    (1 - gz, gx, gy))
        pass_rows(f, 8 * f + 1, O)
        return copy

    def second_halos(f, depth):
        depth.wait_recv()
        pass_rows(f, 8 * f + 3, pl.ds(pl.multiple_of(40 - 32 * gz, 8), 8))
        for half in (0, 1):
            packed = zero_w
            for i in range(8):
                v = E[7 * f, 9 + 8 * half + i, W]
                packed = jnp.where(lane_of(v) // 16 == i, roll(v, lax.rem(16 * i + 16 * (1 - gy), 128)), packed)
            PS[f, half] = packed
        arrived[f] += [
            send(8 * f + 5, PS.at[f], PR.at[f, pl.ds(1, 2)], (gz, gx, 1 - gy)),
            send(8 * f + 6, PS.at[f, 0], PR.at[f, 3], (gz, prev, 1 - gy), -1),
            send(8 * f + 7, PS.at[f, 1], PR.at[f, 0], (gz, nxt, 1 - gy), 1)]

    depth = first_halos(0)
    lay_out(1)
    second_halos(0, depth)
    depth = first_halos(1)
    second_halos(1, depth)

    two = jnp.full((8, Y), 2.0, jnp.float32)

    def rims(r, _, memo):
        return [(E, (slot, r, pl.ds(at, 8)), two) for slot in range(10) for at in (0, PAD - 8)]
    run(0, 17, 2, rims)

    def strip_rims(j, _, memo):
        return [(S, (f, k, j, pl.ds(at, 8)), two)
                for f in (0, 1) for k in range(LEVELS + 1) for at in (0, PAD - 8)]
    run(1, 4, 2, strip_rims)
    run(0, 17, 2, lambda r, _, m: [(G, (p, q, r), zero_w) for p in range(LEVELS + 1) for q in range(3)])
    for k in range(LEVELS):
        HZ[k, 0] = zero_w
    run(0, 2, 5, lambda j, _, m: [(SG, (p, q, j), zero_w) for p in (0, 1) for q in range(3)])
    run(0, 4, 5, lambda i, _, m: [(HX, (q, i), zero_o) for q in range(3)])
    run(0, 4, 4, lambda i, _, m: [(SK, (0, i), zero_o), (SK, (1, i), zero_o), (GB, (LEVELS, i + 1), zero_o)])
    run(0, 1, 8, lambda j, _, m: [(SSK, (j,), zero_o), (SGB, (LEVELS, j), zero_o)])
    for k in range(LEVELS + 1):
        GB[k, 0] = zero_o
        CT[0] = zero_o
        CT[X + 1] = zero_o
        GB[k, X + 1] = zero_o
    for q in range(8):
        for p in range(3):
            T[q, p] = jnp.zeros((PAD, Y), jnp.float32)
        for p in range(2):
            T2[q, p] = jnp.zeros((PAD, Y), jnp.float32)
    for r in (0, 1, ROWS, ROWS + 1):
        for slot in range(10) if r in (0, ROWS + 1) else (0, 7):
            E[slot, r, W] = zero_w + 2.0

    @pl.when(gx == 0)
    def _():
        for f in (0, 1):
            PR[f, 0] = zero_w + 2.0
            for r in range(2, 9):
                E[7 * f, r, W] = zero_w + 2.0
        RX[1] = jnp.zeros((7, Z, Y), jnp.float32)

    @pl.when(gx == nx - 1)
    def _():
        for f in (0, 1):
            PR[f, 3] = zero_w + 2.0
            for r in range(25, 32):
                E[7 * f, r, W] = zero_w + 2.0
        RX[0] = jnp.zeros((7, Z, Y), jnp.float32)

    seam_turn = 111 + 2 * gy

    def place(r):
        g = lax.div(r, 8)
        return r - 8 * g, seam_turn - 32 * g

    def sides(v, seen):
        lane = lane_of(v)
        t = jnp.where(lane == seam, seen, v)
        return jnp.where(lane == 0, t, roll(v, 1)), jnp.where(lane == 127, t, roll(v, 127))

    def strip_sides(v):
        return roll(v, 1), roll(v, 127)

    def gather_sides(lower, upper, seen):
        lane = lane_of(lower)
        t = jnp.where(lane == seam, seen, 0.0)
        return jnp.where(lane == 127, t, roll(lower, 127)) + jnp.where(lane == 0, t, roll(upper, 1))

    def wrap_strip(ref, at, window, value):
        v = ref[at + (8, window)]
        v = jnp.where(lane_of(v) < first_lane, value, v)
        ref[at + (8, window)] = v
        ref[at + (0, window)] = roll(v, 32)
        v = ref[at + (1, window)]
        v = jnp.where(lane_of(v) >= last_lane, value, v)
        ref[at + (1, window)] = v
        ref[at + (9, window)] = roll(v, 96)

    def cap_rows(f, k):
        @pl.when(gx == 0)
        def _():
            E[slot_of(f, k), 8, W] = zero_w + 2.0

        @pl.when(gx == nx - 1)
        def _():
            E[slot_of(f, k), 25, W] = zero_w + 2.0

    def build_strip(f):
        def row(j, _, memo):
            acc = zero_w
            lane = lane_of(acc) // 16
            for g in range(4):
                own = roll(E[7 * f, 8 * g + j + 1, W], lax.rem(32 * g + 16, 128))
                other = roll(PR[f, g], lax.rem(32 * g - 16 * j + 16 * (1 - gy) + 128, 128))
                acc = jnp.where(lane == 2 * g + gy, own, acc)
                acc = jnp.where(lane == 2 * g + 1 - gy, other, acc)
            return [(S, (f, 0, j + 1, W), acc)]
        run(0, 2, 4, row)
        wrap_strip(S, (f, 0), W, 2.0)

    def eroded(ref, at, i, q, memo, pair):
        def centre(step):
            return once(memo, q + step, lambda: ref[at + (i + step, W)])
        c = centre(0)
        lower, upper = pair(c)
        m = jnp.minimum(jnp.minimum(c, lower), upper)
        m = jnp.minimum(m, jnp.minimum(ref[at + (i, WL)], ref[at + (i, WU)]))
        return jnp.minimum(m, jnp.minimum(centre(-1), centre(1))), lower

    def depth_max(ref, at, i):
        c = ref[at + (i, O)]
        plane = plane_of(c)
        lower = jnp.where(plane == zlow, c, ref[at + (i, OL)])
        upper = jnp.where(plane == zhigh, c, ref[at + (i, OU)])
        return max3(lower, c, upper)

    def level_forward(f, k, slot, first, rows):
        def strip_erode(j, q, memo):
            m, lower = eroded(S, (f, k), j + 1, q, memo, strip_sides)
            return [(S, (f, k + 1, j + 1, W), m)] + ([(SLE, (k, j), lower)] if f == 0 else [])
        run(0, 1, 8, strip_erode)
        wrap_strip(S, (f, k + 1), W, 2.0)

        def erode(r, q, memo):
            j, g = r % 8, r // 8
            seen = roll(S[f, k, j + 1, W], seam_turn - 32 * g)
            m, lower = eroded(E, (slot_of(f, k),), r + 1, q, memo, lambda c: sides(c, seen))
            if r in (7, 24):
                m = jnp.where(gx == (0 if r == 7 else nx - 1), zero_w + 2.0, m)
            return [(E, (slot_of(f, k + 1), r + 1, W), m)] + ([(LE, (k, r), lower)] if f == 0 else [])
        run(first, 1, rows, erode)

        def strip_depth(j, _, memo):
            return [(SM1, (slot, j + 1), depth_max(S, (f, k + 1), j + 1))]
        run(0, 1, 8, strip_depth)
        wrap_strip(SM1, (slot,), slice(None), 0.0)

        def strip_rows(j, q, memo):
            v = max3(*[once(memo, q + d, lambda d=d: SM1[slot, j + d]) for d in range(3)])
            todo = [(SM2, (slot, j), v)]
            if f == 0:
                lower, upper = strip_sides(v)
                best = max3(lower, v, upper)
                delta = jnp.maximum(S[f, k, j + 1, O] - best, 0.0)
                prior = SSK[j]
                todo += [(SLM, (k, j), lower), (SBM, (k, j), best), (SD, (k, j), delta), (SSP, (k, j), prior),
                         (SSK, (j,), prior + jnp.maximum(delta - prior * delta, 0.0))]
            return todo
        run(0, 1, 8, strip_rows)

        def depth_rows(i, _, memo):
            m = depth_max(E, (slot_of(f, k + 1),), i + 8)
            if i in (0, X + 1):
                m = jnp.where(gx == (0 if i == 0 else nx - 1), zero_o, m)
            return [(M1, (slot, i), m)]
        run(0, 1, X + 2, depth_rows)

        def rest(i, q, memo):
            v = max3(*[once(memo, q + d, lambda d=d: M1[slot, i + d]) for d in range(3)])
            r = i + 8
            lower, upper = sides(v, roll(SM2[slot, i % 8], seam_turn - 32 * (r // 8)))
            best = max3(lower, v, upper)
            delta = jnp.maximum(E[slot_of(f, k), r + 1, O] - best, 0.0)
            prior = SK[f, i]
            todo = [(M2, (slot, i), v), (SK, (f, i), prior + jnp.maximum(delta - prior * delta, 0.0))]
            if f == 0:
                todo += [(D, (k, i), delta), (SP, (k, i), prior), (LM, (k, i), lower), (BM, (k, i), best)]
            return todo
        run(0, 1, X, rest)

    def ar_copy(n, phase, slot, src, dst, number, device):
        return pltpu.make_async_remote_copy(
            src_ref=src, dst_ref=dst, send_sem=ar_send.at[n, phase, number], recv_sem=ar_recv.at[n, phase, slot],
            device_id=device, device_id_type=MESH)

    def ar_first(n, d):
        return ar_copy(n, 0, me1, ARS.at[n], AR1.at[n, me1], d, member(lax.rem(me1 + d, GROUP)))

    def ar_second(n, d):
        return ar_copy(n, 1, hi, AR2S.at[n], AR2.at[n, hi], d, (gz, lax.rem(hi + d, nhi) * LO + lo, gy))

    def ar_start(n, f):
        def add(b, carry):
            both, alone = carry
            for q in range(4):
                v = SK[f, 4 * b + q]
                both, alone = both + v * E[7 - 7 * f, 4 * b + q + 9, O], alone + v
            return both, alone
        both, alone = lax.fori_loop(0, X // 4, add, (zero_o, zero_o))
        both = jnp.sum(both, axis=0, keepdims=True)
        alone = jnp.sum(alone, axis=0, keepdims=True)
        sub = plane_of(two)
        tile = jnp.where(sub == 0, both, jnp.where(sub == 1, alone, 0.0))
        ARS[n] = tile
        AR1[n, me1] = tile
        for d in range(1, GROUP):
            ar_first(n, d).start()

    def ar_middle(n):
        for d in range(1, GROUP):
            s = lax.rem(me1 + d, GROUP)
            ar_copy(n, 0, s, ARS.at[n], AR1.at[n, s], d, member(s)).wait_recv()
        tile = AR1[n, 0]
        for s in range(1, GROUP):
            tile = tile + AR1[n, s]
        AR2S[n] = tile
        AR2[n, hi] = tile
        for d in range(1, nhi):
            ar_second(n, d).start()

    def ar_end(n):
        for d in range(1, nhi):
            s = lax.rem(hi + d, nhi)
            ar_copy(n, 1, s, AR2S.at[n], AR2.at[n, s], d, (gz, s * LO + lo, gy)).wait_recv()
        tile = AR2[n, 0]
        for s in range(1, nhi):
            tile = tile + AR2[n, s]
        for d in range(1, GROUP):
            ar_first(n, d).wait_send()
        for d in range(1, nhi):
            ar_second(n, d).wait_send()
        tile = jnp.sum(tile, axis=1, keepdims=True)
        return tile[0:1], tile[1:2]

    for f in (0, 1):
        for copy in arrived[f]:
            copy.wait_recv()
        cap_rows(f, 0)
        build_strip(f)

        def level(first, rows, k, f=f):
            level_forward(f, k, k if f == 0 else LEVELS, first, rows)
            if f == 1 and rows == 28:
                @pl.when(k == 2)
                def _():
                    ar_middle(0)
            return 0
        lax.fori_loop(0, 4, lambda k, _: level(2, 28, k), 0)
        lax.fori_loop(4, LEVELS, lambda k, _: level(6, 20, k), 0)
        ar_start(f, f)

    def chain(i, _, memo):
        t = zero_o + 1.0
        todo = []
        for k in range(LEVELS - 1, -1, -1):
            delta, prior = D[k, i], SP[k, i]
            on = delta - prior * delta > 0
            GB[k, i + 1] = jnp.where(on, t * (1.0 - prior), 0.0)
            t = jnp.where(on, t * (1.0 - delta), t)
        return todo
    run(0, 4, 4, chain)

    def strip_chain(j, _, memo):
        t = zero_o + 1.0
        lane = lane_of(t)
        mine = (lane >= 32) & (lane < 96)
        for k in range(LEVELS - 1, -1, -1):
            delta, prior = SD[k, j], SSP[k, j]
            on = delta - prior * delta > 0
            SGB[k, j] = jnp.where(on & mine, t * (1.0 - prior), 0.0)
            t = jnp.where(on, t * (1.0 - delta), t)
        return []
    run(0, 2, 4, strip_chain)

    both, alone = ar_end(0)
    pred_total = alone
    tprec = (both + 1.0) / (pred_total + 1.0)

    run(0, 2, 8, lambda i, _, m: [(CT, (i + 1,), E[7, i + 9, O] - tprec)])
    run(0, 1, 8, lambda j, _, m: [(SCT, (j,), S[1, 0, j + 1, O] - tprec)])

    def strip_back(step, _):
        k = LEVELS - 1 - step
        old = lax.rem(step, 2)
        new = 1 - old

        def strip_cols(j, _, memo):
            a = SM2[k, j]
            gc, gl, gu = route(-SGB[k, j] * SCT[j], SBM[k, j], (a, SLM[k, j]))
            todo = [(SX, (k, j), jnp.where(gy == 0, gl, gu))]
            g = gc + roll(gl, 127) + roll(gu, 1)
            gc, gl, gu = route(g, a, (SM1[k, j + 1], SM1[k, j]))
            return todo + [(SHX, (0, j + 1), gc), (SHX, (1, j + 1), gl), (SHX, (2, j + 1), gu)]
        run(0, 1, 8, strip_cols)
        SHX[1, 9] = roll(SHX[1, 1], 96)
        SHX[2, 0] = roll(SHX[2, 8], 32)

        def strip_depth(j, q, memo):
            g = SHX[0, j + 1] + SHX[1, j + 2] + SHX[2, j]
            gc, gl, gu = route(g, SM1[k, j + 1], (S[0, k + 1, j + 1, O], S[0, k + 1, j + 1, OL]))
            T[q, 0, O] = gc + SGB[k + 1, j] * SCT[j]
            T[q, 1, O] = gl
            T[q, 2, O] = gu
            g = SG[old, 0, j + 1] + SG[old, 1, j + 2] + SG[old, 2, j]
            g = g + T[q, 0, W] + T[q, 1, WU] + T[q, 2, WL]
            c = S[0, k, j + 1, W]
            gc, zl, zu, xl, xu, yl, yu = route(
                g, S[0, k + 1, j + 1, W],
                (c, S[0, k, j + 1, WL], S[0, k, j + 1, WU], S[0, k, j, W], S[0, k, j + 2, W], SLE[k, j]))
            T2[q, 0, W] = zl
            T2[q, 1, W] = zu
            return [(SX2, (k, j), jnp.where(gy == 0, yl, yu)),
                    (SG, (new, 0, j + 1), gc + roll(yl, 127) + roll(yu, 1) + T2[q, 0, WU] + T2[q, 1, WL]),
                    (SG, (new, 1, j + 1), xl), (SG, (new, 2, j + 1), xu)]
        run(0, 1, 8, strip_depth)
        SG[new, 1, 9] = roll(SG[new, 1, 1], 96)
        SG[new, 2, 0] = roll(SG[new, 2, 8], 32)
        return 0
    lax.fori_loop(0, LEVELS, strip_back, 0)

    def open_cols(k, i, j, g):
        a = M2[k, i]
        by = seam_turn - 32 * g
        gc, gl, gu = route(-GB[k, i + 1] * CT[i + 1], BM[k, i], (a, LM[k, i]))
        g = gc + gather_sides(gl, gu, roll(SX[k, j], by))
        gc, gl, gu = route(g, a, (M1[k, i + 1], M1[k, i]))
        return [(HX, (0, i + 2), gc), (HX, (1, i + 2), gl), (HX, (2, i + 2), gu)]

    def open_depths(k, i, q):
        g = HX[0, i + 1] + HX[1, i + 2] + HX[2, i]
        gc, gl, gu = route(g, M1[k, i], (E[k + 1, i + 8, O], E[k + 1, i + 8, OL]))
        T[q, 0, O] = gc + GB[k + 1, i] * CT[i]
        T[q, 1, O] = gl
        T[q, 2, O] = gu
        return [(HZ, (k, i + 1), T[q, 0, W] + T[q, 1, WU] + T[q, 2, WL])]

    def open_all(k, _):
        lax.fori_loop(0, 2, lambda b, c: run(8 * b, 1, 8, lambda i, q, memo: open_cols(k, i, q, b + 1)) or 0, 0)
        run(0, 3, 6, lambda i, q, memo: open_depths(k, i, q))
        return 0

    def open_outer(k, _):
        lax.fori_loop(0, 2, lambda b, c: run(12 * b, 1, 4, lambda i, q, memo: open_cols(k, i, 4 * b + q, b + 1)) or 0, 0)
        run(lambda b: 14 * b, 2, 4, lambda i, q, memo: open_depths(k, i, q))
        return 0

    def open_inner(k):
        lax.fori_loop(0, 2, lambda b, c: run(8 * b, 1, 8, lambda i, q, memo: open_cols(k, i, q, b + 1)) or 0, 0)
        run(4, 2, 5, lambda i, q, memo: open_depths(k, i, q))

    lax.fori_loop(3, LEVELS, open_all, 0)
    ar_middle(1)
    lax.fori_loop(0, 3, open_outer, 0)

    def erode_back(k, r, q, memo):
        g = G[k + 1, 0, r + 1] + G[k + 1, 1, r + 2] + G[k + 1, 2, r] + HZ[k, jnp.where((r > 6) & (r < 25), r - 6, 0)]
        j, by = place(r)
        under, c, over = [once(memo, q + d, lambda d=d: E[k, r + d, W]) for d in range(3)]
        gc, zl, zu, xl, xu, yl, yu = route(
            g, E[k + 1, r + 1, W],
            (c, E[k, r + 1, WL], E[k, r + 1, WU], under, over, LE[k, r]))
        T2[q, 0, W] = zl
        T2[q, 1, W] = zu
        return [(G, (k, 0, r + 1), gc + gather_sides(yl, yu, roll(SX2[k, j], by)) + T2[q, 0, WU] + T2[q, 1, WL]),
                (G, (k, 1, r + 1), xl), (G, (k, 2, r + 1), xu)]

    def outer(step, _):
        k = LEVELS - 1 - step
        run(lambda b: jnp.where(b == 0, 2 + k, 23 - k), 2, 7, lambda r, q, memo: erode_back(k, r, q, memo))
        return 0
    lax.fori_loop(0, LEVELS, outer, 0)

    beyond = pl.multiple_of(32 - 32 * gz, 8)
    mine = pl.multiple_of(8 * gz, 8)
    inner = pl.multiple_of(24 - 24 * gz, 8)
    quiet = pl.ds(mine, Z - 8)
    edge = pl.ds(inner, 8)
    back_rows = []

    def total(r, _, memo):
        v = G[0, 0, r + 1] + G[0, 1, r + 2] + G[0, 2, r]
        return [(F, (r,), v)]

    def from_depth(r, _, memo):
        return [(FO, (r, edge), F[r, pl.ds(mine + inner, 8)] + RZ[r])]

    def own_planes(r, _, memo):
        return [(FO, (r,), F[r, pl.ds(mine, Z)])]

    def return_rows(base, planes, now):
        back_rows.append(send(base, FO.at[pl.ds(1, 7), planes], RX.at[0, :, planes], below, -1, now))
        back_rows.append(send(base + 1, FO.at[pl.ds(24, 7), planes], RX.at[1, :, planes], above, 1, now))

    def to_depth(number, rows):
        return send(number, F.at[rows, pl.ds(beyond, 8)], RZ.at[rows], (1 - gz, gx, gy))

    for start in (1, 24):
        run(start, 1, 7, total)
    margin = [to_depth(16, pl.ds(1, 7)), to_depth(17, pl.ds(24, 7))]
    for start in (1, 24):
        run(start, 1, 7, own_planes)
    return_rows(18, quiet, True)
    return_rows(20, edge, False)

    def inside(step, _):
        k = LEVELS - 1 - step
        at = (k + 1) // 2

        @pl.when(k < 3)
        def _():
            open_inner(k)
        run(8 + 2 * at, 4 - at, 4, lambda r, q, memo: erode_back(k, r, q, memo))

        @pl.when(step == 1)
        def _():
            for copy in margin:
                copy.wait_recv()
            for start in (1, 24):
                run(start, 1, 7, from_depth)
            for copy in back_rows[2:]:
                copy.start()
        return 0
    lax.fori_loop(0, LEVELS, inside, 0)
    run(8, 2, 8, total)
    copy = to_depth(22, pl.ds(8, 16))
    run(8, 2, 8, own_planes)
    copy.wait_recv()
    run(8, 2, 8, from_depth)

    both, alone = ar_end(1)
    tsens = (both + 1.0) / (alone + 1.0)
    square = (tprec + tsens) * (tprec + tsens)
    voxels = float(2 * nx * 2 * Z * X * Y)
    by_prec = -2.0 * tsens * tsens / square / (pred_total + 1.0) * voxels
    by_sens = -2.0 * tprec * tprec / square / (alone + 1.0) * voxels
    loss[...] = 1.0 - 2.0 * tprec * tsens / (tprec + tsens)

    for copy in back_rows:
        copy.wait_recv()

    def give(x, _, memo, extra):
        g = FO[x + 8] + GB[0, x + 1] * CT[x + 1]
        if extra is not None:
            g = g + extra(x)
        g = g * by_prec + SK[1, x] * by_sens
        return [(out, (x,), g)]
    run(0, 1, 7, functools.partial(give, extra=lambda x: RX[1, x]))
    run(7, 1, 2, functools.partial(give, extra=None))
    run(9, 1, 7, functools.partial(give, extra=lambda x: RX[0, x - 9]))
    for copy in copies:
        copy.wait_send()


def local(prediction, label):
    nx = lax.axis_size("gx")
    nhi = nx // LO
    f32 = jnp.float32

    def vmem(*shape):
        return pltpu.VMEM(shape + (Y,), f32)

    grad, loss = pl.pallas_call(
        functools.partial(kernel, nx),
        out_shape=(jax.ShapeDtypeStruct((X, Z, Y), f32), jax.ShapeDtypeStruct((1, 1), f32)),
        in_specs=[pl.BlockSpec(memory_space=pl.ANY)] * 2,
        out_specs=[pl.BlockSpec(memory_space=pltpu.VMEM)] * 2,
        scratch_shapes=[
            vmem(Z * X), vmem(Z * X), pltpu.SemaphoreType.DMA((2,)),
            vmem(10, ROWS + 2, PAD), vmem(2, 7, 10, PAD),
            vmem(7, X + 2, Z), vmem(7, X, Z), vmem(7, 10, Z), vmem(7, 8, Z),
            vmem(6, X, Z), vmem(6, X, Z), vmem(6, 8, Z), vmem(6, 8, Z),
            vmem(7, X + 2, Z), vmem(7, 8, Z), vmem(X + 2, Z), vmem(8, Z),
            vmem(2, X, Z), vmem(8, Z),
            vmem(3, X + 4, Z), vmem(3, 10, Z), vmem(LEVELS, X + 3, WIN),
            vmem(7, 3, ROWS + 2, WIN), vmem(2, 3, 10, WIN),
            vmem(8, 3, PAD), vmem(8, 2, PAD), vmem(6, 8, Z), vmem(6, 8, WIN),
            vmem(6, ROWS, WIN), vmem(6, 8, WIN),
            vmem(6, X, Z), vmem(6, X, Z), vmem(6, 8, Z), vmem(6, 8, Z),
            vmem(ROWS, WIN), vmem(ROWS, Z), vmem(ROWS, 8), vmem(2, 7, Z),
            vmem(2, 2, WIN), vmem(2, 4, WIN),
            vmem(2, 8), vmem(2, GROUP, 8), vmem(2, 8), vmem(2, nhi, 8),
            pltpu.SemaphoreType.DMA((23,)), pltpu.SemaphoreType.DMA((23,)),
            pltpu.SemaphoreType.DMA((2, 2, GROUP)), pltpu.SemaphoreType.DMA((2, 2, GROUP)),
        ],
        compiler_params=pltpu.CompilerParams(
            collective_id=0, has_side_effects=True, vmem_limit_bytes=62 * 1024 * 1024),
    )(prediction.reshape(Z * X, Y), label.reshape(Z * X, Y))
    return loss.reshape(()), jnp.transpose(grad, (1, 0, 2))


def solution(mesh):
    in_specs = (P("gz", "gx", "gy"), P("gz", "gx", "gy"))
    out_specs = (P(), P("gz", "gx", "gy"))
    return jax.shard_map(local, mesh=mesh, in_specs=in_specs, out_specs=out_specs, check_vma=False)
```

```python
import functools

import jax
import jax.numpy as jnp
from jax import lax
from jax.experimental import pallas as pl
from jax.experimental.pallas import tpu as pltpu
from jax.sharding import PartitionSpec as P

LEVELS = 6
Z, X, Y = 32, 16, 128
WIN = Z + 8
PAD = WIN + 16
ROWS = X + 16
GROUP = 8
LO = 2
SEMS = 64
MESH = pl.DeviceIdType.MESH

W, WL, WU = pl.ds(8, WIN), pl.ds(7, WIN), pl.ds(9, WIN)


def lane_of(v):
    return lax.broadcasted_iota(jnp.int32, v.shape, 1)


def plane_of(v):
    return lax.broadcasted_iota(jnp.int32, v.shape, 0)


def roll(v, by):
    return pltpu.roll(v, by, 1)


def max3(a, b, c):
    return jnp.maximum(jnp.maximum(a, b), c)


def route(g, best, candidates):
    zero = jnp.zeros_like(g)
    parts = []
    for value in candidates:
        hit = value == best
        part = jnp.where(hit, g, zero)
        parts.append(part)
        g = g - part
    parts.append(g)
    return parts


def run(start, blocks, size, row):
    def block(b, _):
        todo, memo = [], {}
        first = start(b) if callable(start) else start + b * size
        for q in range(size):
            todo += row(first + q, q, memo)
        for ref, at, value in todo:
            ref[at] = value
        return 0
    if isinstance(blocks, int) and blocks == 1:
        block(0, 0)
        return
    else:
        lax.fori_loop(0, blocks, block, 0)


def once(memo, key, load):
    if key not in memo:
        memo[key] = load()
    return memo[key]


def slot_of(f, k):
    if f == 0:
        return k
    if isinstance(k, int) and k == 0:
        return 7
    return jnp.where(k == 0, 7, 8 + lax.rem(k, 2))


def kernel(nx, pred_hbm, label_hbm, out, loss, pred, label, in_sem, E, S, M1, M2, SM1, SM2, SP, SSP, GB, SGB, CT, SCT, SK, SSK,
           HX, SHX, HZ, G, SG, T, T2, SX, SX2, LE, SLE, LM, BM, SLM, SBM, F, FO, RZ, RX, PS, PR, ARS, AR1, AR2S, AR2,
           send_sem, recv_sem, ar_send, ar_recv):
    gz, gx, gy = lax.axis_index("gz"), lax.axis_index("gx"), lax.axis_index("gy")
    prev, nxt = lax.rem(gx + nx - 1, nx), lax.rem(gx + 1, nx)
    nhi = nx // LO
    hi, lo = gx // LO, lax.rem(gx, LO)
    me1 = (gz * LO + lo) * 2 + gy
    o = pl.multiple_of(8 + 8 * gz, 8)
    O, OL, OU = pl.ds(o, Z), pl.ds(o - 1, Z), pl.ds(o + 1, Z)
    seam = 127 * (1 - gy)
    zlow = jnp.where(gz == 0, 0, -1)
    zhigh = jnp.where(gz == 1, Z - 1, -1)
    first_lane = jnp.where(gx == 0, 32, 0)
    last_lane = jnp.where(gx == nx - 1, 96, 128)

    def member(i):
        return (i // (2 * LO), hi * LO + lax.rem(i // 2, LO), lax.rem(i, 2))

    loads = [pltpu.make_async_copy(src, dst, in_sem.at[f])
             for f, (src, dst) in enumerate(((pred_hbm, pred), (label_hbm, label)))]
    for load in loads:
        load.start()

    barrier = pltpu.get_barrier_semaphore()
    has_prev, has_nxt = gx > 0, gx < nx - 1
    for inside, row in ((has_prev, prev), (has_nxt, nxt)):
        @pl.when(inside)
        def _(row=row):
            for cols in (gy, 1 - gy):
                pl.semaphore_signal(barrier, inc=1, device_id=(gz, row, cols), device_id_type=MESH)
    greet = [member(lax.rem(me1 + d, GROUP)) for d in range(1, GROUP)]
    greet += [(gz, lax.rem(hi + d, nhi) * LO + lo, gy) for d in range(1, nhi)]
    for device in greet:
        pl.semaphore_signal(barrier, inc=1, device_id=device, device_id_type=MESH)

    def lay_out(f):
        ref = (pred, label)[f]
        loads[f].wait()

        def bring(x, _, memo):
            return [(E, (7 * f, 9 + x, pl.ds(o + 8 * t, 8)), ref[pl.ds(x + X * 8 * t, 8, stride=X), :])
                    for t in range(Z // 8)]
        run(0, 2, 8, bring)

    lay_out(0)
    zero_w = jnp.zeros((WIN, Y), jnp.float32)
    zero_o = jnp.zeros((Z, Y), jnp.float32)
    pl.semaphore_wait(barrier, len(greet) + jnp.where(has_prev, 2, 0) + jnp.where(has_nxt, 2, 0))

    copies = []

    def only(inside, act):
        if inside is None:
            act()
        else:
            pl.when(inside)(act)

    class Sent:
        def __init__(self, copy, sends, gets):
            self.copy, self.sends, self.gets = copy, sends, gets

        def start(self):
            only(self.sends, self.copy.start)

        def wait_recv(self):
            only(self.gets, self.copy.wait_recv)

        def wait_send(self):
            only(self.sends, self.copy.wait_send)

    def send(number, src, dst, device, step=0, now=True):
        copy = pltpu.make_async_remote_copy(
            src_ref=src, dst_ref=dst, send_sem=send_sem.at[number], recv_sem=recv_sem.at[number],
            device_id=device, device_id_type=MESH)
        sends = {0: None, -1: has_prev, 1: has_nxt}[step]
        gets = {0: None, -1: has_nxt, 1: has_prev}[step]
        copies.append(Sent(copy, sends, gets))
        if now:
            copies[-1].start()
        return copies[-1]

    near = pl.multiple_of(32 - 16 * gz, 8)
    far = pl.multiple_of(8 + 32 * gz, 8)
    below, above = (gz, prev, gy), (gz, nxt, gy)
    arrived = [[], []]

    def pass_rows(f, base, planes):
        arrived[f] += [
            send(base, E.at[7 * f, pl.ds(9, 7), planes], E.at[7 * f, pl.ds(25, 7), planes], below, -1),
            send(base + 1, E.at[7 * f, pl.ds(18, 7), planes], E.at[7 * f, pl.ds(2, 7), planes], above, 1)]

    def first_halos(f):
        copy = send(8 * f, E.at[7 * f, pl.ds(9, X), pl.ds(near, 8)], E.at[7 * f, pl.ds(9, X), pl.ds(far, 8)],
                    (1 - gz, gx, gy))
        pass_rows(f, 8 * f + 1, O)
        return copy

    def second_halos(f, depth):
        depth.wait_recv()
        pass_rows(f, 8 * f + 3, pl.ds(pl.multiple_of(40 - 32 * gz, 8), 8))
        for half in (0, 1):
            packed = zero_w
            for i in range(8):
                v = E[7 * f, 9 + 8 * half + i, W]
                packed = jnp.where(lane_of(v) // 16 == i, roll(v, lax.rem(16 * i + 16 * (1 - gy), 128)), packed)
            PS[f, half] = packed
        arrived[f] += [
            send(8 * f + 5, PS.at[f], PR.at[f, pl.ds(1, 2)], (gz, gx, 1 - gy)),
            send(8 * f + 6, PS.at[f, 0], PR.at[f, 3], (gz, prev, 1 - gy), -1),
            send(8 * f + 7, PS.at[f, 1], PR.at[f, 0], (gz, nxt, 1 - gy), 1)]

    depth = first_halos(0)
    lay_out(1)
    second_halos(0, depth)
    depth = first_halos(1)
    second_halos(1, depth)

    two = jnp.full((8, Y), 2.0, jnp.float32)

    def rims(r, _, memo):
        return [(E, (slot, r, pl.ds(at, 8)), two) for slot in range(10) for at in (0, PAD - 8)]
    run(0, 17, 2, rims)

    def strip_rims(j, _, memo):
        return [(S, (f, k, j, pl.ds(at, 8)), two)
                for f in (0, 1) for k in range(LEVELS + 1) for at in (0, PAD - 8)]
    run(1, 4, 2, strip_rims)
    run(0, 17, 2, lambda r, _, m: [(G, (p, q, r), zero_w) for p in range(LEVELS + 1) for q in range(3)])
    for k in range(LEVELS):
        HZ[k, 0] = zero_w
    run(0, 2, 5, lambda j, _, m: [(SG, (p, q, j), zero_w) for p in (0, 1) for q in range(3)])
    run(0, 4, 5, lambda i, _, m: [(HX, (q, i), zero_o) for q in range(3)])
    run(0, 4, 4, lambda i, _, m: [(SK, (0, i), zero_o), (SK, (1, i), zero_o), (GB, (LEVELS, i + 1), zero_o)])
    run(0, 1, 8, lambda j, _, m: [(SSK, (j,), zero_o), (SGB, (LEVELS, j), zero_o)])
    for k in range(LEVELS + 1):
        GB[k, 0] = zero_o
        CT[0] = zero_o
        CT[X + 1] = zero_o
        GB[k, X + 1] = zero_o
    for q in range(8):
        for p in range(3):
            T[q, p] = jnp.zeros((PAD, Y), jnp.float32)
    for q in range(8):
        for p in range(2):
            T2[q, p] = jnp.zeros((PAD, Y), jnp.float32)
    for r in (0, 1, ROWS, ROWS + 1):
        for slot in range(10) if r in (0, ROWS + 1) else (0, 7):
            E[slot, r, W] = zero_w + 2.0

    @pl.when(gx == 0)
    def _():
        for f in (0, 1):
            PR[f, 0] = zero_w + 2.0
            for r in range(2, 9):
                E[7 * f, r, W] = zero_w + 2.0
        RX[1] = jnp.zeros((7, Z, Y), jnp.float32)

    @pl.when(gx == nx - 1)
    def _():
        for f in (0, 1):
            PR[f, 3] = zero_w + 2.0
            for r in range(25, 32):
                E[7 * f, r, W] = zero_w + 2.0
        RX[0] = jnp.zeros((7, Z, Y), jnp.float32)

    seam_turn = 111 + 2 * gy

    def place(r):
        g = lax.div(r, 8)
        return r - 8 * g, seam_turn - 32 * g

    def sides(v, seen):
        lane = lane_of(v)
        t = jnp.where(lane == seam, seen, v)
        return jnp.where(lane == 0, t, roll(v, 1)), jnp.where(lane == 127, t, roll(v, 127))

    def strip_sides(v):
        return roll(v, 1), roll(v, 127)

    def gather_sides(lower, upper, seen):
        lane = lane_of(lower)
        t = jnp.where(lane == seam, seen, 0.0)
        return jnp.where(lane == 127, t, roll(lower, 127)) + jnp.where(lane == 0, t, roll(upper, 1))

    def wrap_strip(ref, at, window, value):
        v = ref[at + (8, window)]
        v = jnp.where(lane_of(v) < first_lane, value, v)
        ref[at + (8, window)] = v
        ref[at + (0, window)] = roll(v, 32)
        v = ref[at + (1, window)]
        v = jnp.where(lane_of(v) >= last_lane, value, v)
        ref[at + (1, window)] = v
        ref[at + (9, window)] = roll(v, 96)

    def cap_rows(f, k):
        @pl.when(gx == 0)
        def _():
            E[slot_of(f, k), 8, W] = zero_w + 2.0

        @pl.when(gx == nx - 1)
        def _():
            E[slot_of(f, k), 25, W] = zero_w + 2.0

    def build_strip(f):
        def row(j, _, memo):
            acc = zero_w
            lane = lane_of(acc) // 16
            for g in range(4):
                own = roll(E[7 * f, 8 * g + j + 1, W], lax.rem(32 * g + 16, 128))
                other = roll(PR[f, g], lax.rem(32 * g - 16 * j + 16 * (1 - gy) + 128, 128))
                acc = jnp.where(lane == 2 * g + gy, own, acc)
                acc = jnp.where(lane == 2 * g + 1 - gy, other, acc)
            return [(S, (f, 0, j + 1, W), acc)]
        run(0, 2, 4, row)
        wrap_strip(S, (f, 0), W, 2.0)

    def eroded(ref, at, i, q, memo, pair):
        def centre(step):
            return once(memo, q + step, lambda: ref[at + (i + step, W)])
        c = centre(0)
        lower, upper = pair(c)
        m = jnp.minimum(jnp.minimum(c, lower), upper)
        m = jnp.minimum(m, jnp.minimum(ref[at + (i, WL)], ref[at + (i, WU)]))
        return jnp.minimum(m, jnp.minimum(centre(-1), centre(1))), lower

    def depth_max(ref, at, i):
        c = ref[at + (i, O)]
        plane = plane_of(c)
        lower = jnp.where(plane == zlow, c, ref[at + (i, OL)])
        upper = jnp.where(plane == zhigh, c, ref[at + (i, OU)])
        return max3(lower, c, upper)

    def level_forward(f, k, slot, first, rows):
        def strip_erode(j, q, memo):
            m, lower = eroded(S, (f, k), j + 1, q, memo, strip_sides)
            return [(S, (f, k + 1, j + 1, W), m)] + ([(SLE, (k, j), lower)] if f == 0 else [])
        run(0, 1, 8, strip_erode)
        wrap_strip(S, (f, k + 1), W, 2.0)

        def erode(r, q, memo):
            j, g = r % 8, r // 8
            seen = roll(S[f, k, j + 1, W], seam_turn - 32 * g)
            m, lower = eroded(E, (slot_of(f, k),), r + 1, q, memo, lambda c: sides(c, seen))
            if r in (7, 24):
                m = jnp.where(gx == (0 if r == 7 else nx - 1), zero_w + 2.0, m)
            return [(E, (slot_of(f, k + 1), r + 1, W), m)] + ([(LE, (k, r), lower)] if f == 0 else [])
        run(first, 1, rows, erode)

        def strip_depth(j, _, memo):
            return [(SM1, (slot, j + 1), depth_max(S, (f, k + 1), j + 1))]
        run(0, 1, 8, strip_depth)
        wrap_strip(SM1, (slot,), slice(None), 0.0)

        def strip_rows(j, q, memo):
            v = max3(*[once(memo, q + d, lambda d=d: SM1[slot, j + d]) for d in range(3)])
            todo = [(SM2, (slot, j), v)]
            if f == 0:
                lower, upper = strip_sides(v)
                best = max3(lower, v, upper)
                delta = jnp.maximum(S[f, k, j + 1, O] - best, 0.0)
                prior = SSK[j]
                todo += [(SLM, (k, j), lower), (SBM, (k, j), best), (SGB, (k, j), delta), (SSP, (k, j), prior),
                         (SSK, (j,), prior + jnp.maximum(delta - prior * delta, 0.0))]
            return todo
        run(0, 1, 8, strip_rows)

        def depth_rows(i, _, memo):
            m = depth_max(E, (slot_of(f, k + 1),), i + 8)
            if i in (0, X + 1):
                m = jnp.where(gx == (0 if i == 0 else nx - 1), zero_o, m)
            return [(M1, (slot, i), m)]
        run(0, 1, X + 2, depth_rows)

        def rest(i, q, memo):
            v = max3(*[once(memo, q + d, lambda d=d: M1[slot, i + d]) for d in range(3)])
            r = i + 8
            lower, upper = sides(v, roll(SM2[slot, i % 8], seam_turn - 32 * (r // 8)))
            best = max3(lower, v, upper)
            delta = jnp.maximum(E[slot_of(f, k), r + 1, O] - best, 0.0)
            prior = SK[f, i]
            todo = [(SK, (f, i), prior + jnp.maximum(delta - prior * delta, 0.0))]
            if f == 0:
                todo += [(M2, (k, i), v), (GB, (k, i + 1), delta), (SP, (k, i), prior), (LM, (k, i), lower), (BM, (k, i), best)]
            return todo
        run(0, 1, X, rest)

    def ar_copy(n, phase, slot, src, dst, number, device):
        return pltpu.make_async_remote_copy(
            src_ref=src, dst_ref=dst, send_sem=ar_send.at[n, phase, number], recv_sem=ar_recv.at[n, phase, slot],
            device_id=device, device_id_type=MESH)

    def ar_first(n, d):
        return ar_copy(n, 0, me1, ARS.at[n], AR1.at[n, me1], d, member(lax.rem(me1 + d, GROUP)))

    def ar_second(n, d):
        return ar_copy(n, 1, hi, AR2S.at[n], AR2.at[n, hi], d, (gz, lax.rem(hi + d, nhi) * LO + lo, gy))

    def ar_start(n, f):
        def add(b, carry):
            both, alone = carry
            for q in range(4):
                v = SK[f, 4 * b + q]
                both, alone = both + v * E[7 - 7 * f, 4 * b + q + 9, O], alone + v
            return both, alone
        both, alone = lax.fori_loop(0, X // 4, add, (zero_o, zero_o))
        both = jnp.sum(both, axis=0, keepdims=True)
        alone = jnp.sum(alone, axis=0, keepdims=True)
        sub = plane_of(two)
        tile = jnp.where(sub == 0, both, jnp.where(sub == 1, alone, 0.0))
        ARS[n] = tile
        AR1[n, me1] = tile
        for d in range(1, GROUP):
            ar_first(n, d).start()

    def ar_middle(n):
        for d in range(1, GROUP):
            s = lax.rem(me1 + d, GROUP)
            ar_copy(n, 0, s, ARS.at[n], AR1.at[n, s], d, member(s)).wait_recv()
        tile = AR1[n, 0]
        for s in range(1, GROUP):
            tile = tile + AR1[n, s]
        AR2S[n] = tile
        AR2[n, hi] = tile
        for d in range(1, nhi):
            ar_second(n, d).start()

    def ar_end(n):
        for d in range(1, nhi):
            s = lax.rem(hi + d, nhi)
            ar_copy(n, 1, s, AR2S.at[n], AR2.at[n, s], d, (gz, s * LO + lo, gy)).wait_recv()
        tile = AR2[n, 0]
        for s in range(1, nhi):
            tile = tile + AR2[n, s]
        for d in range(1, GROUP):
            ar_first(n, d).wait_send()
        for d in range(1, nhi):
            ar_second(n, d).wait_send()
        tile = jnp.sum(tile, axis=1, keepdims=True)
        return tile[0:1], tile[1:2]

    for f in (0, 1):
        for copy in arrived[f]:
            copy.wait_recv()
        cap_rows(f, 0)
        build_strip(f)

        def level(first, rows, k, f=f):
            level_forward(f, k, k if f == 0 else LEVELS, first, rows)
            if f == 1 and rows == 28:
                @pl.when(k == 2)
                def _():
                    ar_middle(0)
            return 0
        lax.fori_loop(0, 4, lambda k, _: level(2, 28, k), 0)
        lax.fori_loop(4, LEVELS, lambda k, _: level(6, 20, k), 0)
        ar_start(f, f)

    def chain(i, _, memo):
        t = zero_o + 1.0
        todo = []
        for k in range(LEVELS - 1, -1, -1):
            delta, prior = GB[k, i + 1], SP[k, i]
            on = delta - prior * delta > 0
            GB[k, i + 1] = jnp.where(on, t * (1.0 - prior), 0.0)
            t = jnp.where(on, t * (1.0 - delta), t)
        return todo
    run(0, 4, 4, chain)

    def strip_chain(j, _, memo):
        t = zero_o + 1.0
        lane = lane_of(t)
        mine = (lane >= 32) & (lane < 96)
        for k in range(LEVELS - 1, -1, -1):
            delta, prior = SGB[k, j], SSP[k, j]
            on = delta - prior * delta > 0
            SGB[k, j] = jnp.where(on & mine, t * (1.0 - prior), 0.0)
            t = jnp.where(on, t * (1.0 - delta), t)
        return []
    run(0, 2, 4, strip_chain)

    both, alone = ar_end(0)
    pred_total = alone
    tprec = (both + 1.0) / (pred_total + 1.0)

    run(0, 2, 8, lambda i, _, m: [(CT, (i + 1,), E[7, i + 9, O] - tprec)])
    run(0, 1, 8, lambda j, _, m: [(SCT, (j,), S[1, 0, j + 1, O] - tprec)])

    def strip_back(step, _):
        k = LEVELS - 1 - step
        old = lax.rem(step, 2)
        new = 1 - old

        def strip_cols(j, _, memo):
            a = SM2[k, j]
            gc, gl, gu = route(-SGB[k, j] * SCT[j], SBM[k, j], (a, SLM[k, j]))
            todo = [(SX, (k, j), jnp.where(gy == 0, gl, gu))]
            g = gc + roll(gl, 127) + roll(gu, 1)
            gc, gl, gu = route(g, a, (SM1[k, j + 1], SM1[k, j]))
            return todo + [(SHX, (0, j + 1), gc), (SHX, (1, j + 1), gl), (SHX, (2, j + 1), gu)]
        run(0, 1, 8, strip_cols)
        SHX[1, 9] = roll(SHX[1, 1], 96)
        SHX[2, 0] = roll(SHX[2, 8], 32)

        def strip_depth(j, q, memo):
            g = SHX[0, j + 1] + SHX[1, j + 2] + SHX[2, j]
            gc, gl, gu = route(g, SM1[k, j + 1], (S[0, k + 1, j + 1, O], S[0, k + 1, j + 1, OL]))
            T[q, 0, O] = gc + SGB[k + 1, j] * SCT[j]
            T[q, 1, O] = gl
            T[q, 2, O] = gu
            g = SG[old, 0, j + 1] + SG[old, 1, j + 2] + SG[old, 2, j]
            g = g + T[q, 0, W] + T[q, 1, WU] + T[q, 2, WL]
            c = S[0, k, j + 1, W]
            gc, zl, zu, xl, xu, yl, yu = route(
                g, S[0, k + 1, j + 1, W],
                (c, S[0, k, j + 1, WL], S[0, k, j + 1, WU], S[0, k, j, W], S[0, k, j + 2, W], SLE[k, j]))
            T2[q, 0, W] = zl
            T2[q, 1, W] = zu
            return [(SX2, (k, j), jnp.where(gy == 0, yl, yu)),
                    (SG, (new, 0, j + 1), gc + roll(yl, 127) + roll(yu, 1) + T2[q, 0, WU] + T2[q, 1, WL]),
                    (SG, (new, 1, j + 1), xl), (SG, (new, 2, j + 1), xu)]
        run(0, 1, 8, strip_depth)
        SG[new, 1, 9] = roll(SG[new, 1, 1], 96)
        SG[new, 2, 0] = roll(SG[new, 2, 8], 32)
        return 0

    def open_cols(k, i, j, g):
        a = M2[k, i]
        by = seam_turn - 32 * g
        gc, gl, gu = route(-GB[k, i + 1] * CT[i + 1], BM[k, i], (a, LM[k, i]))
        g = gc + gather_sides(gl, gu, roll(SX[k, j], by))
        gc, gl, gu = route(g, a, (M1[k, i + 1], M1[k, i]))
        return [(HX, (0, i + 2), gc), (HX, (1, i + 2), gl), (HX, (2, i + 2), gu)]

    def open_depths(k, i, q):
        g = HX[0, i + 1] + HX[1, i + 2] + HX[2, i]
        gc, gl, gu = route(g, M1[k, i], (E[k + 1, i + 8, O], E[k + 1, i + 8, OL]))
        T[q, 0, O] = gc + GB[k + 1, i] * CT[i]
        T[q, 1, O] = gl
        T[q, 2, O] = gu
        return [(HZ, (k, i + 1), T[q, 0, W] + T[q, 1, WU] + T[q, 2, WL])]

    def open_all(k, _):
        run(0, 1, X, lambda i, q, memo: open_cols(k, i, i % 8, i // 8 + 1))
        run(0, 1, X + 2, lambda i, q, memo: open_depths(k, i, q % 8))
        return 0

    def open_outer(k, _):
        for start in (0, 12):
            run(start, 1, 4, lambda i, q, memo: open_cols(k, i, i % 8, i // 8 + 1))
        for start in (0, 14):
            run(start, 1, 4, lambda i, q, memo: open_depths(k, i, start // 14 * 4 + q))
        return 0

    def open_inner(k):
        run(2, 1, 12, lambda i, q, memo: open_cols(k, i, i % 8, i // 8 + 1))
        run(4, 1, 10, lambda i, q, memo: open_depths(k, i, q % 8))

    lax.fori_loop(0, 3, lambda step, _: strip_back(step, 0) + open_all(LEVELS - 1 - step, 0), 0)
    ar_middle(1)
    lax.fori_loop(3, LEVELS, lambda step, _: strip_back(step, 0) + open_outer(LEVELS - 1 - step, 0), 0)

    def erode_back(k, r, q, memo):
        g = G[k + 1, 0, r + 1] + G[k + 1, 1, r + 2] + G[k + 1, 2, r] + HZ[k, jnp.where((r > 6) & (r < 25), r - 6, 0)]
        j, by = place(r)
        under, c, over = [once(memo, q + d, lambda d=d: E[k, r + d, W]) for d in range(3)]
        gc, zl, zu, xl, xu, yl, yu = route(
            g, E[k + 1, r + 1, W],
            (c, E[k, r + 1, WL], E[k, r + 1, WU], under, over, LE[k, r]))
        T2[q, 0, W] = zl
        T2[q, 1, W] = zu
        return [(G, (k, 0, r + 1), gc + gather_sides(yl, yu, roll(SX2[k, j], by)) + T2[q, 0, WU] + T2[q, 1, WL]),
                (G, (k, 1, r + 1), xl), (G, (k, 2, r + 1), xu)]

    def outer(step, _):
        k = LEVELS - 1 - step
        run(lambda b: jnp.where(b == 0, 2 + k, 23 - k), 2, 7, lambda r, q, memo: erode_back(k, r, q, memo))
        return 0
    lax.fori_loop(0, LEVELS, outer, 0)

    beyond = pl.multiple_of(32 - 32 * gz, 8)
    mine = pl.multiple_of(8 * gz, 8)
    inner = pl.multiple_of(24 - 24 * gz, 8)
    quiet = pl.ds(mine, Z - 8)
    edge = pl.ds(inner, 8)
    back_rows = []

    def total(r, _, memo):
        v = G[0, 0, r + 1] + G[0, 1, r + 2] + G[0, 2, r]
        return [(F, (r,), v)]

    def from_depth(r, _, memo):
        return [(FO, (r, edge), F[r, pl.ds(mine + inner, 8)] + RZ[r])]

    def own_planes(r, _, memo):
        return [(FO, (r,), F[r, pl.ds(mine, Z)])]

    def return_rows(base, planes, now):
        back_rows.append(send(base, FO.at[pl.ds(1, 7), planes], RX.at[0, :, planes], below, -1, now))
        back_rows.append(send(base + 1, FO.at[pl.ds(24, 7), planes], RX.at[1, :, planes], above, 1, now))

    def to_depth(number, rows):
        return send(number, F.at[rows, pl.ds(beyond, 8)], RZ.at[rows], (1 - gz, gx, gy))

    for start in (1, 24):
        run(start, 1, 7, total)
    margin = [to_depth(16, pl.ds(1, 7)), to_depth(17, pl.ds(24, 7))]
    for start in (1, 24):
        run(start, 1, 7, own_planes)
    return_rows(18, quiet, True)
    return_rows(20, edge, False)

    def inside(step, _):
        k = LEVELS - 1 - step
        at = (k + 1) // 2

        @pl.when(k < 3)
        def _():
            open_inner(k)
        run(8 + 2 * at, 4 - at, 4, lambda r, q, memo: erode_back(k, r, q, memo))

        @pl.when(step == 1)
        def _():
            for copy in margin:
                copy.wait_recv()
            for start in (1, 24):
                run(start, 1, 7, from_depth)
            for copy in back_rows[2:]:
                copy.start()
        return 0
    lax.fori_loop(0, LEVELS, inside, 0)
    run(8, 2, 8, total)
    copy = to_depth(22, pl.ds(8, 16))
    run(8, 2, 8, own_planes)
    copy.wait_recv()
    run(8, 2, 8, from_depth)

    both, alone = ar_end(1)
    tsens = (both + 1.0) / (alone + 1.0)
    square = (tprec + tsens) * (tprec + tsens)
    voxels = float(2 * nx * 2 * Z * X * Y)
    by_prec = -2.0 * tsens * tsens / square / (pred_total + 1.0) * voxels
    by_sens = -2.0 * tprec * tprec / square / (alone + 1.0) * voxels
    loss[...] = 1.0 - 2.0 * tprec * tsens / (tprec + tsens)

    for copy in back_rows:
        copy.wait_recv()

    def give(x, _, memo, extra):
        g = FO[x + 8] + GB[0, x + 1] * CT[x + 1]
        if extra is not None:
            g = g + extra(x)
        g = g * by_prec + SK[1, x] * by_sens
        return [(out, (x,), g)]
    run(0, 1, 7, functools.partial(give, extra=lambda x: RX[1, x]))
    run(7, 1, 2, functools.partial(give, extra=None))
    run(9, 1, 7, functools.partial(give, extra=lambda x: RX[0, x - 9]))
    for copy in copies:
        copy.wait_send()


def local(prediction, label):
    nx = lax.axis_size("gx")
    nhi = nx // LO
    f32 = jnp.float32

    def vmem(*shape):
        return pltpu.VMEM(shape + (Y,), f32)

    grad, loss = pl.pallas_call(
        functools.partial(kernel, nx),
        out_shape=(jax.ShapeDtypeStruct((X, Z, Y), f32), jax.ShapeDtypeStruct((1, 1), f32)),
        in_specs=[pl.BlockSpec(memory_space=pl.ANY)] * 2,
        out_specs=[pl.BlockSpec(memory_space=pltpu.VMEM)] * 2,
        scratch_shapes=[
            vmem(Z * X), vmem(Z * X), pltpu.SemaphoreType.DMA((2,)),
            vmem(10, ROWS + 2, PAD), vmem(2, 7, 10, PAD),
            vmem(7, X + 2, Z), vmem(6, X, Z), vmem(7, 10, Z), vmem(7, 8, Z),
            vmem(6, X, Z), vmem(6, 8, Z),
            vmem(7, X + 2, Z), vmem(7, 8, Z), vmem(X + 2, Z), vmem(8, Z),
            vmem(2, X, Z), vmem(8, Z),
            vmem(3, X + 4, Z), vmem(3, 10, Z), vmem(LEVELS, X + 3, WIN),
            vmem(7, 3, ROWS + 2, WIN), vmem(2, 3, 10, WIN),
            vmem(8, 3, PAD), vmem(8, 2, PAD), vmem(6, 8, Z), vmem(6, 8, WIN),
            vmem(6, ROWS, WIN), vmem(6, 8, WIN),
            vmem(6, X, Z), vmem(6, X, Z), vmem(6, 8, Z), vmem(6, 8, Z),
            vmem(ROWS, WIN), vmem(ROWS, Z), vmem(ROWS, 8), vmem(2, 7, Z),
            vmem(2, 2, WIN), vmem(2, 4, WIN),
            vmem(2, 8), vmem(2, GROUP, 8), vmem(2, 8), vmem(2, nhi, 8),
            pltpu.SemaphoreType.DMA((23,)), pltpu.SemaphoreType.DMA((23,)),
            pltpu.SemaphoreType.DMA((2, 2, max(GROUP, nhi))), pltpu.SemaphoreType.DMA((2, 2, max(GROUP, nhi))),
        ],
        compiler_params=pltpu.CompilerParams(
            collective_id=0, has_side_effects=True, vmem_limit_bytes=62 * 1024 * 1024),
    )(prediction.reshape(Z * X, Y), label.reshape(Z * X, Y))
    return loss.reshape(()), jnp.transpose(grad, (1, 0, 2))


def solution(mesh):
    in_specs = (P("gz", "gx", "gy"), P("gz", "gx", "gy"))
    out_specs = (P(), P("gz", "gx", "gy"))
    return jax.shard_map(local, mesh=mesh, in_specs=in_specs, out_specs=out_specs, check_vma=False)
```

```python
import functools

import jax
import jax.numpy as jnp
from jax import lax
from jax.experimental import pallas as pl
from jax.experimental.pallas import tpu as pltpu
from jax.sharding import PartitionSpec as P

LEVELS = 6
Z, X, Y = 32, 16, 128
WIN = Z + 8
PAD = WIN + 16
ROWS = X + 16
GROUP = 8
LO = 2
SEMS = 64
MESH = pl.DeviceIdType.MESH

W, WL, WU = pl.ds(8, WIN), pl.ds(7, WIN), pl.ds(9, WIN)


def lane_of(v):
    return lax.broadcasted_iota(jnp.int32, v.shape, 1)


def plane_of(v):
    return lax.broadcasted_iota(jnp.int32, v.shape, 0)


def roll(v, by):
    return pltpu.roll(v, by, 1)


def max3(a, b, c):
    return jnp.maximum(jnp.maximum(a, b), c)


def route(g, best, candidates):
    zero = jnp.zeros_like(g)
    parts = []
    for value in candidates:
        hit = value == best
        part = jnp.where(hit, g, zero)
        parts.append(part)
        g = g - part
    parts.append(g)
    return parts


def run(start, blocks, size, row):
    def block(b, _):
        todo, memo = [], {}
        first = start(b) if callable(start) else start + b * size
        for q in range(size):
            todo += row(first + q, q, memo)
        for ref, at, value in todo:
            ref[at] = value
        return 0
    if isinstance(blocks, int) and blocks == 1:
        block(0, 0)
        return
    else:
        lax.fori_loop(0, blocks, block, 0)


def once(memo, key, load):
    if key not in memo:
        memo[key] = load()
    return memo[key]


def slot_of(f, k):
    if f == 0:
        return k
    if isinstance(k, int) and k == 0:
        return 7
    return jnp.where(k == 0, 7, 8 + lax.rem(k, 2))


def kernel(nx, pred_hbm, label_hbm, out, loss, pred, label, in_sem, E, S, M1, M2, SM1, SM2, SP, SSP, GB, SGB, CT, SCT, SK, SSK,
           HX, SHX, HZ, G, SG, T, T2, SX, SX2, LE, SLE, LM, BM, SLM, SBM, F, FO, RZ, RX, PS, PR, ARS, AR1, AR2S, AR2,
           send_sem, recv_sem, ar_send, ar_recv):
    gz, gx, gy = lax.axis_index("gz"), lax.axis_index("gx"), lax.axis_index("gy")
    prev, nxt = lax.rem(gx + nx - 1, nx), lax.rem(gx + 1, nx)
    nhi = nx // LO
    hi, lo = gx // LO, lax.rem(gx, LO)
    me1 = (gz * LO + lo) * 2 + gy
    o = pl.multiple_of(8 + 8 * gz, 8)
    O, OL, OU = pl.ds(o, Z), pl.ds(o - 1, Z), pl.ds(o + 1, Z)
    seam = 127 * (1 - gy)
    zlow = jnp.where(gz == 0, 0, -1)
    zhigh = jnp.where(gz == 1, Z - 1, -1)
    first_lane = jnp.where(gx == 0, 32, 0)
    last_lane = jnp.where(gx == nx - 1, 96, 128)

    def member(i):
        return (i // (2 * LO), hi * LO + lax.rem(i // 2, LO), lax.rem(i, 2))

    loads = [pltpu.make_async_copy(src, dst.at[pl.ds(0, Z * X)], in_sem.at[f])
             for f, (src, dst) in enumerate(((pred_hbm, pred), (label_hbm, label)))]
    for load in loads:
        load.start()

    barrier = pltpu.get_barrier_semaphore()
    has_prev, has_nxt = gx > 0, gx < nx - 1
    for inside, row in ((has_prev, prev), (has_nxt, nxt)):
        @pl.when(inside)
        def _(row=row):
            for cols in (gy, 1 - gy):
                pl.semaphore_signal(barrier, inc=1, device_id=(gz, row, cols), device_id_type=MESH)
    greet = [member(lax.rem(me1 + d, GROUP)) for d in range(1, GROUP)]
    greet += [(gz, lax.rem(hi + d, nhi) * LO + lo, gy) for d in range(1, nhi)]
    for device in greet:
        pl.semaphore_signal(barrier, inc=1, device_id=device, device_id_type=MESH)

    def lay_out(f):
        ref = (pred, label)[f]
        loads[f].wait()

        def bring(x, _, memo):
            return [(E, (7 * f, 9 + x, pl.ds(o + 8 * t, 8)), ref[pl.ds(x + X * 8 * t, 8, stride=X), :])
                    for t in range(Z // 8)]
        run(0, 2, 8, bring)

    lay_out(0)
    zero_w = jnp.zeros((WIN, Y), jnp.float32)
    zero_o = jnp.zeros((Z, Y), jnp.float32)
    pl.semaphore_wait(barrier, len(greet) + jnp.where(has_prev, 2, 0) + jnp.where(has_nxt, 2, 0))

    copies = []

    def only(inside, act):
        if inside is None:
            act()
        else:
            pl.when(inside)(act)

    class Sent:
        def __init__(self, copy, sends, gets):
            self.copy, self.sends, self.gets = copy, sends, gets

        def start(self):
            only(self.sends, self.copy.start)

        def wait_recv(self):
            only(self.gets, self.copy.wait_recv)

        def wait_send(self):
            only(self.sends, self.copy.wait_send)

    def send(number, src, dst, device, step=0, now=True):
        copy = pltpu.make_async_remote_copy(
            src_ref=src, dst_ref=dst, send_sem=send_sem.at[number], recv_sem=recv_sem.at[number],
            device_id=device, device_id_type=MESH)
        sends = {0: None, -1: has_prev, 1: has_nxt}[step]
        gets = {0: None, -1: has_nxt, 1: has_prev}[step]
        copies.append(Sent(copy, sends, gets))
        if now:
            copies[-1].start()
        return copies[-1]

    near = pl.multiple_of(32 - 16 * gz, 8)
    far = pl.multiple_of(8 + 32 * gz, 8)
    below, above = (gz, prev, gy), (gz, nxt, gy)
    arrived = [[], []]

    def pass_rows(f, base, planes):
        arrived[f] += [
            send(base, E.at[7 * f, pl.ds(9, 7), planes], E.at[7 * f, pl.ds(25, 7), planes], below, -1),
            send(base + 1, E.at[7 * f, pl.ds(18, 7), planes], E.at[7 * f, pl.ds(2, 7), planes], above, 1)]

    def first_halos(f):
        copy = send(8 * f, E.at[7 * f, pl.ds(9, X), pl.ds(near, 8)], E.at[7 * f, pl.ds(9, X), pl.ds(far, 8)],
                    (1 - gz, gx, gy))
        pass_rows(f, 8 * f + 1, O)
        return copy

    def second_halos(f, depth):
        depth.wait_recv()
        pass_rows(f, 8 * f + 3, pl.ds(pl.multiple_of(40 - 32 * gz, 8), 8))
        for half in (0, 1):
            packed = zero_w
            for i in range(8):
                v = E[7 * f, 9 + 8 * half + i, W]
                packed = jnp.where(lane_of(v) // 16 == i, roll(v, lax.rem(16 * i + 16 * (1 - gy), 128)), packed)
            PS[f, half] = packed
        arrived[f] += [
            send(8 * f + 5, PS.at[f], PR.at[f, pl.ds(1, 2)], (gz, gx, 1 - gy)),
            send(8 * f + 6, PS.at[f, 0], PR.at[f, 3], (gz, prev, 1 - gy), -1),
            send(8 * f + 7, PS.at[f, 1], PR.at[f, 0], (gz, nxt, 1 - gy), 1)]

    depth = first_halos(0)
    lay_out(1)
    second_halos(0, depth)
    depth = first_halos(1)
    second_halos(1, depth)

    two = jnp.full((8, Y), 2.0, jnp.float32)

    def rims(r, _, memo):
        return [(E, (slot, r, pl.ds(at, 8)), two) for slot in range(10) for at in (0, PAD - 8)]
    run(0, 17, 2, rims)

    def strip_rims(j, _, memo):
        return [(S, (f, k, j, pl.ds(at, 8)), two)
                for f in (0, 1) for k in range(LEVELS + 1) for at in (0, PAD - 8)]
    run(1, 4, 2, strip_rims)
    run(0, 17, 2, lambda r, _, m: [(G, (p, q, r), zero_w) for p in range(LEVELS + 1) for q in range(3)])
    for k in range(LEVELS):
        HZ[k, 0] = zero_w
    run(0, 2, 5, lambda j, _, m: [(SG, (p, q, j), zero_w) for p in (0, 1) for q in range(3)])
    run(0, 4, 5, lambda i, _, m: [(HX, (q, i), zero_o) for q in range(3)])
    run(0, 4, 4, lambda i, _, m: [(SK, (0, i), zero_o), (SK, (1, i), zero_o), (GB, (LEVELS, i + 1), zero_o)])
    run(0, 1, 8, lambda j, _, m: [(SSK, (j,), zero_o), (SGB, (LEVELS, j), zero_o)])
    for k in range(LEVELS + 1):
        GB[k, 0] = zero_o
        CT[0] = zero_o
        CT[X + 1] = zero_o
        GB[k, X + 1] = zero_o
    for q in range(8):
        for p in range(3):
            T[q, p] = jnp.zeros((PAD, Y), jnp.float32)
    for q in range(8):
        for p in range(2):
            T2[q, p] = jnp.zeros((PAD, Y), jnp.float32)
    for r in (0, 1, ROWS, ROWS + 1):
        for slot in range(10) if r in (0, ROWS + 1) else (0, 7):
            E[slot, r, W] = zero_w + 2.0

    @pl.when(gx == 0)
    def _():
        for f in (0, 1):
            PR[f, 0] = zero_w + 2.0
            for r in range(2, 9):
                E[7 * f, r, W] = zero_w + 2.0
        RX[1] = jnp.zeros((7, Z, Y), jnp.float32)

    @pl.when(gx == nx - 1)
    def _():
        for f in (0, 1):
            PR[f, 3] = zero_w + 2.0
            for r in range(25, 32):
                E[7 * f, r, W] = zero_w + 2.0
        RX[0] = jnp.zeros((7, Z, Y), jnp.float32)

    seam_turn = 111 + 2 * gy

    def place(r):
        g = lax.div(r, 8)
        return r - 8 * g, seam_turn - 32 * g

    def sides(v, seen):
        lane = lane_of(v)
        t = jnp.where(lane == seam, seen, v)
        return jnp.where(lane == 0, t, roll(v, 1)), jnp.where(lane == 127, t, roll(v, 127))

    def strip_sides(v):
        return roll(v, 1), roll(v, 127)

    def gather_sides(lower, upper, seen):
        lane = lane_of(lower)
        t = jnp.where(lane == seam, seen, 0.0)
        return jnp.where(lane == 127, t, roll(lower, 127)) + jnp.where(lane == 0, t, roll(upper, 1))

    def wrap_strip(ref, at, window, value):
        v = ref[at + (8, window)]
        v = jnp.where(lane_of(v) < first_lane, value, v)
        ref[at + (8, window)] = v
        ref[at + (0, window)] = roll(v, 32)
        v = ref[at + (1, window)]
        v = jnp.where(lane_of(v) >= last_lane, value, v)
        ref[at + (1, window)] = v
        ref[at + (9, window)] = roll(v, 96)

    def cap_rows(f, k):
        @pl.when(gx == 0)
        def _():
            E[slot_of(f, k), 8, W] = zero_w + 2.0

        @pl.when(gx == nx - 1)
        def _():
            E[slot_of(f, k), 25, W] = zero_w + 2.0

    def build_strip(f):
        def row(j, _, memo):
            acc = zero_w
            lane = lane_of(acc) // 16
            for g in range(4):
                own = roll(E[7 * f, 8 * g + j + 1, W], lax.rem(32 * g + 16, 128))
                other = roll(PR[f, g], lax.rem(32 * g - 16 * j + 16 * (1 - gy) + 128, 128))
                acc = jnp.where(lane == 2 * g + gy, own, acc)
                acc = jnp.where(lane == 2 * g + 1 - gy, other, acc)
            return [(S, (f, 0, j + 1, W), acc)]
        run(0, 2, 4, row)
        wrap_strip(S, (f, 0), W, 2.0)

    def eroded(ref, at, i, q, memo, pair):
        def centre(step):
            return once(memo, q + step, lambda: ref[at + (i + step, W)])
        c = centre(0)
        lower, upper = pair(c)
        m = jnp.minimum(jnp.minimum(c, lower), upper)
        m = jnp.minimum(m, jnp.minimum(ref[at + (i, WL)], ref[at + (i, WU)]))
        return jnp.minimum(m, jnp.minimum(centre(-1), centre(1))), lower

    def depth_max(ref, at, i):
        c = ref[at + (i, O)]
        plane = plane_of(c)
        lower = jnp.where(plane == zlow, c, ref[at + (i, OL)])
        upper = jnp.where(plane == zhigh, c, ref[at + (i, OU)])
        return max3(lower, c, upper)

    def level_forward(f, k, slot, first, rows):
        def strip_erode(j, q, memo):
            m, lower = eroded(S, (f, k), j + 1, q, memo, strip_sides)
            return [(S, (f, k + 1, j + 1, W), m)] + ([(SLE, (k, j), lower)] if f == 0 else [])
        run(0, 1, 8, strip_erode)
        wrap_strip(S, (f, k + 1), W, 2.0)

        def erode(r, q, memo):
            j, g = r % 8, r // 8
            seen = roll(S[f, k, j + 1, W], seam_turn - 32 * g)
            m, lower = eroded(E, (slot_of(f, k),), r + 1, q, memo, lambda c: sides(c, seen))
            if r in (7, 24):
                m = jnp.where(gx == (0 if r == 7 else nx - 1), zero_w + 2.0, m)
            return [(E, (slot_of(f, k + 1), r + 1, W), m)] + ([(LE, (k, r), lower)] if f == 0 else [])
        run(first, 1, rows, erode)

        def strip_depth(j, _, memo):
            return [(SM1, (slot, j + 1), depth_max(S, (f, k + 1), j + 1))]
        run(0, 1, 8, strip_depth)
        wrap_strip(SM1, (slot,), slice(None), 0.0)

        def strip_rows(j, q, memo):
            v = max3(*[once(memo, q + d, lambda d=d: SM1[slot, j + d]) for d in range(3)])
            todo = [(SM2, (slot, j), v)]
            if f == 0:
                lower, upper = strip_sides(v)
                best = max3(lower, v, upper)
                delta = jnp.maximum(S[f, k, j + 1, O] - best, 0.0)
                prior = SSK[j]
                todo += [(SLM, (k, j), lower), (SBM, (k, j), best), (SGB, (k, j), delta), (SSP, (k, j), prior),
                         (SSK, (j,), prior + jnp.maximum(delta - prior * delta, 0.0))]
            return todo
        run(0, 1, 8, strip_rows)

        def depth_rows(i, _, memo):
            m = depth_max(E, (slot_of(f, k + 1),), i + 8)
            if i in (0, X + 1):
                m = jnp.where(gx == (0 if i == 0 else nx - 1), zero_o, m)
            return [(M1, (slot, i), m)]
        run(0, 1, X + 2, depth_rows)

        def rest(i, q, memo):
            v = max3(*[once(memo, q + d, lambda d=d: M1[slot, i + d]) for d in range(3)])
            r = i + 8
            lower, upper = sides(v, roll(SM2[slot, i % 8], seam_turn - 32 * (r // 8)))
            best = max3(lower, v, upper)
            delta = jnp.maximum(E[slot_of(f, k), r + 1, O] - best, 0.0)
            prior = SK[f, i]
            todo = [(SK, (f, i), prior + jnp.maximum(delta - prior * delta, 0.0))]
            if f == 0:
                todo += [(M2, (k, i), v), (GB, (k, i + 1), delta), (SP, (k, i), prior), (LM, (k, i), lower), (BM, (k, i), best)]
            return todo
        run(0, 1, X, rest)

    def ar_copy(n, phase, slot, src, dst, number, device):
        return pltpu.make_async_remote_copy(
            src_ref=src, dst_ref=dst, send_sem=ar_send.at[n, phase, number], recv_sem=ar_recv.at[n, phase, slot],
            device_id=device, device_id_type=MESH)

    def ar_first(n, d):
        return ar_copy(n, 0, me1, ARS.at[n], AR1.at[n, me1], d, member(lax.rem(me1 + d, GROUP)))

    def ar_second(n, d):
        return ar_copy(n, 1, hi, AR2S.at[n], AR2.at[n, hi], d, (gz, lax.rem(hi + d, nhi) * LO + lo, gy))

    def ar_start(n, f):
        def add(b, carry):
            both, alone = carry
            for q in range(4):
                v = SK[f, 4 * b + q]
                both, alone = both + v * E[7 - 7 * f, 4 * b + q + 9, O], alone + v
            return both, alone
        both, alone = lax.fori_loop(0, X // 4, add, (zero_o, zero_o))
        both = jnp.sum(both, axis=0, keepdims=True)
        alone = jnp.sum(alone, axis=0, keepdims=True)
        sub = plane_of(two)
        tile = jnp.where(sub == 0, both, jnp.where(sub == 1, alone, 0.0))
        ARS[n] = tile
        AR1[n, me1] = tile
        for d in range(1, GROUP):
            ar_first(n, d).start()

    def ar_middle(n):
        for d in range(1, GROUP):
            s = lax.rem(me1 + d, GROUP)
            ar_copy(n, 0, s, ARS.at[n], AR1.at[n, s], d, member(s)).wait_recv()
        tile = AR1[n, 0]
        for s in range(1, GROUP):
            tile = tile + AR1[n, s]
        AR2S[n] = tile
        AR2[n, hi] = tile
        for d in range(1, nhi):
            ar_second(n, d).start()

    def ar_end(n):
        for d in range(1, nhi):
            s = lax.rem(hi + d, nhi)
            ar_copy(n, 1, s, AR2S.at[n], AR2.at[n, s], d, (gz, s * LO + lo, gy)).wait_recv()
        tile = AR2[n, 0]
        for s in range(1, nhi):
            tile = tile + AR2[n, s]
        for d in range(1, GROUP):
            ar_first(n, d).wait_send()
        for d in range(1, nhi):
            ar_second(n, d).wait_send()
        tile = jnp.sum(tile, axis=1, keepdims=True)
        return tile[0:1], tile[1:2]

    for f in (0, 1):
        for copy in arrived[f]:
            copy.wait_recv()
        cap_rows(f, 0)
        build_strip(f)

        def level(first, rows, k, f=f):
            level_forward(f, k, k if f == 0 else LEVELS, first, rows)
            if f == 1 and rows == 28:
                @pl.when(k == 2)
                def _():
                    ar_middle(0)
            return 0
        lax.fori_loop(0, 4, lambda k, _: level(2, 28, k), 0)
        lax.fori_loop(4, LEVELS, lambda k, _: level(6, 20, k), 0)
        ar_start(f, f)

    def chain(i, _, memo):
        t = zero_o + 1.0
        todo = []
        for k in range(LEVELS - 1, -1, -1):
            delta, prior = GB[k, i + 1], SP[k, i]
            on = delta - prior * delta > 0
            GB[k, i + 1] = jnp.where(on, t * (1.0 - prior), 0.0)
            t = jnp.where(on, t * (1.0 - delta), t)
        return todo
    run(0, 4, 4, chain)

    def strip_chain(j, _, memo):
        t = zero_o + 1.0
        lane = lane_of(t)
        mine = (lane >= 32) & (lane < 96)
        for k in range(LEVELS - 1, -1, -1):
            delta, prior = SGB[k, j], SSP[k, j]
            on = delta - prior * delta > 0
            SGB[k, j] = jnp.where(on & mine, t * (1.0 - prior), 0.0)
            t = jnp.where(on, t * (1.0 - delta), t)
        return []
    run(0, 2, 4, strip_chain)

    both, alone = ar_end(0)
    pred_total = alone
    tprec = (both + 1.0) / (pred_total + 1.0)

    run(0, 2, 8, lambda i, _, m: [(CT, (i + 1,), E[7, i + 9, O] - tprec)])
    run(0, 1, 8, lambda j, _, m: [(SCT, (j,), S[1, 0, j + 1, O] - tprec)])

    def strip_back(step, _):
        k = LEVELS - 1 - step
        old = lax.rem(step, 2)
        new = 1 - old

        def strip_cols(j, _, memo):
            a = SM2[k, j]
            gc, gl, gu = route(-SGB[k, j] * SCT[j], SBM[k, j], (a, SLM[k, j]))
            todo = [(SX, (k, j), jnp.where(gy == 0, gl, gu))]
            g = gc + roll(gl, 127) + roll(gu, 1)
            gc, gl, gu = route(g, a, (SM1[k, j + 1], SM1[k, j]))
            return todo + [(SHX, (0, j + 1), gc), (SHX, (1, j + 1), gl), (SHX, (2, j + 1), gu)]
        run(0, 1, 8, strip_cols)
        SHX[1, 9] = roll(SHX[1, 1], 96)
        SHX[2, 0] = roll(SHX[2, 8], 32)

        def strip_depth(j, q, memo):
            g = SHX[0, j + 1] + SHX[1, j + 2] + SHX[2, j]
            gc, gl, gu = route(g, SM1[k, j + 1], (S[0, k + 1, j + 1, O], S[0, k + 1, j + 1, OL]))
            T[q, 0, O] = gc + SGB[k + 1, j] * SCT[j]
            T[q, 1, O] = gl
            T[q, 2, O] = gu
            g = SG[old, 0, j + 1] + SG[old, 1, j + 2] + SG[old, 2, j]
            g = g + T[q, 0, W] + T[q, 1, WU] + T[q, 2, WL]
            c = S[0, k, j + 1, W]
            gc, zl, zu, xl, xu, yl, yu = route(
                g, S[0, k + 1, j + 1, W],
                (c, S[0, k, j + 1, WL], S[0, k, j + 1, WU], S[0, k, j, W], S[0, k, j + 2, W], SLE[k, j]))
            T2[q, 0, W] = zl
            T2[q, 1, W] = zu
            return [(SX2, (k, j), jnp.where(gy == 0, yl, yu)),
                    (SG, (new, 0, j + 1), gc + roll(yl, 127) + roll(yu, 1) + T2[q, 0, WU] + T2[q, 1, WL]),
                    (SG, (new, 1, j + 1), xl), (SG, (new, 2, j + 1), xu)]
        run(0, 1, 8, strip_depth)
        SG[new, 1, 9] = roll(SG[new, 1, 1], 96)
        SG[new, 2, 0] = roll(SG[new, 2, 8], 32)
        return 0

    def open_cols(k, i, j, g):
        a = M2[k, i]
        by = seam_turn - 32 * g
        gc, gl, gu = route(-GB[k, i + 1] * CT[i + 1], BM[k, i], (a, LM[k, i]))
        g = gc + gather_sides(gl, gu, roll(SX[k, j], by))
        gc, gl, gu = route(g, a, (M1[k, i + 1], M1[k, i]))
        return [(HX, (0, i + 2), gc), (HX, (1, i + 2), gl), (HX, (2, i + 2), gu)]

    def open_depths(k, i, q):
        g = HX[0, i + 1] + HX[1, i + 2] + HX[2, i]
        gc, gl, gu = route(g, M1[k, i], (E[k + 1, i + 8, O], E[k + 1, i + 8, OL]))
        T[q, 0, O] = gc + GB[k + 1, i] * CT[i]
        T[q, 1, O] = gl
        T[q, 2, O] = gu
        return [(HZ, (k, i + 1), T[q, 0, W] + T[q, 1, WU] + T[q, 2, WL])]

    def open_all(k, _):
        run(0, 1, X, lambda i, q, memo: open_cols(k, i, i % 8, i // 8 + 1))
        run(0, 1, X + 2, lambda i, q, memo: open_depths(k, i, q % 8))
        return 0

    def open_outer(k, _):
        for start in (0, 12):
            run(start, 1, 4, lambda i, q, memo: open_cols(k, i, i % 8, i // 8 + 1))
        for start in (0, 14):
            run(start, 1, 4, lambda i, q, memo: open_depths(k, i, start // 14 * 4 + q))
        return 0

    def open_inner(k):
        run(2, 1, 12, lambda i, q, memo: open_cols(k, i, i % 8, i // 8 + 1))
        run(4, 1, 10, lambda i, q, memo: open_depths(k, i, q % 8))

    lax.fori_loop(0, 3, lambda step, _: strip_back(step, 0) + open_all(LEVELS - 1 - step, 0), 0)
    ar_middle(1)
    lax.fori_loop(3, LEVELS, lambda step, _: strip_back(step, 0) + open_outer(LEVELS - 1 - step, 0), 0)

    def erode_back(k, r, q, memo):
        g = G[k + 1, 0, r + 1] + G[k + 1, 1, r + 2] + G[k + 1, 2, r] + HZ[k, jnp.where((r > 6) & (r < 25), r - 6, 0)]
        j, by = place(r)
        under, c, over = [once(memo, q + d, lambda d=d: E[k, r + d, W]) for d in range(3)]
        gc, zl, zu, xl, xu, yl, yu = route(
            g, E[k + 1, r + 1, W],
            (c, E[k, r + 1, WL], E[k, r + 1, WU], under, over, LE[k, r]))
        T2[q, 0, W] = zl
        T2[q, 1, W] = zu
        return [(G, (k, 0, r + 1), gc + gather_sides(yl, yu, roll(SX2[k, j], by)) + T2[q, 0, WU] + T2[q, 1, WL]),
                (G, (k, 1, r + 1), xl), (G, (k, 2, r + 1), xu)]

    def outer(step, _):
        k = LEVELS - 1 - step
        run(lambda b: jnp.where(b == 0, 2 + k, 23 - k), 2, 7, lambda r, q, memo: erode_back(k, r, q, memo))
        return 0
    lax.fori_loop(0, LEVELS, outer, 0)

    beyond = pl.multiple_of(32 - 32 * gz, 8)
    mine = pl.multiple_of(8 * gz, 8)
    inner = pl.multiple_of(24 - 24 * gz, 8)
    quiet = pl.ds(mine, Z - 8)
    edge = pl.ds(inner, 8)
    back_rows = []

    def total(r, _, memo):
        v = G[0, 0, r + 1] + G[0, 1, r + 2] + G[0, 2, r]
        return [(F, (r,), v)]

    def from_depth(r, _, memo):
        return [(FO, (r, edge), F[r, pl.ds(mine + inner, 8)] + RZ[r])]

    def own_planes(r, _, memo):
        return [(FO, (r,), F[r, pl.ds(mine, Z)])]

    def return_rows(base, planes, now):
        back_rows.append(send(base, FO.at[pl.ds(1, 7), planes], RX.at[0, :, planes], below, -1, now))
        back_rows.append(send(base + 1, FO.at[pl.ds(24, 7), planes], RX.at[1, :, planes], above, 1, now))

    def to_depth(number, rows):
        return send(number, F.at[rows, pl.ds(beyond, 8)], RZ.at[rows], (1 - gz, gx, gy))

    for start in (1, 24):
        run(start, 1, 7, total)
    margin = [to_depth(16, pl.ds(1, 7)), to_depth(17, pl.ds(24, 7))]
    for start in (1, 24):
        run(start, 1, 7, own_planes)
    return_rows(18, quiet, True)
    return_rows(20, edge, False)

    def inside(step, _):
        k = LEVELS - 1 - step
        at = (k + 1) // 2

        @pl.when(k < 3)
        def _():
            open_inner(k)
        run(8 + 2 * at, 4 - at, 4, lambda r, q, memo: erode_back(k, r, q, memo))

        @pl.when(step == 1)
        def _():
            for copy in margin:
                copy.wait_recv()
            for start in (1, 24):
                run(start, 1, 7, from_depth)
            for copy in back_rows[2:]:
                copy.start()
        return 0
    lax.fori_loop(0, LEVELS, inside, 0)
    run(8, 2, 8, total)
    copy = to_depth(22, pl.ds(8, 16))
    run(8, 2, 8, own_planes)
    copy.wait_recv()
    run(8, 2, 8, from_depth)

    both, alone = ar_end(1)
    tsens = (both + 1.0) / (alone + 1.0)
    square = (tprec + tsens) * (tprec + tsens)
    voxels = float(2 * nx * 2 * Z * X * Y)
    by_prec = -2.0 * tsens * tsens / square / (pred_total + 1.0) * voxels
    by_sens = -2.0 * tprec * tprec / square / (alone + 1.0) * voxels
    loss[...] = 1.0 - 2.0 * tprec * tsens / (tprec + tsens)

    for copy in back_rows:
        copy.wait_recv()

    def give(x, _, memo, extra):
        g = FO[x + 8] + GB[0, x + 1] * CT[x + 1]
        if extra is not None:
            g = g + extra(x)
        g = g * by_prec + SK[1, x] * by_sens
        return [(out, (x,), g)]
    run(0, 1, 7, functools.partial(give, extra=lambda x: RX[1, x]))
    run(7, 1, 2, functools.partial(give, extra=None))
    run(9, 1, 7, functools.partial(give, extra=lambda x: RX[0, x - 9]))
    for copy in copies:
        copy.wait_send()


def local(prediction, label):
    nx = lax.axis_size("gx")
    nhi = nx // LO
    f32 = jnp.float32

    def vmem(*shape):
        return pltpu.VMEM(shape + (Y,), f32)

    grad, loss = pl.pallas_call(
        functools.partial(kernel, nx),
        out_shape=(jax.ShapeDtypeStruct((X, Z, Y), f32), jax.ShapeDtypeStruct((1, 1), f32)),
        in_specs=[pl.BlockSpec(memory_space=pl.ANY)] * 2,
        out_specs=[pl.BlockSpec(memory_space=pltpu.VMEM)] * 2,
        scratch_shapes=[
            vmem(Z * X + 256), vmem(Z * X + 256), pltpu.SemaphoreType.DMA((2,)),
            vmem(10, ROWS + 2, PAD), vmem(2, 7, 10, PAD),
            vmem(7, X + 2, Z), vmem(6, X, Z), vmem(7, 10, Z), vmem(7, 8, Z),
            vmem(6, X, Z), vmem(6, 8, Z),
            vmem(7, X + 2, Z), vmem(7, 8, Z), vmem(X + 2, Z), vmem(8, Z),
            vmem(2, X, Z), vmem(8, Z),
            vmem(3, X + 4, Z), vmem(3, 10, Z), vmem(LEVELS, X + 3, WIN),
            vmem(7, 3, ROWS + 2, WIN), vmem(2, 3, 10, WIN),
            vmem(8, 3, PAD), vmem(8, 2, PAD), vmem(6, 8, Z), vmem(6, 8, WIN),
            vmem(6, ROWS, WIN), vmem(6, 8, WIN),
            vmem(6, X, Z), vmem(6, X, Z), vmem(6, 8, Z), vmem(6, 8, Z),
            vmem(ROWS, WIN), vmem(ROWS, Z), vmem(ROWS, 8), vmem(2, 7, Z),
            vmem(2, 2, WIN), vmem(2, 4, WIN),
            vmem(2, 8), vmem(2, GROUP, 8), vmem(2, 8), vmem(2, nhi, 8),
            pltpu.SemaphoreType.DMA((23,)), pltpu.SemaphoreType.DMA((23,)),
            pltpu.SemaphoreType.DMA((2, 2, max(GROUP, nhi))), pltpu.SemaphoreType.DMA((2, 2, max(GROUP, nhi))),
        ],
        compiler_params=pltpu.CompilerParams(
            collective_id=0, has_side_effects=True, vmem_limit_bytes=62 * 1024 * 1024),
    )(prediction.reshape(Z * X, Y), label.reshape(Z * X, Y))
    return loss.reshape(()), jnp.transpose(grad, (1, 0, 2))


def solution(mesh):
    in_specs = (P("gz", "gx", "gy"), P("gz", "gx", "gy"))
    out_specs = (P(), P("gz", "gx", "gy"))
    return jax.shard_map(local, mesh=mesh, in_specs=in_specs, out_specs=out_specs, check_vma=False)
```

```python
import functools

import jax
import jax.numpy as jnp
from jax import lax
from jax.experimental import pallas as pl
from jax.experimental.pallas import tpu as pltpu
from jax.sharding import PartitionSpec as P

LEVELS = 6
Z, X, Y = 32, 16, 128
WIN = Z + 8
PAD = WIN + 16
ROWS = X + 16
GROUP = 8
LO = 2
SEMS = 64
MESH = pl.DeviceIdType.MESH

W, WL, WU = pl.ds(8, WIN), pl.ds(7, WIN), pl.ds(9, WIN)


def lane_of(v):
    return lax.broadcasted_iota(jnp.int32, v.shape, 1)


def plane_of(v):
    return lax.broadcasted_iota(jnp.int32, v.shape, 0)


def roll(v, by):
    return pltpu.roll(v, by, 1)


def max3(a, b, c):
    return jnp.maximum(jnp.maximum(a, b), c)


def route(g, best, candidates):
    zero = jnp.zeros_like(g)
    parts = []
    for value in candidates:
        hit = value == best
        part = jnp.where(hit, g, zero)
        parts.append(part)
        g = g - part
    parts.append(g)
    return parts


def run(start, blocks, size, row):
    def block(b, _):
        todo, memo = [], {}
        first = start(b) if callable(start) else start + b * size
        for q in range(size):
            todo += row(first + q, q, memo)
        for ref, at, value in todo:
            ref[at] = value
        return 0
    if isinstance(blocks, int) and blocks == 1:
        block(0, 0)
        return
    else:
        lax.fori_loop(0, blocks, block, 0)


def once(memo, key, load):
    if key not in memo:
        memo[key] = load()
    return memo[key]


def slot_of(f, k):
    if f == 0:
        return k
    if isinstance(k, int) and k == 0:
        return 7
    return jnp.where(k == 0, 7, 8 + lax.rem(k, 2))


def kernel(nx, pred_hbm, label_hbm, out, loss, pred, label, in_sem, E, S, M1, M2, SM1, SM2, SP, SSP, GB, SGB, CT, SCT, SK, SSK,
           HX, SHX, HZ, G, SG, T, T2, SX, SX2, LE, SLE, LM, BM, SLM, SBM, F, FO, RZ, RX, PS, PR, ARS, AR1, AR2S, AR2,
           send_sem, recv_sem, ar_send, ar_recv):
    gz, gx, gy = lax.axis_index("gz"), lax.axis_index("gx"), lax.axis_index("gy")
    prev, nxt = lax.rem(gx + nx - 1, nx), lax.rem(gx + 1, nx)
    nhi = nx // LO
    hi, lo = gx // LO, lax.rem(gx, LO)
    me1 = (gz * LO + lo) * 2 + gy
    o = pl.multiple_of(8 + 8 * gz, 8)
    O, OL, OU = pl.ds(o, Z), pl.ds(o - 1, Z), pl.ds(o + 1, Z)
    seam = 127 * (1 - gy)
    zlow = jnp.where(gz == 0, 0, -1)
    zhigh = jnp.where(gz == 1, Z - 1, -1)
    first_lane = jnp.where(gx == 0, 32, 0)
    last_lane = jnp.where(gx == nx - 1, 96, 128)

    def member(i):
        return (i // (2 * LO), hi * LO + lax.rem(i // 2, LO), lax.rem(i, 2))

    loads = [pltpu.make_async_copy(src, dst.at[pl.ds(0, Z * X)], in_sem.at[f])
             for f, (src, dst) in enumerate(((pred_hbm, pred), (label_hbm, label)))]
    for load in loads:
        load.start()

    barrier = pltpu.get_barrier_semaphore()
    has_prev, has_nxt = gx > 0, gx < nx - 1
    for inside, row in ((has_prev, prev), (has_nxt, nxt)):
        @pl.when(inside)
        def _(row=row):
            for cols in (gy, 1 - gy):
                pl.semaphore_signal(barrier, inc=1, device_id=(gz, row, cols), device_id_type=MESH)
    greet = [member(lax.rem(me1 + d, GROUP)) for d in range(1, GROUP)]
    greet += [(gz, lax.rem(hi + d, nhi) * LO + lo, gy) for d in range(1, nhi)]
    for device in greet:
        pl.semaphore_signal(barrier, inc=1, device_id=device, device_id_type=MESH)

    def lay_out(f):
        ref = (pred, label)[f]
        loads[f].wait()

        def bring(x, _, memo):
            return [(E, (7 * f, 9 + x, pl.ds(o + 8 * t, 8)), ref[pl.ds(x + X * 8 * t, 8, stride=X), :])
                    for t in range(Z // 8)]
        run(0, 2, 8, bring)

    lay_out(0)
    zero_w = jnp.zeros((WIN, Y), jnp.float32)
    zero_o = jnp.zeros((Z, Y), jnp.float32)
    pl.semaphore_wait(barrier, len(greet) + jnp.where(has_prev, 2, 0) + jnp.where(has_nxt, 2, 0))

    copies = []

    def only(inside, act):
        if inside is None:
            act()
        else:
            pl.when(inside)(act)

    class Sent:
        def __init__(self, copy, sends, gets):
            self.copy, self.sends, self.gets = copy, sends, gets

        def start(self):
            only(self.sends, self.copy.start)

        def wait_recv(self):
            only(self.gets, self.copy.wait_recv)

        def wait_send(self):
            only(self.sends, self.copy.wait_send)

    def send(number, src, dst, device, step=0, now=True):
        copy = pltpu.make_async_remote_copy(
            src_ref=src, dst_ref=dst, send_sem=send_sem.at[number], recv_sem=recv_sem.at[number],
            device_id=device, device_id_type=MESH)
        sends = {0: None, -1: has_prev, 1: has_nxt}[step]
        gets = {0: None, -1: has_nxt, 1: has_prev}[step]
        copies.append(Sent(copy, sends, gets))
        if now:
            copies[-1].start()
        return copies[-1]

    near = pl.multiple_of(32 - 16 * gz, 8)
    far = pl.multiple_of(8 + 32 * gz, 8)
    below, above = (gz, prev, gy), (gz, nxt, gy)
    arrived = [[], []]

    def pass_rows(f, base, planes):
        arrived[f] += [
            send(base, E.at[7 * f, pl.ds(9, 7), planes], E.at[7 * f, pl.ds(25, 7), planes], below, -1),
            send(base + 1, E.at[7 * f, pl.ds(18, 7), planes], E.at[7 * f, pl.ds(2, 7), planes], above, 1)]

    def first_halos(f):
        copy = send(8 * f, E.at[7 * f, pl.ds(9, X), pl.ds(near, 8)], E.at[7 * f, pl.ds(9, X), pl.ds(far, 8)],
                    (1 - gz, gx, gy))
        pass_rows(f, 8 * f + 1, O)
        return copy

    def second_halos(f, depth):
        depth.wait_recv()
        pass_rows(f, 8 * f + 3, pl.ds(pl.multiple_of(40 - 32 * gz, 8), 8))
        for half in (0, 1):
            packed = zero_w
            for i in range(8):
                v = E[7 * f, 9 + 8 * half + i, W]
                packed = jnp.where(lane_of(v) // 16 == i, roll(v, lax.rem(16 * i + 16 * (1 - gy), 128)), packed)
            PS[f, half] = packed
        arrived[f] += [
            send(8 * f + 5, PS.at[f], PR.at[f, pl.ds(1, 2)], (gz, gx, 1 - gy)),
            send(8 * f + 6, PS.at[f, 0], PR.at[f, 3], (gz, prev, 1 - gy), -1),
            send(8 * f + 7, PS.at[f, 1], PR.at[f, 0], (gz, nxt, 1 - gy), 1)]

    depth = first_halos(0)
    lay_out(1)
    second_halos(0, depth)
    depth = first_halos(1)
    second_halos(1, depth)

    two = jnp.full((8, Y), 2.0, jnp.float32)

    def rims(r, _, memo):
        return [(E, (slot, r, pl.ds(at, 8)), two) for slot in range(10) for at in (0, PAD - 8)]
    run(0, 17, 2, rims)

    def strip_rims(j, _, memo):
        return [(S, (f, k, j, pl.ds(at, 8)), two)
                for f in (0, 1) for k in range(LEVELS + 1) for at in (0, PAD - 8)]
    run(1, 4, 2, strip_rims)
    run(0, 17, 2, lambda r, _, m: [(G, (p, q, r), zero_w) for p in range(LEVELS + 1) for q in range(3)])
    for k in range(LEVELS):
        HZ[k, 0] = zero_w
    run(0, 2, 5, lambda j, _, m: [(SG, (p, q, j), zero_w) for p in (0, 1) for q in range(3)])
    run(0, 4, 5, lambda i, _, m: [(HX, (q, i), zero_o) for q in range(3)])
    run(0, 4, 4, lambda i, _, m: [(SK, (0, i), zero_o), (SK, (1, i), zero_o), (GB, (LEVELS, i + 1), zero_o)])
    run(0, 1, 8, lambda j, _, m: [(SSK, (j,), zero_o), (SGB, (LEVELS, j), zero_o)])
    for k in range(LEVELS + 1):
        GB[k, 0] = zero_o
        CT[0] = zero_o
        CT[X + 1] = zero_o
        GB[k, X + 1] = zero_o
    for q in range(8):
        for p in range(3):
            T[q, p] = jnp.zeros((PAD, Y), jnp.float32)
    for q in range(8):
        for p in range(2):
            T2[q, p] = jnp.zeros((PAD, Y), jnp.float32)
    for r in (0, 1, ROWS, ROWS + 1):
        for slot in range(10) if r in (0, ROWS + 1) else (0, 7):
            E[slot, r, W] = zero_w + 2.0

    @pl.when(gx == 0)
    def _():
        for f in (0, 1):
            PR[f, 0] = zero_w + 2.0
            for r in range(2, 9):
                E[7 * f, r, W] = zero_w + 2.0
        RX[1] = jnp.zeros((7, Z, Y), jnp.float32)

    @pl.when(gx == nx - 1)
    def _():
        for f in (0, 1):
            PR[f, 3] = zero_w + 2.0
            for r in range(25, 32):
                E[7 * f, r, W] = zero_w + 2.0
        RX[0] = jnp.zeros((7, Z, Y), jnp.float32)

    seam_turn = 111 + 2 * gy

    def place(r):
        g = lax.div(r, 8)
        return r - 8 * g, seam_turn - 32 * g

    def sides(v, seen):
        lane = lane_of(v)
        t = jnp.where(lane == seam, seen, v)
        return jnp.where(lane == 0, t, roll(v, 1)), jnp.where(lane == 127, t, roll(v, 127))

    def strip_sides(v):
        return roll(v, 1), roll(v, 127)

    def gather_sides(lower, upper, seen):
        lane = lane_of(lower)
        t = jnp.where(lane == seam, seen, 0.0)
        return jnp.where(lane == 127, t, roll(lower, 127)) + jnp.where(lane == 0, t, roll(upper, 1))

    def wrap_strip(ref, at, window, value):
        v = ref[at + (8, window)]
        v = jnp.where(lane_of(v) < first_lane, value, v)
        ref[at + (8, window)] = v
        ref[at + (0, window)] = roll(v, 32)
        v = ref[at + (1, window)]
        v = jnp.where(lane_of(v) >= last_lane, value, v)
        ref[at + (1, window)] = v
        ref[at + (9, window)] = roll(v, 96)

    def cap_rows(f, k):
        @pl.when(gx == 0)
        def _():
            E[slot_of(f, k), 8, W] = zero_w + 2.0

        @pl.when(gx == nx - 1)
        def _():
            E[slot_of(f, k), 25, W] = zero_w + 2.0

    def build_strip(f):
        def row(j, _, memo):
            acc = zero_w
            lane = lane_of(acc) // 16
            for g in range(4):
                own = roll(E[7 * f, 8 * g + j + 1, W], lax.rem(32 * g + 16, 128))
                other = roll(PR[f, g], lax.rem(32 * g - 16 * j + 16 * (1 - gy) + 128, 128))
                acc = jnp.where(lane == 2 * g + gy, own, acc)
                acc = jnp.where(lane == 2 * g + 1 - gy, other, acc)
            return [(S, (f, 0, j + 1, W), acc)]
        run(0, 2, 4, row)
        wrap_strip(S, (f, 0), W, 2.0)

    def eroded(ref, at, i, q, memo, pair):
        def centre(step):
            return once(memo, q + step, lambda: ref[at + (i + step, W)])
        c = centre(0)
        lower, upper = pair(c)
        m = jnp.minimum(jnp.minimum(c, lower), upper)
        m = jnp.minimum(m, jnp.minimum(ref[at + (i, WL)], ref[at + (i, WU)]))
        return jnp.minimum(m, jnp.minimum(centre(-1), centre(1))), lower

    def depth_max(ref, at, i):
        c = ref[at + (i, O)]
        plane = plane_of(c)
        lower = jnp.where(plane == zlow, c, ref[at + (i, OL)])
        upper = jnp.where(plane == zhigh, c, ref[at + (i, OU)])
        return max3(lower, c, upper)

    def level_forward(f, k, slot, first, rows):
        def strip_erode(j, q, memo):
            m, lower = eroded(S, (f, k), j + 1, q, memo, strip_sides)
            return [(S, (f, k + 1, j + 1, W), m)] + ([(SLE, (k, j), lower)] if f == 0 else [])
        run(0, 1, 8, strip_erode)
        wrap_strip(S, (f, k + 1), W, 2.0)

        def erode(r, q, memo):
            j, g = r % 8, r // 8
            seen = roll(S[f, k, j + 1, W], seam_turn - 32 * g)
            m, lower = eroded(E, (slot_of(f, k),), r + 1, q, memo, lambda c: sides(c, seen))
            if r in (7, 24):
                m = jnp.where(gx == (0 if r == 7 else nx - 1), zero_w + 2.0, m)
            return [(E, (slot_of(f, k + 1), r + 1, W), m)] + ([(LE, (k, r), lower)] if f == 0 else [])
        run(first, 1, rows, erode)

        def strip_depth(j, _, memo):
            return [(SM1, (slot, j + 1), depth_max(S, (f, k + 1), j + 1))]
        run(0, 1, 8, strip_depth)
        wrap_strip(SM1, (slot,), slice(None), 0.0)

        def strip_rows(j, q, memo):
            v = max3(*[once(memo, q + d, lambda d=d: SM1[slot, j + d]) for d in range(3)])
            todo = [(SM2, (slot, j), v)]
            if f == 0:
                lower, upper = strip_sides(v)
                best = max3(lower, v, upper)
                delta = jnp.maximum(S[f, k, j + 1, O] - best, 0.0)
                prior = SSK[j]
                todo += [(SLM, (k, j), lower), (SBM, (k, j), best), (SGB, (k, j), delta), (SSP, (k, j), prior),
                         (SSK, (j,), prior + jnp.maximum(delta - prior * delta, 0.0))]
            return todo
        run(0, 1, 8, strip_rows)

        def depth_rows(i, _, memo):
            m = depth_max(E, (slot_of(f, k + 1),), i + 8)
            if i in (0, X + 1):
                m = jnp.where(gx == (0 if i == 0 else nx - 1), zero_o, m)
            return [(M1, (slot, i), m)]
        run(0, 1, X + 2, depth_rows)

        def rest(i, q, memo):
            v = max3(*[once(memo, q + d, lambda d=d: M1[slot, i + d]) for d in range(3)])
            r = i + 8
            lower, upper = sides(v, roll(SM2[slot, i % 8], seam_turn - 32 * (r // 8)))
            best = max3(lower, v, upper)
            delta = jnp.maximum(E[slot_of(f, k), r + 1, O] - best, 0.0)
            prior = SK[f, i]
            todo = [(SK, (f, i), prior + jnp.maximum(delta - prior * delta, 0.0))]
            if f == 0:
                todo += [(M2, (k, i), v), (GB, (k, i + 1), delta), (SP, (k, i), prior), (LM, (k, i), lower), (BM, (k, i), best)]
            return todo
        run(0, 1, X, rest)

    def ar_copy(n, phase, slot, src, dst, number, device):
        return pltpu.make_async_remote_copy(
            src_ref=src, dst_ref=dst, send_sem=ar_send.at[n, phase, number], recv_sem=ar_recv.at[n, phase, slot],
            device_id=device, device_id_type=MESH)

    def ar_first(n, d):
        return ar_copy(n, 0, me1, ARS.at[n], AR1.at[n, me1], d, member(lax.rem(me1 + d, GROUP)))

    def ar_second(n, d):
        return ar_copy(n, 1, hi, AR2S.at[n], AR2.at[n, hi], d, (gz, lax.rem(hi + d, nhi) * LO + lo, gy))

    def ar_start(n, f):
        def add(b, carry):
            both, alone = carry
            for q in range(4):
                v = SK[f, 4 * b + q]
                both, alone = both + v * E[7 - 7 * f, 4 * b + q + 9, O], alone + v
            return both, alone
        both, alone = lax.fori_loop(0, X // 4, add, (zero_o, zero_o))
        both = jnp.sum(both, axis=0, keepdims=True)
        alone = jnp.sum(alone, axis=0, keepdims=True)
        sub = plane_of(two)
        tile = jnp.where(sub == 0, both, jnp.where(sub == 1, alone, 0.0))
        ARS[n] = tile
        AR1[n, me1] = tile
        for d in range(1, GROUP):
            ar_first(n, d).start()

    def ar_middle(n):
        for d in range(1, GROUP):
            s = lax.rem(me1 + d, GROUP)
            ar_copy(n, 0, s, ARS.at[n], AR1.at[n, s], d, member(s)).wait_recv()
        tile = AR1[n, 0]
        for s in range(1, GROUP):
            tile = tile + AR1[n, s]
        AR2S[n] = tile
        AR2[n, hi] = tile
        for d in range(1, nhi):
            ar_second(n, d).start()

    def ar_end(n):
        for d in range(1, nhi):
            s = lax.rem(hi + d, nhi)
            ar_copy(n, 1, s, AR2S.at[n], AR2.at[n, s], d, (gz, s * LO + lo, gy)).wait_recv()
        tile = AR2[n, 0]
        for s in range(1, nhi):
            tile = tile + AR2[n, s]
        for d in range(1, GROUP):
            ar_first(n, d).wait_send()
        for d in range(1, nhi):
            ar_second(n, d).wait_send()
        tile = jnp.sum(tile, axis=1, keepdims=True)
        return tile[0:1], tile[1:2]

    for f in (0, 1):
        for copy in arrived[f]:
            copy.wait_recv()
        cap_rows(f, 0)
        build_strip(f)

        def level(first, rows, k, f=f):
            level_forward(f, k, k if f == 0 else LEVELS, first, rows)
            if f == 1 and rows == 28:
                @pl.when(k == 1)
                def _():
                    ar_middle(0)
            return 0
        lax.fori_loop(0, 4, lambda k, _: level(2, 28, k), 0)
        lax.fori_loop(4, LEVELS, lambda k, _: level(6, 20, k), 0)
        ar_start(f, f)

    def chain(i, _, memo):
        t = zero_o + 1.0
        todo = []
        for k in range(LEVELS - 1, -1, -1):
            delta, prior = GB[k, i + 1], SP[k, i]
            on = delta - prior * delta > 0
            GB[k, i + 1] = jnp.where(on, t * (1.0 - prior), 0.0)
            t = jnp.where(on, t * (1.0 - delta), t)
        return todo
    run(0, 4, 4, chain)

    def strip_chain(j, _, memo):
        t = zero_o + 1.0
        lane = lane_of(t)
        mine = (lane >= 32) & (lane < 96)
        for k in range(LEVELS - 1, -1, -1):
            delta, prior = SGB[k, j], SSP[k, j]
            on = delta - prior * delta > 0
            SGB[k, j] = jnp.where(on & mine, t * (1.0 - prior), 0.0)
            t = jnp.where(on, t * (1.0 - delta), t)
        return []
    run(0, 2, 4, strip_chain)

    both, alone = ar_end(0)
    pred_total = alone
    tprec = (both + 1.0) / (pred_total + 1.0)

    run(0, 2, 8, lambda i, _, m: [(CT, (i + 1,), E[7, i + 9, O] - tprec)])
    run(0, 1, 8, lambda j, _, m: [(SCT, (j,), S[1, 0, j + 1, O] - tprec)])

    def strip_back(step, _):
        k = LEVELS - 1 - step
        old = lax.rem(step, 2)
        new = 1 - old

        def strip_cols(j, _, memo):
            a = SM2[k, j]
            gc, gl, gu = route(-SGB[k, j] * SCT[j], SBM[k, j], (a, SLM[k, j]))
            todo = [(SX, (k, j), jnp.where(gy == 0, gl, gu))]
            g = gc + roll(gl, 127) + roll(gu, 1)
            gc, gl, gu = route(g, a, (SM1[k, j + 1], SM1[k, j]))
            return todo + [(SHX, (0, j + 1), gc), (SHX, (1, j + 1), gl), (SHX, (2, j + 1), gu)]
        run(0, 1, 8, strip_cols)
        SHX[1, 9] = roll(SHX[1, 1], 96)
        SHX[2, 0] = roll(SHX[2, 8], 32)

        def strip_depth(j, q, memo):
            g = SHX[0, j + 1] + SHX[1, j + 2] + SHX[2, j]
            gc, gl, gu = route(g, SM1[k, j + 1], (S[0, k + 1, j + 1, O], S[0, k + 1, j + 1, OL]))
            T[q, 0, O] = gc + SGB[k + 1, j] * SCT[j]
            T[q, 1, O] = gl
            T[q, 2, O] = gu
            g = SG[old, 0, j + 1] + SG[old, 1, j + 2] + SG[old, 2, j]
            g = g + T[q, 0, W] + T[q, 1, WU] + T[q, 2, WL]
            c = S[0, k, j + 1, W]
            gc, zl, zu, xl, xu, yl, yu = route(
                g, S[0, k + 1, j + 1, W],
                (c, S[0, k, j + 1, WL], S[0, k, j + 1, WU], S[0, k, j, W], S[0, k, j + 2, W], SLE[k, j]))
            T2[q, 0, W] = zl
            T2[q, 1, W] = zu
            return [(SX2, (k, j), jnp.where(gy == 0, yl, yu)),
                    (SG, (new, 0, j + 1), gc + roll(yl, 127) + roll(yu, 1) + T2[q, 0, WU] + T2[q, 1, WL]),
                    (SG, (new, 1, j + 1), xl), (SG, (new, 2, j + 1), xu)]
        run(0, 1, 8, strip_depth)
        SG[new, 1, 9] = roll(SG[new, 1, 1], 96)
        SG[new, 2, 0] = roll(SG[new, 2, 8], 32)
        return 0

    def open_cols(k, i, j, g):
        a = M2[k, i]
        by = seam_turn - 32 * g
        gc, gl, gu = route(-GB[k, i + 1] * CT[i + 1], BM[k, i], (a, LM[k, i]))
        g = gc + gather_sides(gl, gu, roll(SX[k, j], by))
        gc, gl, gu = route(g, a, (M1[k, i + 1], M1[k, i]))
        return [(HX, (0, i + 2), gc), (HX, (1, i + 2), gl), (HX, (2, i + 2), gu)]

    def open_depths(k, i, q):
        g = HX[0, i + 1] + HX[1, i + 2] + HX[2, i]
        gc, gl, gu = route(g, M1[k, i], (E[k + 1, i + 8, O], E[k + 1, i + 8, OL]))
        T[q, 0, O] = gc + GB[k + 1, i] * CT[i]
        T[q, 1, O] = gl
        T[q, 2, O] = gu
        return [(HZ, (k, i + 1), T[q, 0, W] + T[q, 1, WU] + T[q, 2, WL])]

    def open_all(k, _):
        run(0, 1, X, lambda i, q, memo: open_cols(k, i, i % 8, i // 8 + 1))
        run(0, 1, X + 2, lambda i, q, memo: open_depths(k, i, q % 8))
        return 0

    def open_outer(k, _):
        for start in (0, 12):
            run(start, 1, 4, lambda i, q, memo: open_cols(k, i, i % 8, i // 8 + 1))
        for start in (0, 14):
            run(start, 1, 4, lambda i, q, memo: open_depths(k, i, start // 14 * 4 + q))
        return 0

    def open_inner(k):
        run(2, 1, 12, lambda i, q, memo: open_cols(k, i, i % 8, i // 8 + 1))
        run(4, 1, 10, lambda i, q, memo: open_depths(k, i, q % 8))

    lax.fori_loop(0, 3, lambda step, _: strip_back(step, 0) + open_all(LEVELS - 1 - step, 0), 0)
    ar_middle(1)
    lax.fori_loop(3, LEVELS, lambda step, _: strip_back(step, 0) + open_outer(LEVELS - 1 - step, 0), 0)

    def erode_back(k, r, q, memo):
        g = G[k + 1, 0, r + 1] + G[k + 1, 1, r + 2] + G[k + 1, 2, r] + HZ[k, jnp.where((r > 6) & (r < 25), r - 6, 0)]
        j, by = place(r)
        under, c, over = [once(memo, q + d, lambda d=d: E[k, r + d, W]) for d in range(3)]
        gc, zl, zu, xl, xu, yl, yu = route(
            g, E[k + 1, r + 1, W],
            (c, E[k, r + 1, WL], E[k, r + 1, WU], under, over, LE[k, r]))
        T2[q, 0, W] = zl
        T2[q, 1, W] = zu
        return [(G, (k, 0, r + 1), gc + gather_sides(yl, yu, roll(SX2[k, j], by)) + T2[q, 0, WU] + T2[q, 1, WL]),
                (G, (k, 1, r + 1), xl), (G, (k, 2, r + 1), xu)]

    def outer(step, _):
        k = LEVELS - 1 - step
        run(lambda b: jnp.where(b == 0, 2 + k, 23 - k), 2, 7, lambda r, q, memo: erode_back(k, r, q, memo))
        return 0
    lax.fori_loop(0, LEVELS, outer, 0)

    beyond = pl.multiple_of(32 - 32 * gz, 8)
    mine = pl.multiple_of(8 * gz, 8)
    inner = pl.multiple_of(24 - 24 * gz, 8)
    quiet = pl.ds(mine, Z - 8)
    edge = pl.ds(inner, 8)
    back_rows = []

    def total(r, _, memo):
        v = G[0, 0, r + 1] + G[0, 1, r + 2] + G[0, 2, r]
        return [(F, (r,), v)]

    def from_depth(r, _, memo):
        return [(FO, (r, edge), F[r, pl.ds(mine + inner, 8)] + RZ[r])]

    def own_planes(r, _, memo):
        return [(FO, (r,), F[r, pl.ds(mine, Z)])]

    def return_rows(base, ref, at, planes, now):
        back_rows.append(send(base, ref.at[pl.ds(1, 7), at], RX.at[0, :, planes], below, -1, now))
        back_rows.append(send(base + 1, ref.at[pl.ds(24, 7), at], RX.at[1, :, planes], above, 1, now))

    def to_depth(number, rows):
        return send(number, F.at[rows, pl.ds(beyond, 8)], RZ.at[rows], (1 - gz, gx, gy))

    for start in (1, 24):
        run(start, 1, 7, total)
    return_rows(18, F, pl.ds(pl.multiple_of(16 * gz, 8), Z - 8), quiet, True)
    margin = [to_depth(16, pl.ds(1, 7)), to_depth(17, pl.ds(24, 7))]
    return_rows(20, FO, edge, edge, False)

    def inside(step, _):
        k = LEVELS - 1 - step
        at = (k + 1) // 2

        @pl.when(k < 3)
        def _():
            open_inner(k)
        run(8 + 2 * at, 4 - at, 4, lambda r, q, memo: erode_back(k, r, q, memo))

        @pl.when(step == 1)
        def _():
            for copy in margin:
                copy.wait_recv()
            for start in (1, 24):
                run(start, 1, 7, from_depth)
            for copy in back_rows[2:]:
                copy.start()
        return 0
    lax.fori_loop(0, LEVELS, inside, 0)
    run(8, 2, 8, total)
    copy = to_depth(22, pl.ds(8, 16))
    run(8, 2, 8, own_planes)
    copy.wait_recv()
    run(8, 2, 8, from_depth)

    both, alone = ar_end(1)
    tsens = (both + 1.0) / (alone + 1.0)
    square = (tprec + tsens) * (tprec + tsens)
    voxels = float(2 * nx * 2 * Z * X * Y)
    by_prec = -2.0 * tsens * tsens / square / (pred_total + 1.0) * voxels
    by_sens = -2.0 * tprec * tprec / square / (alone + 1.0) * voxels
    loss[...] = 1.0 - 2.0 * tprec * tsens / (tprec + tsens)

    for copy in back_rows:
        copy.wait_recv()

    def give(x, _, memo, extra):
        g = FO[x + 8] + GB[0, x + 1] * CT[x + 1]
        if extra is not None:
            g = g + extra(x)
        g = g * by_prec + SK[1, x] * by_sens
        return [(out, (x,), g)]
    run(0, 1, 7, functools.partial(give, extra=lambda x: RX[1, x]))
    run(7, 1, 2, functools.partial(give, extra=None))
    run(9, 1, 7, functools.partial(give, extra=lambda x: RX[0, x - 9]))
    for copy in copies:
        copy.wait_send()


def local(prediction, label):
    nx = lax.axis_size("gx")
    nhi = nx // LO
    f32 = jnp.float32

    def vmem(*shape):
        return pltpu.VMEM(shape + (Y,), f32)

    grad, loss = pl.pallas_call(
        functools.partial(kernel, nx),
        out_shape=(jax.ShapeDtypeStruct((X, Z, Y), f32), jax.ShapeDtypeStruct((1, 1), f32)),
        in_specs=[pl.BlockSpec(memory_space=pl.ANY)] * 2,
        out_specs=[pl.BlockSpec(memory_space=pltpu.VMEM)] * 2,
        scratch_shapes=[
            vmem(Z * X + 256), vmem(Z * X + 256), pltpu.SemaphoreType.DMA((2,)),
            vmem(10, ROWS + 2, PAD), vmem(2, 7, 10, PAD),
            vmem(7, X + 2, Z), vmem(6, X, Z), vmem(7, 10, Z), vmem(7, 8, Z),
            vmem(6, X, Z), vmem(6, 8, Z),
            vmem(7, X + 2, Z), vmem(7, 8, Z), vmem(X + 2, Z), vmem(8, Z),
            vmem(2, X, Z), vmem(8, Z),
            vmem(3, X + 4, Z), vmem(3, 10, Z), vmem(LEVELS, X + 3, WIN),
            vmem(7, 3, ROWS + 2, WIN), vmem(2, 3, 10, WIN),
            vmem(8, 3, PAD), vmem(8, 2, PAD), vmem(6, 8, Z), vmem(6, 8, WIN),
            vmem(6, ROWS, WIN), vmem(6, 8, WIN),
            vmem(6, X, Z), vmem(6, X, Z), vmem(6, 8, Z), vmem(6, 8, Z),
            vmem(ROWS, WIN), vmem(ROWS, Z), vmem(ROWS, 8), vmem(2, 7, Z),
            vmem(2, 2, WIN), vmem(2, 4, WIN),
            vmem(2, 8), vmem(2, GROUP, 8), vmem(2, 8), vmem(2, nhi, 8),
            pltpu.SemaphoreType.DMA((23,)), pltpu.SemaphoreType.DMA((23,)),
            pltpu.SemaphoreType.DMA((2, 2, max(GROUP, nhi))), pltpu.SemaphoreType.DMA((2, 2, max(GROUP, nhi))),
        ],
        compiler_params=pltpu.CompilerParams(
            collective_id=0, has_side_effects=True, vmem_limit_bytes=62 * 1024 * 1024),
    )(prediction.reshape(Z * X, Y), label.reshape(Z * X, Y))
    return loss.reshape(()), jnp.transpose(grad, (1, 0, 2))


def solution(mesh):
    in_specs = (P("gz", "gx", "gy"), P("gz", "gx", "gy"))
    out_specs = (P(), P("gz", "gx", "gy"))
    return jax.shard_map(local, mesh=mesh, in_specs=in_specs, out_specs=out_specs, check_vma=False)
```
